32 devices in a mesh: seq: 16 (over z, x, core), chan: 2 (over y).
Axes of the slice: x: 2, y: 2, z: 4, core: 2. Of those that a mesh axis runs over, the one named last changes fastest.
Arguments:
- grad_out: bfloat16 [2048, 4096], P('seq', 'chan'), may hold values from -6 to 6
- out_weight: bfloat16 [4096, 4096], P('seq', 'chan'), may hold values from -0.09375 to 0.09375
- gate_stream: bfloat16 [4096, 2048], P('chan', 'seq'), may hold values from -6 to 6
- conv_output: bfloat16 [4096, 2048], P('chan', 'seq'), may hold values from -6 to 6
- key_stream: bfloat16 [4096, 2048], P('chan', 'seq'), may hold values from -6 to 6
- value_stream: bfloat16 [4096, 2048], P('chan', 'seq'), may hold values from -6 to 6
- long_filter: bfloat16 [4096, 2048], P(('chan', 'seq')), may hold values from 0 to 1
Outputs:
- grad_gate: bfloat16 [4096, 2048], P('chan', 'seq')
- grad_key: bfloat16 [4096, 2048], P('chan', 'seq')
- grad_value: bfloat16 [4096, 2048], P('chan', 'seq')
The draws below stay inside these ranges and needn't reach their ends.
All inputs are finite; a program needn't handle non-finite values.
Results may differ from the reference program's by a relative error of at most 0.007.
Values may be sent and summed in bfloat16 or wider, within the bound.
No kernel may reach another device: no remote copies, remote signals or barrier semaphores. Data moves between devices by JAX's collectives and lax.ppermute only.
A program may use at most 64 MiB of HBM per device.

```python
import math
import jax
import jax.numpy as jnp
from jax import lax

FEATURES = 4096
CONV_CHANNELS = 4096
SEQUENCE_LENGTH = 2048


def draw_long_filter(key, part):
    random_keys = jax.random.split(key, 6)
    delay_index = jnp.arange(SEQUENCE_LENGTH, dtype=jnp.int32)[None, :]
    slow_share = 0.5
    slow_pick = jax.random.uniform(random_keys[0], (CONV_CHANNELS, 1), jnp.float32)
    slow_rate = jnp.exp(jax.random.uniform(random_keys[1], (CONV_CHANNELS, 1), jnp.float32, math.log(0.05 / SEQUENCE_LENGTH), math.log(2.0 / SEQUENCE_LENGTH)))
    fast_rate = jnp.exp(jax.random.uniform(random_keys[2], (CONV_CHANNELS, 1), jnp.float32, math.log(2.0 / SEQUENCE_LENGTH), math.log(1.0 / 30.0)))
    falloff_speed = jnp.where(slow_pick < slow_share, slow_rate, fast_rate)
    jitter_level = 0.5 + jax.random.uniform(random_keys[3], (CONV_CHANNELS, SEQUENCE_LENGTH), jnp.float32)
    spike_delay = jax.random.randint(random_keys[4], (CONV_CHANNELS, 3), 0, SEQUENCE_LENGTH, jnp.int32)
    spike_retain = jax.random.uniform(random_keys[5], (CONV_CHANNELS, 3), jnp.float32, 0.5, 0.8)
    spike_factor = jnp.ones((CONV_CHANNELS, SEQUENCE_LENGTH), jnp.float32)
    for spike_index in range(3):
        elapsed_steps = delay_index >= spike_delay[:, spike_index:spike_index + 1]
        spike_factor = spike_factor * jnp.where(elapsed_steps, spike_retain[:, spike_index:spike_index + 1], 1.0)
    filter_magnitude = jnp.sqrt(2.0 * falloff_speed + 1.0 / SEQUENCE_LENGTH)
    filter_coefficients = filter_magnitude * jnp.exp(-falloff_speed * delay_index.astype(jnp.float32)) * jitter_level * spike_factor
    return filter_coefficients.astype(jnp.bfloat16)


def levels(key, shape, shards, smallest, largest):
    def one(axis_at, blocks):
        draws = jax.random.uniform(jax.random.fold_in(jax.random.fold_in(key, 6), axis_at), (blocks,), jnp.float32, smallest / len(shards), largest / len(shards))
        return jnp.repeat(jnp.exp(draws), shape[axis_at] // blocks).reshape((-1,) + (1,) * (len(shape) - axis_at - 1))

    loudness = one(*shards[0])
    for cut in shards[1:]:
        loudness = loudness * one(*cut)
    return loudness


def scatter_about(rng, shape, spread, limit, cuts=(), kind=jnp.bfloat16):
    level = levels(rng, shape, cuts, -0.22, 0.18) if cuts else 1.0
    entries = jax.random.normal(rng, shape, jnp.float32) * spread * level
    return jnp.minimum(jnp.maximum(entries, -limit), limit).astype(kind)


def setup_inputs(seed: int = 0) -> dict:
    arg_keys = jax.random.split(jax.random.key(seed), 8)
    grad_out = scatter_about(arg_keys[0], (SEQUENCE_LENGTH, FEATURES), 1.0, 6.0, ((0, 16), (1, 2)))
    out_weight = scatter_about(arg_keys[1], (FEATURES, CONV_CHANNELS), FEATURES ** -0.5, 0.09375, ((0, 16), (1, 2)))
    gate_stream = scatter_about(arg_keys[2], (CONV_CHANNELS, SEQUENCE_LENGTH), 1.0, 6.0, ((0, 2), (1, 16)))
    conv_output = scatter_about(arg_keys[3], (CONV_CHANNELS, SEQUENCE_LENGTH), 1.0, 6.0, ((0, 2), (1, 16)))
    key_stream = scatter_about(arg_keys[4], (CONV_CHANNELS, SEQUENCE_LENGTH), 1.0, 6.0, ((0, 2), (1, 16)))
    value_stream = scatter_about(arg_keys[5], (CONV_CHANNELS, SEQUENCE_LENGTH), 1.0, 6.0, ((0, 2), (1, 16)))
    long_filter = draw_long_filter(jax.random.fold_in(arg_keys[7], 71), 0)
    return {"grad_out": grad_out, "out_weight": out_weight, "gate_stream": gate_stream, "conv_output": conv_output, "key_stream": key_stream, "value_stream": value_stream, "long_filter": long_filter}


def correlate(gated_grad, filter_coefficients):
    seq_len = gated_grad.shape[1]
    block_count = gated_grad.shape[0] // 64

    def block_corr(pair_input):
        signal, kernel = pair_input
        spec_signal = jnp.fft.rfft(signal, 2 * seq_len, axis=-1)
        spec_kernel = jnp.fft.rfft(kernel, 2 * seq_len, axis=-1)
        joined = jnp.conj(spec_kernel) * spec_signal
        return jnp.fft.irfft(joined, 2 * seq_len, axis=-1)[:, :seq_len]

    result = lax.map(block_corr, (gated_grad.reshape(block_count, 64, seq_len), filter_coefficients.reshape(block_count, 64, seq_len)))
    return result.reshape(-1, seq_len)


def reference(grad_out, out_weight, gate_stream, conv_output, key_stream, value_stream, long_filter):
    grad_mix = jnp.dot(out_weight.astype(jnp.float32).T, grad_out.astype(jnp.float32).T, precision=lax.Precision.HIGHEST)
    grad_gate = (grad_mix * conv_output.astype(jnp.float32)).astype(jnp.bfloat16)
    gated_grad = (grad_mix * gate_stream.astype(jnp.float32)).astype(jnp.bfloat16)
    gated_grad = lax.optimization_barrier(gated_grad)
    corr_full = correlate(gated_grad.astype(jnp.float32), long_filter.astype(jnp.float32))
    grad_inner = lax.optimization_barrier(corr_full.astype(jnp.bfloat16))
    inner_wide = grad_inner.astype(jnp.float32)
    grad_key = (inner_wide * value_stream.astype(jnp.float32)).astype(jnp.bfloat16)
    grad_value = (inner_wide * key_stream.astype(jnp.float32)).astype(jnp.bfloat16)
    return (grad_gate, grad_key, grad_value)
```

```python
import functools
import math

import jax
import jax.numpy as jnp
import numpy as np
from jax import lax
from jax.experimental import pallas as pl
from jax.experimental.pallas import tpu as pltpu
from jax.sharding import PartitionSpec as P

VMEM_BYTES = 48 * 1024 * 1024


def split_table(table):
    high = table.astype(jnp.bfloat16)
    low = (table.astype(np.float32) - high.astype(np.float32)).astype(jnp.bfloat16)
    return high, low


def dft_constants(blocks, width):
    outer = 2 * blocks
    lines = blocks + 1
    lane = np.arange(width)
    twist = 2.0 * np.pi * (np.arange(lines)[:, None] * lane[None, :] % (outer * width)) / (outer * width)
    inner = 2.0 * np.pi * (lane[:, None] * lane[None, :] % width) / width
    cos, sin = np.cos(inner), np.sin(inner)
    forward = np.block([[cos, -sin], [sin, cos]]).astype(np.float32)
    backward = np.block([[cos, sin], [-sin, cos]]).astype(np.float32)
    twist = np.stack([np.cos(twist), np.sin(twist)]).astype(np.float32)
    return twist, split_table(forward), split_table(backward)


def scaled_sum(terms):
    total = None
    for scale, value in terms:
        if abs(scale) < 1e-12:
            continue
        if abs(scale - 1.0) < 1e-12:
            term = value
        elif abs(scale + 1.0) < 1e-12:
            term = -value
        else:
            term = value * np.float32(scale)
        total = term if total is None else total + term
    return total


def real_lines(parts, period):
    count = len(parts)
    half = period // 2
    if half % 2 or count < 2:
        cosines, sines = [], []
        for k in range(half + 1):
            angle = [2.0 * math.pi * (i * k % period) / period for i in range(count)]
            cosines.append(scaled_sum([(math.cos(a), p) for a, p in zip(angle, parts)]))
            sines.append(scaled_sum([(math.sin(a), p) for a, p in zip(angle, parts)]))
        return cosines, sines
    even_cos, even_sin = real_lines(parts[0::2], half)
    quarter = half // 2
    cosines, sines = [None] * (half + 1), [None] * (half + 1)
    odd = parts[1::2]
    for k in range(quarter + 1):
        angle = [2.0 * math.pi * ((2 * m + 1) * k % period) / period for m in range(len(odd))]
        odd_cos = scaled_sum([(math.cos(a), p) for a, p in zip(angle, odd)])
        odd_sin = scaled_sum([(math.sin(a), p) for a, p in zip(angle, odd)])
        cosines[k] = add(even_cos[k], odd_cos)
        sines[k] = add(even_sin[k], odd_sin)
        if k != half - k:
            cosines[half - k] = subtract(even_cos[k], odd_cos)
            sines[half - k] = subtract(odd_sin, even_sin[k])
    return cosines, sines


def add(a, b):
    if a is None or b is None:
        return b if a is None else a
    return a + b


def subtract(a, b):
    if b is None:
        return a
    return -b if a is None else a - b


def real_parts(re, im, period, count):
    half = period // 2
    if half % 2 or count < 2:
        out = []
        for i in range(count):
            angle = [2.0 * math.pi * (i * k % period) / period for k in range(half + 1)]
            terms = [(math.cos(a), r) for a, r in zip(angle, re) if r is not None]
            terms += [(-math.sin(a), m) for a, m in zip(angle, im) if m is not None]
            out.append(scaled_sum(terms))
        return out
    quarter = half // 2
    sum_re, sum_im, gap_re, gap_im = [], [], [], []
    for k in range(quarter + 1):
        if k == half - k:
            sum_re.append(re[k]); sum_im.append(None)
            gap_re.append(None); gap_im.append(im[k])
        else:
            sum_re.append(add(re[k], re[half - k])); sum_im.append(subtract(im[k], im[half - k]))
            gap_re.append(subtract(re[k], re[half - k])); gap_im.append(add(im[k], im[half - k]))
    out = [None] * count
    out[0::2] = real_parts(sum_re, sum_im, half, (count + 1) // 2)
    for i in range(1, count, 2):
        angle = [2.0 * math.pi * (i * k % period) / period for k in range(quarter + 1)]
        terms = [(math.cos(a), r) for a, r in zip(angle, gap_re) if r is not None]
        terms += [(-math.sin(a), m) for a, m in zip(angle, gap_im) if m is not None]
        out[i] = scaled_sum(terms)
    return out


def put_split(pair_ref, row, rows, re, im):
    width = re.shape[-1]
    for at, value in ((0, re), (1, im)):
        high = value.astype(jnp.bfloat16)
        low = (value - high.astype(jnp.float32)).astype(jnp.bfloat16)
        pair_ref[row : row + rows, at * width : (at + 1) * width] = high
        pair_ref[row : row + rows, (2 + at) * width : (3 + at) * width] = low


def wide_dot(pair, high, low):
    depth = high.shape[0]
    return (
        jnp.dot(pair[:, :depth], high, preferred_element_type=jnp.float32)
        + jnp.dot(pair[:, depth:], high, preferred_element_type=jnp.float32)
        + jnp.dot(pair[:, :depth], low, preferred_element_type=jnp.float32)
    )


def to_spectrum(read, twist_ref, high_ref, low_ref, pair_ref, out_ref, blocks, channels, rows):
    width = twist_ref.shape[2]
    for at in range(0, channels, rows):
        parts = [read(i, at).astype(jnp.float32) for i in range(blocks)]
        cosines, sines = real_lines(parts, 2 * blocks)
        for k in range(blocks + 1):
            turn_cos, turn_sin = twist_ref[0, k : k + 1, :], twist_ref[1, k : k + 1, :]
            re, im = cosines[k], sines[k]
            if im is None:
                new_re, new_im = re * turn_cos, -(re * turn_sin)
            else:
                new_re, new_im = re * turn_cos - im * turn_sin, -(re * turn_sin + im * turn_cos)
            put_split(pair_ref, k * channels + at, rows, new_re, new_im)
    out_ref[...] = wide_dot(pair_ref[...], high_ref[...], low_ref[...])


def filter_kernel(blocks, rows, taps_ref, twist_ref, high_ref, low_ref, out_ref, pair_ref, spec_ref):
    channels = taps_ref.shape[0]
    width = twist_ref.shape[2]
    to_spectrum(
        lambda i, at: taps_ref[at : at + rows, i * width : (i + 1) * width],
        twist_ref, high_ref, low_ref, pair_ref, spec_ref, blocks, channels, rows,
    )
    total = 2 * blocks * width
    for k in range(blocks + 1):
        scale = (1.0 if k in (0, blocks) else 2.0) / total
        out_ref[k] = spec_ref[k * channels : (k + 1) * channels, :] * np.float32(scale)


def filter_spectrum(taps, blocks, step):
    channels, length = taps.shape
    width = length // blocks
    twist, forward, _ = dft_constants(blocks, width)
    lines = blocks + 1
    whole = lambda *shape: pl.BlockSpec(shape, lambda c: (0,) * len(shape))
    return pl.pallas_call(
        functools.partial(filter_kernel, blocks, min(16, step)),
        grid=(channels // step,),
        in_specs=[
            pl.BlockSpec((step, length), lambda c: (c, 0)),
            whole(2, lines, width), whole(2 * width, 2 * width), whole(2 * width, 2 * width),
        ],
        out_specs=pl.BlockSpec((lines, step, 2 * width), lambda c: (0, c, 0)),
        out_shape=jax.ShapeDtypeStruct((lines, channels, 2 * width), jnp.float32),
        scratch_shapes=[
            pltpu.VMEM((lines * step, 4 * width), jnp.bfloat16),
            pltpu.VMEM((lines * step, 2 * width), jnp.float32),
        ],
        compiler_params=pltpu.CompilerParams(vmem_limit_bytes=VMEM_BYTES),
        name="filter_spectrum",
    )(taps, twist, *forward)


def correlate_kernel(
    blocks, rows, sig_ref, filt_ref, twist_ref, fh_ref, fl_ref, bh_ref, bl_ref, out_ref, pair_ref, spec_ref
):
    channels, width = sig_ref.shape[1:]
    to_spectrum(
        lambda i, at: sig_ref[i, at : at + rows, :],
        twist_ref, fh_ref, fl_ref, pair_ref, spec_ref, blocks, channels, rows,
    )
    for k in range(blocks + 1):
        for at in range(0, channels, rows):
            row = k * channels + at
            sig_re = spec_ref[row : row + rows, :width]
            sig_im = spec_ref[row : row + rows, width:]
            filt_re = filt_ref[k, at : at + rows, :width]
            filt_im = filt_ref[k, at : at + rows, width:]
            put_split(
                pair_ref, row, rows,
                filt_re * sig_re + filt_im * sig_im, filt_re * sig_im - filt_im * sig_re,
            )
    spec_ref[...] = wide_dot(pair_ref[...], bh_ref[...], bl_ref[...])
    for at in range(0, channels, rows):
        re_lines, im_lines = [], []
        for k in range(blocks + 1):
            turn_cos, turn_sin = twist_ref[0, k : k + 1, :], twist_ref[1, k : k + 1, :]
            row = k * channels + at
            re, im = spec_ref[row : row + rows, :width], spec_ref[row : row + rows, width:]
            re_lines.append(re * turn_cos - im * turn_sin)
            im_lines.append(re * turn_sin + im * turn_cos)
        for i, value in enumerate(real_parts(re_lines, im_lines, 2 * blocks, blocks)):
            out_ref[i, at : at + rows, :] = value.astype(jnp.bfloat16)


def correlate(signal, spectrum, step):
    blocks, channels, width = signal.shape
    twist, forward, backward = dft_constants(blocks, width)
    lines = blocks + 1
    whole = lambda *shape: pl.BlockSpec(shape, lambda c: (0,) * len(shape))
    table = whole(2 * width, 2 * width)
    return pl.pallas_call(
        functools.partial(correlate_kernel, blocks, min(16, step)),
        grid=(channels // step,),
        in_specs=[
            pl.BlockSpec((blocks, step, width), lambda c: (0, c, 0)),
            pl.BlockSpec((lines, step, 2 * width), lambda c: (0, c, 0)),
            whole(2, lines, width), table, table, table, table,
        ],
        out_specs=pl.BlockSpec((blocks, step, width), lambda c: (0, c, 0)),
        out_shape=jax.ShapeDtypeStruct((blocks, channels, width), jnp.bfloat16),
        scratch_shapes=[
            pltpu.VMEM((lines * step, 4 * width), jnp.bfloat16),
            pltpu.VMEM((lines * step, 2 * width), jnp.float32),
        ],
        compiler_params=pltpu.CompilerParams(vmem_limit_bytes=VMEM_BYTES),
        name="correlate",
    )(signal, spectrum, twist, *forward, *backward)


def dft_tables(count_outer, count_inner):
    total_len = count_outer * count_inner
    index_outer = jnp.arange(count_outer, dtype=jnp.int32)
    index_inner = jnp.arange(count_inner, dtype=jnp.int32)
    angle_outer = (index_outer[:, None] * index_outer[None, :] % count_outer).astype(
        jnp.float32
    ) * (2.0 * math.pi / count_outer)
    angle_inner = (index_inner[:, None] * index_inner[None, :] % count_inner).astype(
        jnp.float32
    ) * (2.0 * math.pi / count_inner)
    angle_twist = (index_outer[:, None] * index_inner[None, :] % total_len).astype(jnp.float32) * (
        2.0 * math.pi / total_len
    )
    return (
        jnp.cos(angle_outer),
        -jnp.sin(angle_outer),
        jnp.cos(angle_inner),
        -jnp.sin(angle_inner),
        jnp.cos(angle_twist),
        -jnp.sin(angle_twist),
    )


def outer_exact(table, signal):
    table_high = table.astype(jnp.bfloat16)
    table_low = (table - table_high.astype(jnp.float32)).astype(jnp.bfloat16)
    first = jnp.einsum("ab,cbk->cak", table_high, signal, preferred_element_type=jnp.float32)
    return first + jnp.einsum("ab,cbk->cak", table_low, signal, preferred_element_type=jnp.float32)


def outer_wide(table, values):
    return jnp.einsum(
        "ab,cbk->cak",
        table,
        values,
        precision=lax.Precision.HIGH,
        preferred_element_type=jnp.float32,
    )


def inner_wide(values, table):
    return jnp.einsum(
        "cak,kl->cal",
        values,
        table,
        precision=lax.Precision.HIGH,
        preferred_element_type=jnp.float32,
    )


def spectral_forward(signal, tables):
    outer_cos, outer_sin, inner_cos, inner_sin, twist_cos, twist_sin = tables
    part_re = outer_exact(outer_cos, signal)
    part_im = outer_exact(outer_sin, signal)
    turned_re = part_re * twist_cos - part_im * twist_sin
    turned_im = part_re * twist_sin + part_im * twist_cos
    spec_re = inner_wide(turned_re, inner_cos) - inner_wide(turned_im, inner_sin)
    spec_im = inner_wide(turned_re, inner_sin) + inner_wide(turned_im, inner_cos)
    return (spec_re, spec_im)


def spectral_inverse_real(spec_re, spec_im, tables):
    outer_cos, outer_sin, inner_cos, inner_sin, twist_cos, twist_sin = tables
    back_re = inner_wide(spec_re, inner_cos) + inner_wide(spec_im, inner_sin)
    back_im = inner_wide(spec_im, inner_cos) - inner_wide(spec_re, inner_sin)
    turned_re = back_re * twist_cos + back_im * twist_sin
    turned_im = back_im * twist_cos - back_re * twist_sin
    total_len = spec_re.shape[1] * spec_re.shape[2]
    return (outer_wide(outer_cos, turned_re) + outer_wide(outer_sin, turned_im)) / total_len


def correlate_plain(gathered, filters, tables):
    channel_count, seq_len = gathered.shape
    count_outer = tables[0].shape[0]
    count_inner = tables[2].shape[0]
    padding = jnp.zeros((2 * channel_count, seq_len), jnp.bfloat16)
    stacked = jnp.concatenate([gathered, filters], axis=0)
    padded = jnp.concatenate([stacked, padding], axis=1).reshape(
        2 * channel_count, count_outer, count_inner
    )
    both_re, both_im = spectral_forward(padded, tables)
    signal_re, kernel_re = (both_re[:channel_count], both_re[channel_count:])
    signal_im, kernel_im = (both_im[:channel_count], both_im[channel_count:])
    joined_re = kernel_re * signal_re + kernel_im * signal_im
    joined_im = kernel_re * signal_im - kernel_im * signal_re
    result = spectral_inverse_real(joined_re, joined_im, tables)
    return result.reshape(channel_count, -1)[:, :seq_len].astype(jnp.bfloat16)


def per_device_gathered(
    grad_out, out_weight, gate_stream, conv_output, key_stream, value_stream, long_filter
):
    seq_count = lax.axis_size("seq")
    token_count = grad_out.shape[0]
    chan_width = out_weight.shape[1]
    group_width = chan_width // seq_count
    full_grad = lax.all_gather(grad_out, "chan", axis=1, tiled=True)
    tables = dft_tables(2 * seq_count, token_count)
    grad_mix = jnp.einsum(
        "nc,tn->ct",
        lax.all_gather(out_weight, "seq", axis=0, tiled=True),
        full_grad,
        preferred_element_type=jnp.float32,
    )
    gated_grad = (grad_mix * gate_stream.astype(jnp.float32)).astype(jnp.bfloat16)
    regrouped = lax.all_to_all(
        gated_grad.reshape(seq_count, group_width, token_count),
        "seq",
        split_axis=0,
        concat_axis=2,
        tiled=True,
    )
    inner_grad = correlate_plain(regrouped[0], long_filter, tables)
    returned = lax.all_to_all(inner_grad[None], "seq", split_axis=2, concat_axis=0, tiled=True)
    grad_inner = returned.reshape(chan_width, token_count)
    grad_gate = (grad_mix * conv_output.astype(jnp.float32)).astype(jnp.bfloat16)
    inner_grad_wide = grad_inner.astype(jnp.float32)
    grad_key = (inner_grad_wide * value_stream.astype(jnp.float32)).astype(jnp.bfloat16)
    grad_value = (inner_grad_wide * key_stream.astype(jnp.float32)).astype(jnp.bfloat16)
    return (grad_gate, grad_key, grad_value)


def mix_kernel(block_rows, slot_ref, grad_ref, *refs):
    pieces, (own_ref, other_ref) = refs[:-2], refs[-2:]
    total = None
    for distance, piece in enumerate(pieces):
        at = pl.multiple_of((slot_ref[0] ^ distance) * block_rows, block_rows)
        term = jnp.dot(grad_ref[:, pl.ds(at, block_rows)], piece[...], preferred_element_type=jnp.float32)
        total = term if total is None else total + term
    mixed = total.T
    tokens = own_ref.shape[1]
    own_ref[...] = mixed[:, :tokens]
    other_ref[...] = mixed[:, tokens:].astype(jnp.bfloat16)


def partial_mix(slot, grads, pieces, step):
    rows, channels = pieces[0].shape
    tokens, depth = grads.shape
    half = tokens // 2
    out_spec = pl.BlockSpec((step, half), lambda c: (c, 0))
    return pl.pallas_call(
        functools.partial(mix_kernel, rows),
        grid=(channels // step,),
        in_specs=[
            pl.BlockSpec(memory_space=pltpu.SMEM),
            pl.BlockSpec((tokens, depth), lambda c: (0, 0)),
        ]
        + [pl.BlockSpec((rows, step), lambda c: (0, c)) for _ in pieces],
        out_specs=(out_spec, out_spec),
        out_shape=(
            jax.ShapeDtypeStruct((channels, half), jnp.float32),
            jax.ShapeDtypeStruct((channels, half), jnp.bfloat16),
        ),
        compiler_params=pltpu.CompilerParams(vmem_limit_bytes=VMEM_BYTES),
        cost_estimate=pl.CostEstimate(
            flops=2 * tokens * depth * channels, bytes_accessed=2 * depth * (channels + tokens), transcendentals=0
        ),
        name="partial_mix",
    )(slot, grads, *pieces)


def swap(values, axis, count, mask):
    return lax.ppermute(values, axis, [(i, i ^ mask) for i in range(count)])


def per_device(
    grad_out, out_weight, gate_stream, conv_output, key_stream, value_stream, long_filter
):
    seq_count = lax.axis_size("seq")
    token_count, shard_features = grad_out.shape
    weight_rows, chan_width = out_weight.shape
    group_width = chan_width // seq_count
    group = seq_count // 2
    place = lax.axis_index("seq")
    side = place // group
    spectrum = filter_spectrum(long_filter, seq_count, min(16, group_width))

    shard = lax.axis_index("chan")
    peer_grad = swap(grad_out, "chan", 2, 1)
    mine, theirs = (
        jnp.where(shard == want, grad_out, peer_grad) for want in (side, 1 - side)
    )
    peer_tokens = swap(theirs, "seq", seq_count, group)
    grads = jnp.concatenate([mine, peer_tokens], axis=0)

    half = chan_width // 2
    near, far = 2, 4
    across = swap(out_weight, "seq", seq_count, near)
    along = swap(out_weight, "seq", seq_count, far)
    corner_a = swap(across[:, :half], "seq", seq_count, far)
    corner_b = swap(along[:, half:], "seq", seq_count, near)
    corner = jnp.concatenate([corner_a, corner_b], axis=1)
    same = [out_weight, across, along, corner]
    pieces = []
    for piece in same:
        pieces += [piece, swap(piece, "seq", seq_count, 1)]
    slot = (place % group).reshape(1).astype(jnp.int32)
    own, other = partial_mix(slot, grads, pieces, min(512, chan_width))
    received = swap(other, "seq", seq_count, group)
    grad_mix = own + received.astype(jnp.float32)

    gated_grad = (grad_mix * gate_stream.astype(jnp.float32)).astype(jnp.bfloat16)
    regrouped = lax.all_to_all(
        gated_grad.reshape(seq_count, group_width, token_count), "seq", split_axis=0, concat_axis=0, tiled=True
    )
    inner_grad = correlate(regrouped, spectrum, min(16, group_width))
    returned = lax.all_to_all(inner_grad, "seq", split_axis=0, concat_axis=0, tiled=True)
    grad_inner = returned.reshape(chan_width, token_count).astype(jnp.float32)
    grad_gate = (grad_mix * conv_output.astype(jnp.float32)).astype(jnp.bfloat16)
    grad_key = (grad_inner * value_stream.astype(jnp.float32)).astype(jnp.bfloat16)
    grad_value = (grad_inner * key_stream.astype(jnp.float32)).astype(jnp.bfloat16)
    return (grad_gate, grad_key, grad_value)


def solution(mesh):
    in_specs = (
        P("seq", "chan"),
        P("seq", "chan"),
        P("chan", "seq"),
        P("chan", "seq"),
        P("chan", "seq"),
        P("chan", "seq"),
        P(("chan", "seq"), None),
    )
    out_specs = (P("chan", "seq"), P("chan", "seq"), P("chan", "seq"))
    square = mesh.shape["chan"] == 2 and mesh.shape["seq"] == 16
    return jax.shard_map(
        per_device if square else per_device_gathered,
        mesh=mesh, in_specs=in_specs, out_specs=out_specs, check_vma=False,
    )
```

```python
import functools
import math

import jax
import jax.numpy as jnp
import numpy as np
from jax import lax
from jax.experimental import pallas as pl
from jax.experimental.pallas import tpu as pltpu
from jax.sharding import PartitionSpec as P

VMEM_BYTES = 48 * 1024 * 1024


def split_table(table):
    high = table.astype(jnp.bfloat16)
    low = (table.astype(np.float32) - high.astype(np.float32)).astype(jnp.bfloat16)
    return high, low


def dft_constants(blocks, width):
    outer = 2 * blocks
    lines = blocks + 1
    lane = np.arange(width)
    twist = 2.0 * np.pi * (np.arange(lines)[:, None] * lane[None, :] % (outer * width)) / (outer * width)
    inner = 2.0 * np.pi * (lane[:, None] * lane[None, :] % width) / width
    cos, sin = np.cos(inner), np.sin(inner)
    forward = np.block([[cos, -sin], [sin, cos]]).astype(np.float32)
    backward = np.block([[cos, sin], [-sin, cos]]).astype(np.float32)
    twist = np.stack([np.cos(twist), np.sin(twist)]).astype(np.float32)
    return twist, split_table(forward), split_table(backward)


def scaled_sum(terms):
    total = None
    for scale, value in terms:
        if abs(scale) < 1e-12:
            continue
        if abs(scale - 1.0) < 1e-12:
            term = value
        elif abs(scale + 1.0) < 1e-12:
            term = -value
        else:
            term = value * np.float32(scale)
        total = term if total is None else total + term
    return total


def real_lines(parts, period):
    count = len(parts)
    half = period // 2
    if half % 2 or count < 2:
        cosines, sines = [], []
        for k in range(half + 1):
            angle = [2.0 * math.pi * (i * k % period) / period for i in range(count)]
            cosines.append(scaled_sum([(math.cos(a), p) for a, p in zip(angle, parts)]))
            sines.append(scaled_sum([(math.sin(a), p) for a, p in zip(angle, parts)]))
        return cosines, sines
    even_cos, even_sin = real_lines(parts[0::2], half)
    quarter = half // 2
    cosines, sines = [None] * (half + 1), [None] * (half + 1)
    odd = parts[1::2]
    for k in range(quarter + 1):
        angle = [2.0 * math.pi * ((2 * m + 1) * k % period) / period for m in range(len(odd))]
        odd_cos = scaled_sum([(math.cos(a), p) for a, p in zip(angle, odd)])
        odd_sin = scaled_sum([(math.sin(a), p) for a, p in zip(angle, odd)])
        cosines[k] = add(even_cos[k], odd_cos)
        sines[k] = add(even_sin[k], odd_sin)
        if k != half - k:
            cosines[half - k] = subtract(even_cos[k], odd_cos)
            sines[half - k] = subtract(odd_sin, even_sin[k])
    return cosines, sines


def add(a, b):
    if a is None or b is None:
        return b if a is None else a
    return a + b


def subtract(a, b):
    if b is None:
        return a
    return -b if a is None else a - b


def real_parts(re, im, period, count):
    half = period // 2
    if half % 2 or count < 2:
        out = []
        for i in range(count):
            angle = [2.0 * math.pi * (i * k % period) / period for k in range(half + 1)]
            terms = [(math.cos(a), r) for a, r in zip(angle, re) if r is not None]
            terms += [(-math.sin(a), m) for a, m in zip(angle, im) if m is not None]
            out.append(scaled_sum(terms))
        return out
    quarter = half // 2
    sum_re, sum_im, gap_re, gap_im = [], [], [], []
    for k in range(quarter + 1):
        if k == half - k:
            sum_re.append(re[k]); sum_im.append(None)
            gap_re.append(None); gap_im.append(im[k])
        else:
            sum_re.append(add(re[k], re[half - k])); sum_im.append(subtract(im[k], im[half - k]))
            gap_re.append(subtract(re[k], re[half - k])); gap_im.append(add(im[k], im[half - k]))
    out = [None] * count
    out[0::2] = real_parts(sum_re, sum_im, half, (count + 1) // 2)
    for i in range(1, count, 2):
        angle = [2.0 * math.pi * (i * k % period) / period for k in range(quarter + 1)]
        terms = [(math.cos(a), r) for a, r in zip(angle, gap_re) if r is not None]
        terms += [(-math.sin(a), m) for a, m in zip(angle, gap_im) if m is not None]
        out[i] = scaled_sum(terms)
    return out


def put_split(pair_ref, row, rows, re, im):
    width = re.shape[-1]
    for at, value in ((0, re), (1, im)):
        high = value.astype(jnp.bfloat16)
        low = (value - high.astype(jnp.float32)).astype(jnp.bfloat16)
        pair_ref[row : row + rows, at * width : (at + 1) * width] = high
        pair_ref[row : row + rows, (2 + at) * width : (3 + at) * width] = low


def wide_dot(pair, high, low):
    depth = high.shape[0]
    return (
        jnp.dot(pair[:, :depth], high, preferred_element_type=jnp.float32)
        + jnp.dot(pair[:, depth:], high, preferred_element_type=jnp.float32)
        + jnp.dot(pair[:, :depth], low, preferred_element_type=jnp.float32)
    )


def to_spectrum(read, twist_ref, high_ref, low_ref, pair_ref, out_ref, blocks, channels, rows):
    width = twist_ref.shape[2]
    for at in range(0, channels, rows):
        parts = [read(i, at).astype(jnp.float32) for i in range(blocks)]
        cosines, sines = real_lines(parts, 2 * blocks)
        for k in range(blocks + 1):
            turn_cos, turn_sin = twist_ref[0, k : k + 1, :], twist_ref[1, k : k + 1, :]
            re, im = cosines[k], sines[k]
            if im is None:
                new_re, new_im = re * turn_cos, -(re * turn_sin)
            else:
                new_re, new_im = re * turn_cos - im * turn_sin, -(re * turn_sin + im * turn_cos)
            put_split(pair_ref, k * channels + at, rows, new_re, new_im)
    out_ref[...] = wide_dot(pair_ref[...], high_ref[...], low_ref[...])


def filter_kernel(blocks, rows, taps_ref, twist_ref, high_ref, low_ref, out_ref, pair_ref, spec_ref):
    channels = taps_ref.shape[0]
    width = twist_ref.shape[2]
    to_spectrum(
        lambda i, at: taps_ref[at : at + rows, i * width : (i + 1) * width],
        twist_ref, high_ref, low_ref, pair_ref, spec_ref, blocks, channels, rows,
    )
    total = 2 * blocks * width
    for k in range(blocks + 1):
        scale = (1.0 if k in (0, blocks) else 2.0) / total
        out_ref[k] = spec_ref[k * channels : (k + 1) * channels, :] * np.float32(scale)


def filter_spectrum(taps, blocks, step):
    channels, length = taps.shape
    width = length // blocks
    twist, forward, _ = dft_constants(blocks, width)
    lines = blocks + 1
    whole = lambda *shape: pl.BlockSpec(shape, lambda c: (0,) * len(shape))
    return pl.pallas_call(
        functools.partial(filter_kernel, blocks, min(16, step)),
        grid=(channels // step,),
        in_specs=[
            pl.BlockSpec((step, length), lambda c: (c, 0)),
            whole(2, lines, width), whole(2 * width, 2 * width), whole(2 * width, 2 * width),
        ],
        out_specs=pl.BlockSpec((lines, step, 2 * width), lambda c: (0, c, 0)),
        out_shape=jax.ShapeDtypeStruct((lines, channels, 2 * width), jnp.float32),
        scratch_shapes=[
            pltpu.VMEM((lines * step, 4 * width), jnp.bfloat16),
            pltpu.VMEM((lines * step, 2 * width), jnp.float32),
        ],
        compiler_params=pltpu.CompilerParams(vmem_limit_bytes=VMEM_BYTES),
        name="filter_spectrum",
    )(taps, twist, *forward)


def correlate_kernel(
    blocks, rows, sig_ref, filt_ref, twist_ref, fh_ref, fl_ref, bh_ref, bl_ref, out_ref, pair_ref, spec_ref
):
    channels, width = sig_ref.shape[1:]
    to_spectrum(
        lambda i, at: sig_ref[i, at : at + rows, :],
        twist_ref, fh_ref, fl_ref, pair_ref, spec_ref, blocks, channels, rows,
    )
    for k in range(blocks + 1):
        for at in range(0, channels, rows):
            row = k * channels + at
            sig_re = spec_ref[row : row + rows, :width]
            sig_im = spec_ref[row : row + rows, width:]
            filt_re = filt_ref[k, at : at + rows, :width]
            filt_im = filt_ref[k, at : at + rows, width:]
            put_split(
                pair_ref, row, rows,
                filt_re * sig_re + filt_im * sig_im, filt_re * sig_im - filt_im * sig_re,
            )
    spec_ref[...] = wide_dot(pair_ref[...], bh_ref[...], bl_ref[...])
    for at in range(0, channels, rows):
        re_lines, im_lines = [], []
        for k in range(blocks + 1):
            turn_cos, turn_sin = twist_ref[0, k : k + 1, :], twist_ref[1, k : k + 1, :]
            row = k * channels + at
            re, im = spec_ref[row : row + rows, :width], spec_ref[row : row + rows, width:]
            re_lines.append(re * turn_cos - im * turn_sin)
            im_lines.append(re * turn_sin + im * turn_cos)
        for i, value in enumerate(real_parts(re_lines, im_lines, 2 * blocks, blocks)):
            out_ref[i, at : at + rows, :] = value.astype(jnp.bfloat16)


def correlate(signal, spectrum, step):
    blocks, channels, width = signal.shape
    twist, forward, backward = dft_constants(blocks, width)
    lines = blocks + 1
    whole = lambda *shape: pl.BlockSpec(shape, lambda c: (0,) * len(shape))
    table = whole(2 * width, 2 * width)
    return pl.pallas_call(
        functools.partial(correlate_kernel, blocks, min(16, step)),
        grid=(channels // step,),
        in_specs=[
            pl.BlockSpec((blocks, step, width), lambda c: (0, c, 0)),
            pl.BlockSpec((lines, step, 2 * width), lambda c: (0, c, 0)),
            whole(2, lines, width), table, table, table, table,
        ],
        out_specs=pl.BlockSpec((blocks, step, width), lambda c: (0, c, 0)),
        out_shape=jax.ShapeDtypeStruct((blocks, channels, width), jnp.bfloat16),
        scratch_shapes=[
            pltpu.VMEM((lines * step, 4 * width), jnp.bfloat16),
            pltpu.VMEM((lines * step, 2 * width), jnp.float32),
        ],
        compiler_params=pltpu.CompilerParams(vmem_limit_bytes=VMEM_BYTES),
        name="correlate",
    )(signal, spectrum, twist, *forward, *backward)


def dft_tables(count_outer, count_inner):
    total_len = count_outer * count_inner
    index_outer = jnp.arange(count_outer, dtype=jnp.int32)
    index_inner = jnp.arange(count_inner, dtype=jnp.int32)
    angle_outer = (index_outer[:, None] * index_outer[None, :] % count_outer).astype(
        jnp.float32
    ) * (2.0 * math.pi / count_outer)
    angle_inner = (index_inner[:, None] * index_inner[None, :] % count_inner).astype(
        jnp.float32
    ) * (2.0 * math.pi / count_inner)
    angle_twist = (index_outer[:, None] * index_inner[None, :] % total_len).astype(jnp.float32) * (
        2.0 * math.pi / total_len
    )
    return (
        jnp.cos(angle_outer),
        -jnp.sin(angle_outer),
        jnp.cos(angle_inner),
        -jnp.sin(angle_inner),
        jnp.cos(angle_twist),
        -jnp.sin(angle_twist),
    )


def outer_exact(table, signal):
    table_high = table.astype(jnp.bfloat16)
    table_low = (table - table_high.astype(jnp.float32)).astype(jnp.bfloat16)
    first = jnp.einsum("ab,cbk->cak", table_high, signal, preferred_element_type=jnp.float32)
    return first + jnp.einsum("ab,cbk->cak", table_low, signal, preferred_element_type=jnp.float32)


def outer_wide(table, values):
    return jnp.einsum(
        "ab,cbk->cak",
        table,
        values,
        precision=lax.Precision.HIGH,
        preferred_element_type=jnp.float32,
    )


def inner_wide(values, table):
    return jnp.einsum(
        "cak,kl->cal",
        values,
        table,
        precision=lax.Precision.HIGH,
        preferred_element_type=jnp.float32,
    )


def spectral_forward(signal, tables):
    outer_cos, outer_sin, inner_cos, inner_sin, twist_cos, twist_sin = tables
    part_re = outer_exact(outer_cos, signal)
    part_im = outer_exact(outer_sin, signal)
    turned_re = part_re * twist_cos - part_im * twist_sin
    turned_im = part_re * twist_sin + part_im * twist_cos
    spec_re = inner_wide(turned_re, inner_cos) - inner_wide(turned_im, inner_sin)
    spec_im = inner_wide(turned_re, inner_sin) + inner_wide(turned_im, inner_cos)
    return (spec_re, spec_im)


def spectral_inverse_real(spec_re, spec_im, tables):
    outer_cos, outer_sin, inner_cos, inner_sin, twist_cos, twist_sin = tables
    back_re = inner_wide(spec_re, inner_cos) + inner_wide(spec_im, inner_sin)
    back_im = inner_wide(spec_im, inner_cos) - inner_wide(spec_re, inner_sin)
    turned_re = back_re * twist_cos + back_im * twist_sin
    turned_im = back_im * twist_cos - back_re * twist_sin
    total_len = spec_re.shape[1] * spec_re.shape[2]
    return (outer_wide(outer_cos, turned_re) + outer_wide(outer_sin, turned_im)) / total_len


def correlate_plain(gathered, filters, tables):
    channel_count, seq_len = gathered.shape
    count_outer = tables[0].shape[0]
    count_inner = tables[2].shape[0]
    padding = jnp.zeros((2 * channel_count, seq_len), jnp.bfloat16)
    stacked = jnp.concatenate([gathered, filters], axis=0)
    padded = jnp.concatenate([stacked, padding], axis=1).reshape(
        2 * channel_count, count_outer, count_inner
    )
    both_re, both_im = spectral_forward(padded, tables)
    signal_re, kernel_re = (both_re[:channel_count], both_re[channel_count:])
    signal_im, kernel_im = (both_im[:channel_count], both_im[channel_count:])
    joined_re = kernel_re * signal_re + kernel_im * signal_im
    joined_im = kernel_re * signal_im - kernel_im * signal_re
    result = spectral_inverse_real(joined_re, joined_im, tables)
    return result.reshape(channel_count, -1)[:, :seq_len].astype(jnp.bfloat16)


def per_device_gathered(
    grad_out, out_weight, gate_stream, conv_output, key_stream, value_stream, long_filter
):
    seq_count = lax.axis_size("seq")
    token_count = grad_out.shape[0]
    chan_width = out_weight.shape[1]
    group_width = chan_width // seq_count
    full_grad = lax.all_gather(grad_out, "chan", axis=1, tiled=True)
    tables = dft_tables(2 * seq_count, token_count)
    grad_mix = jnp.einsum(
        "nc,tn->ct",
        lax.all_gather(out_weight, "seq", axis=0, tiled=True),
        full_grad,
        preferred_element_type=jnp.float32,
    )
    gated_grad = (grad_mix * gate_stream.astype(jnp.float32)).astype(jnp.bfloat16)
    regrouped = lax.all_to_all(
        gated_grad.reshape(seq_count, group_width, token_count),
        "seq",
        split_axis=0,
        concat_axis=2,
        tiled=True,
    )
    inner_grad = correlate_plain(regrouped[0], long_filter, tables)
    returned = lax.all_to_all(inner_grad[None], "seq", split_axis=2, concat_axis=0, tiled=True)
    grad_inner = returned.reshape(chan_width, token_count)
    grad_gate = (grad_mix * conv_output.astype(jnp.float32)).astype(jnp.bfloat16)
    inner_grad_wide = grad_inner.astype(jnp.float32)
    grad_key = (inner_grad_wide * value_stream.astype(jnp.float32)).astype(jnp.bfloat16)
    grad_value = (inner_grad_wide * key_stream.astype(jnp.float32)).astype(jnp.bfloat16)
    return (grad_gate, grad_key, grad_value)


def mix_kernel(block_rows, slot_ref, grad_ref, *refs):
    pieces, (own_ref, other_ref) = refs[:-2], refs[-2:]
    total = None
    for distance, piece in enumerate(pieces):
        at = pl.multiple_of((slot_ref[0] ^ distance) * block_rows, block_rows)
        term = jnp.dot(grad_ref[:, pl.ds(at, block_rows)], piece[...], preferred_element_type=jnp.float32)
        total = term if total is None else total + term
    mixed = total.T
    tokens = own_ref.shape[1]
    own_ref[...] = mixed[:, :tokens]
    other_ref[...] = mixed[:, tokens:].astype(jnp.bfloat16)


def partial_mix(slot, grads, pieces, step):
    rows, channels = pieces[0].shape
    tokens, depth = grads.shape
    half = tokens // 2
    out_spec = pl.BlockSpec((step, half), lambda c: (c, 0))
    return pl.pallas_call(
        functools.partial(mix_kernel, rows),
        grid=(channels // step,),
        in_specs=[
            pl.BlockSpec(memory_space=pltpu.SMEM),
            pl.BlockSpec((tokens, depth), lambda c: (0, 0)),
        ]
        + [pl.BlockSpec((rows, step), lambda c: (0, c)) for _ in pieces],
        out_specs=(out_spec, out_spec),
        out_shape=(
            jax.ShapeDtypeStruct((channels, half), jnp.float32),
            jax.ShapeDtypeStruct((channels, half), jnp.bfloat16),
        ),
        compiler_params=pltpu.CompilerParams(vmem_limit_bytes=VMEM_BYTES),
        cost_estimate=pl.CostEstimate(
            flops=2 * tokens * depth * channels, bytes_accessed=2 * depth * (channels + tokens), transcendentals=0
        ),
        name="partial_mix",
    )(slot, grads, *pieces)


def swap(values, axis, count, mask):
    return lax.ppermute(values, axis, [(i, i ^ mask) for i in range(count)])


def per_device(
    grad_out, out_weight, gate_stream, conv_output, key_stream, value_stream, long_filter
):
    seq_count = lax.axis_size("seq")
    token_count, shard_features = grad_out.shape
    weight_rows, chan_width = out_weight.shape
    group_width = chan_width // seq_count
    group = seq_count // 2
    place = lax.axis_index("seq")
    side = place // group
    spectrum = filter_spectrum(long_filter, seq_count, min(16, group_width))

    shard = lax.axis_index("chan")
    home = shard == side
    rows = token_count // 2
    both = ("seq", "chan")
    at = lambda s, y: s * 2 + y
    away = [(s, 1 - s // group) for s in range(seq_count)]
    straight = [(at(s, y), at(s ^ group, y)) for s, y in away]
    slanted = [(at(s, y), at(s ^ group, 1 - y)) for s, y in away]
    beside = [(at(s, 1 - y), at(s, y)) for s, y in away]
    first = lax.ppermute(grad_out[:rows], both, straight)
    second = lax.ppermute(grad_out[rows:], both, slanted)
    local = lax.ppermute(grad_out, both, beside)
    half = chan_width // 2
    near, far = 2, 4
    across = swap(out_weight, "seq", seq_count, near)
    along = swap(out_weight, "seq", seq_count, far)
    across, along, first, second, local = lax.optimization_barrier((across, along, first, second, local))
    passed = swap(jnp.where(home, first, second), "chan", 2, 1)
    grads = jnp.concatenate(
        [jnp.where(home, grad_out, local), jnp.where(home, first, passed), jnp.where(home, passed, second)], axis=0
    )
    corner_a = swap(across[:, :half], "seq", seq_count, far)
    corner_b = swap(along[:, half:], "seq", seq_count, near)
    corner = jnp.concatenate([corner_a, corner_b], axis=1)
    same = [out_weight, across, along, corner]
    pieces = []
    for piece in same:
        pieces += [piece, swap(piece, "seq", seq_count, 1)]
    slot = (place % group).reshape(1).astype(jnp.int32)
    own, other = partial_mix(slot, grads, pieces, min(512, chan_width))
    received = swap(other, "seq", seq_count, group)
    grad_mix = own + received.astype(jnp.float32)

    gated_grad = (grad_mix * gate_stream.astype(jnp.float32)).astype(jnp.bfloat16)
    regrouped = lax.all_to_all(
        gated_grad.reshape(seq_count, group_width, token_count), "seq", split_axis=0, concat_axis=0, tiled=True
    )
    inner_grad = correlate(regrouped, spectrum, min(16, group_width))
    returned = lax.all_to_all(inner_grad, "seq", split_axis=0, concat_axis=0, tiled=True)
    grad_inner = returned.reshape(chan_width, token_count).astype(jnp.float32)
    grad_gate = (grad_mix * conv_output.astype(jnp.float32)).astype(jnp.bfloat16)
    grad_key = (grad_inner * value_stream.astype(jnp.float32)).astype(jnp.bfloat16)
    grad_value = (grad_inner * key_stream.astype(jnp.float32)).astype(jnp.bfloat16)
    return (grad_gate, grad_key, grad_value)


def solution(mesh):
    in_specs = (
        P("seq", "chan"),
        P("seq", "chan"),
        P("chan", "seq"),
        P("chan", "seq"),
        P("chan", "seq"),
        P("chan", "seq"),
        P(("chan", "seq"), None),
    )
    out_specs = (P("chan", "seq"), P("chan", "seq"), P("chan", "seq"))
    square = mesh.shape["chan"] == 2 and mesh.shape["seq"] == 16
    return jax.shard_map(
        per_device if square else per_device_gathered,
        mesh=mesh, in_specs=in_specs, out_specs=out_specs, check_vma=False,
    )
```

```python
import functools
import math

import jax
import jax.numpy as jnp
import numpy as np
from jax import lax
from jax.experimental import pallas as pl
from jax.experimental.pallas import tpu as pltpu
from jax.sharding import PartitionSpec as P

VMEM_BYTES = 16 * 1024 * 1024


def split_table(table):
    high = table.astype(jnp.bfloat16)
    low = (table.astype(np.float32) - high.astype(np.float32)).astype(jnp.bfloat16)
    return high, low


def dft_constants(blocks, width):
    outer = 2 * blocks
    lines = blocks + 1
    lane = np.arange(width)
    twist = 2.0 * np.pi * (np.arange(lines)[:, None] * lane[None, :] % (outer * width)) / (outer * width)
    inner = 2.0 * np.pi * (lane[:, None] * lane[None, :] % width) / width
    cos, sin = np.cos(inner), np.sin(inner)
    forward = np.block([[cos, -sin], [sin, cos]]).astype(np.float32)
    backward = np.block([[cos, sin], [-sin, cos]]).astype(np.float32)
    twist = np.stack([np.cos(twist), np.sin(twist)]).astype(np.float32)
    return twist, split_table(forward), split_table(backward)


def scaled_sum(terms):
    total = None
    for scale, value in terms:
        if abs(scale) < 1e-12:
            continue
        if abs(scale - 1.0) < 1e-12:
            term = value
        elif abs(scale + 1.0) < 1e-12:
            term = -value
        else:
            term = value * np.float32(scale)
        total = term if total is None else total + term
    return total


def real_lines(parts, period):
    count = len(parts)
    half = period // 2
    if half % 2 or count < 2:
        cosines, sines = [], []
        for k in range(half + 1):
            angle = [2.0 * math.pi * (i * k % period) / period for i in range(count)]
            cosines.append(scaled_sum([(math.cos(a), p) for a, p in zip(angle, parts)]))
            sines.append(scaled_sum([(math.sin(a), p) for a, p in zip(angle, parts)]))
        return cosines, sines
    even_cos, even_sin = real_lines(parts[0::2], half)
    quarter = half // 2
    cosines, sines = [None] * (half + 1), [None] * (half + 1)
    odd = parts[1::2]
    for k in range(quarter + 1):
        angle = [2.0 * math.pi * ((2 * m + 1) * k % period) / period for m in range(len(odd))]
        odd_cos = scaled_sum([(math.cos(a), p) for a, p in zip(angle, odd)])
        odd_sin = scaled_sum([(math.sin(a), p) for a, p in zip(angle, odd)])
        cosines[k] = add(even_cos[k], odd_cos)
        sines[k] = add(even_sin[k], odd_sin)
        if k != half - k:
            cosines[half - k] = subtract(even_cos[k], odd_cos)
            sines[half - k] = subtract(odd_sin, even_sin[k])
    return cosines, sines


def add(a, b):
    if a is None or b is None:
        return b if a is None else a
    return a + b


def subtract(a, b):
    if b is None:
        return a
    return -b if a is None else a - b


def real_parts(re, im, period, count):
    half = period // 2
    if half % 2 or count < 2:
        out = []
        for i in range(count):
            angle = [2.0 * math.pi * (i * k % period) / period for k in range(half + 1)]
            terms = [(math.cos(a), r) for a, r in zip(angle, re) if r is not None]
            terms += [(-math.sin(a), m) for a, m in zip(angle, im) if m is not None]
            out.append(scaled_sum(terms))
        return out
    quarter = half // 2
    sum_re, sum_im, gap_re, gap_im = [], [], [], []
    for k in range(quarter + 1):
        if k == half - k:
            sum_re.append(re[k]); sum_im.append(None)
            gap_re.append(None); gap_im.append(im[k])
        else:
            sum_re.append(add(re[k], re[half - k])); sum_im.append(subtract(im[k], im[half - k]))
            gap_re.append(subtract(re[k], re[half - k])); gap_im.append(add(im[k], im[half - k]))
    out = [None] * count
    out[0::2] = real_parts(sum_re, sum_im, half, (count + 1) // 2)
    for i in range(1, count, 2):
        angle = [2.0 * math.pi * (i * k % period) / period for k in range(quarter + 1)]
        terms = [(math.cos(a), r) for a, r in zip(angle, gap_re) if r is not None]
        terms += [(-math.sin(a), m) for a, m in zip(angle, gap_im) if m is not None]
        out[i] = scaled_sum(terms)
    return out


def put_split(pair_ref, row, rows, re, im):
    width = re.shape[-1]
    for at, value in ((0, re), (1, im)):
        high = value.astype(jnp.bfloat16)
        low = (value - high.astype(jnp.float32)).astype(jnp.bfloat16)
        pair_ref[row : row + rows, at * width : (at + 1) * width] = high
        pair_ref[row : row + rows, (2 + at) * width : (3 + at) * width] = low


def wide_dot(pair, high, low):
    depth = high.shape[0]
    return (
        jnp.dot(pair[:, :depth], high, preferred_element_type=jnp.float32)
        + jnp.dot(pair[:, depth:], high, preferred_element_type=jnp.float32)
        + jnp.dot(pair[:, :depth], low, preferred_element_type=jnp.float32)
    )


def to_spectrum(read, twist_ref, high_ref, low_ref, pair_ref, spec_ref, blocks, channels, rows):
    for at in range(0, channels, rows):
        parts = [read(i, at).astype(jnp.float32) for i in range(blocks)]
        cosines, sines = real_lines(parts, 2 * blocks)
        for k in range(blocks + 1):
            turn_cos, turn_sin = twist_ref[0, k : k + 1, :], twist_ref[1, k : k + 1, :]
            re, im = cosines[k], sines[k]
            if im is None:
                new_re, new_im = re * turn_cos, -(re * turn_sin)
            else:
                new_re, new_im = re * turn_cos - im * turn_sin, -(re * turn_sin + im * turn_cos)
            put_split(pair_ref, k * channels + at, rows, new_re, new_im)
    spec_ref[...] = wide_dot(pair_ref[...], high_ref[...], low_ref[...])


def each_step(channels, step, body):
    pl.loop(0, channels // step)(lambda c: body(pl.multiple_of(c * step, step)))


def table_fetch(hbm_refs, vmem_refs, sems):
    copies = [pltpu.make_async_copy(src, dst, sems.at[i]) for i, (src, dst) in enumerate(zip(hbm_refs, vmem_refs))]
    for copy in copies:
        copy.start()
    side = vmem_refs[1].shape[1]
    return copies, [vmem_refs[1].at[pl.ds(i * side, side)] for i in range(vmem_refs[1].shape[0] // side)]


def filter_kernel(blocks, step, rows, taps_ref, twist_hbm, packed_hbm, out_ref, pair_ref, spec_ref, twist_ref, packed_ref, sems):
    copies, (high_ref, low_ref) = table_fetch((twist_hbm, packed_hbm), (twist_ref, packed_ref), sems)
    channels, length = taps_ref.shape
    width = length // blocks
    total = 2 * blocks * width
    for copy in copies:
        copy.wait()

    def body(start):
        to_spectrum(
            lambda i, at: taps_ref[pl.ds(start + at, rows), i * width : (i + 1) * width],
            twist_ref, high_ref, low_ref, pair_ref, spec_ref, blocks, step, rows,
        )
        for k in range(blocks + 1):
            scale = (1.0 if k in (0, blocks) else 2.0) / total
            out_ref[k, pl.ds(start, step)] = spec_ref[k * step : (k + 1) * step, :] * np.float32(scale)

    each_step(channels, step, body)


def transform_scratch(blocks, width, step, tables):
    lines = blocks + 1
    return [
        pltpu.VMEM((lines * step, 4 * width), jnp.bfloat16),
        pltpu.VMEM((lines * step, 2 * width), jnp.float32),
        pltpu.VMEM((2, lines, width), jnp.float32),
        pltpu.VMEM((tables * 2 * width, 2 * width), jnp.bfloat16),
        pltpu.SemaphoreType.DMA((2,)),
    ]


def filter_spectrum(taps, blocks, step):
    channels, length = taps.shape
    width = length // blocks
    twist, forward, _ = dft_constants(blocks, width)
    in_hbm = pl.BlockSpec(memory_space=pltpu.HBM)
    in_vmem = pl.BlockSpec(memory_space=pltpu.VMEM)
    return pl.pallas_call(
        functools.partial(filter_kernel, blocks, step, min(16, step)),
        in_specs=[in_vmem, in_hbm, in_hbm],
        out_specs=in_vmem,
        out_shape=jax.ShapeDtypeStruct((blocks + 1, channels, 2 * width), jnp.float32),
        scratch_shapes=transform_scratch(blocks, width, step, 2),
        compiler_params=pltpu.CompilerParams(vmem_limit_bytes=VMEM_BYTES),
        name="filter_spectrum",
    )(taps, twist, np.concatenate(forward))


def correlate_kernel(
    blocks, step, rows, sig_ref, filt_ref, twist_hbm, packed_hbm, out_ref, pair_ref, spec_ref, twist_ref, packed_ref, sems
):
    copies, (fh_ref, fl_ref, bh_ref, bl_ref) = table_fetch((twist_hbm, packed_hbm), (twist_ref, packed_ref), sems)
    channels, width = sig_ref.shape[1:]
    for copy in copies:
        copy.wait()

    def body(start):
        to_spectrum(
            lambda i, at: sig_ref[i, pl.ds(start + at, rows), :],
            twist_ref, fh_ref, fl_ref, pair_ref, spec_ref, blocks, step, rows,
        )
        for k in range(blocks + 1):
            for at in range(0, step, rows):
                row = k * step + at
                sig_re = spec_ref[row : row + rows, :width]
                sig_im = spec_ref[row : row + rows, width:]
                filt_re = filt_ref[k, pl.ds(start + at, rows), :width]
                filt_im = filt_ref[k, pl.ds(start + at, rows), width:]
                put_split(
                    pair_ref, row, rows,
                    filt_re * sig_re + filt_im * sig_im, filt_re * sig_im - filt_im * sig_re,
                )
        spec_ref[...] = wide_dot(pair_ref[...], bh_ref[...], bl_ref[...])
        for at in range(0, step, rows):
            re_lines, im_lines = [], []
            for k in range(blocks + 1):
                turn_cos, turn_sin = twist_ref[0, k : k + 1, :], twist_ref[1, k : k + 1, :]
                row = k * step + at
                re, im = spec_ref[row : row + rows, :width], spec_ref[row : row + rows, width:]
                re_lines.append(re * turn_cos - im * turn_sin)
                im_lines.append(re * turn_sin + im * turn_cos)
            for i, value in enumerate(real_parts(re_lines, im_lines, 2 * blocks, blocks)):
                out_ref[i, pl.ds(start + at, rows), :] = value.astype(jnp.bfloat16)

    each_step(channels, step, body)


def correlate(signal, spectrum, step):
    blocks, channels, width = signal.shape
    twist, forward, backward = dft_constants(blocks, width)
    in_hbm = pl.BlockSpec(memory_space=pltpu.HBM)
    in_vmem = pl.BlockSpec(memory_space=pltpu.VMEM)
    return pl.pallas_call(
        functools.partial(correlate_kernel, blocks, step, min(16, step)),
        in_specs=[in_vmem, in_vmem, in_hbm, in_hbm],
        out_specs=in_vmem,
        out_shape=jax.ShapeDtypeStruct((blocks, channels, width), jnp.bfloat16),
        scratch_shapes=transform_scratch(blocks, width, step, 4),
        compiler_params=pltpu.CompilerParams(vmem_limit_bytes=VMEM_BYTES),
        name="correlate",
    )(signal, spectrum, twist, np.concatenate(forward + backward))


def dft_tables(count_outer, count_inner):
    total_len = count_outer * count_inner
    index_outer = jnp.arange(count_outer, dtype=jnp.int32)
    index_inner = jnp.arange(count_inner, dtype=jnp.int32)
    angle_outer = (index_outer[:, None] * index_outer[None, :] % count_outer).astype(
        jnp.float32
    ) * (2.0 * math.pi / count_outer)
    angle_inner = (index_inner[:, None] * index_inner[None, :] % count_inner).astype(
        jnp.float32
    ) * (2.0 * math.pi / count_inner)
    angle_twist = (index_outer[:, None] * index_inner[None, :] % total_len).astype(jnp.float32) * (
        2.0 * math.pi / total_len
    )
    return (
        jnp.cos(angle_outer),
        -jnp.sin(angle_outer),
        jnp.cos(angle_inner),
        -jnp.sin(angle_inner),
        jnp.cos(angle_twist),
        -jnp.sin(angle_twist),
    )


def outer_exact(table, signal):
    table_high = table.astype(jnp.bfloat16)
    table_low = (table - table_high.astype(jnp.float32)).astype(jnp.bfloat16)
    first = jnp.einsum("ab,cbk->cak", table_high, signal, preferred_element_type=jnp.float32)
    return first + jnp.einsum("ab,cbk->cak", table_low, signal, preferred_element_type=jnp.float32)


def outer_wide(table, values):
    return jnp.einsum(
        "ab,cbk->cak",
        table,
        values,
        precision=lax.Precision.HIGH,
        preferred_element_type=jnp.float32,
    )


def inner_wide(values, table):
    return jnp.einsum(
        "cak,kl->cal",
        values,
        table,
        precision=lax.Precision.HIGH,
        preferred_element_type=jnp.float32,
    )


def spectral_forward(signal, tables):
    outer_cos, outer_sin, inner_cos, inner_sin, twist_cos, twist_sin = tables
    part_re = outer_exact(outer_cos, signal)
    part_im = outer_exact(outer_sin, signal)
    turned_re = part_re * twist_cos - part_im * twist_sin
    turned_im = part_re * twist_sin + part_im * twist_cos
    spec_re = inner_wide(turned_re, inner_cos) - inner_wide(turned_im, inner_sin)
    spec_im = inner_wide(turned_re, inner_sin) + inner_wide(turned_im, inner_cos)
    return (spec_re, spec_im)


def spectral_inverse_real(spec_re, spec_im, tables):
    outer_cos, outer_sin, inner_cos, inner_sin, twist_cos, twist_sin = tables
    back_re = inner_wide(spec_re, inner_cos) + inner_wide(spec_im, inner_sin)
    back_im = inner_wide(spec_im, inner_cos) - inner_wide(spec_re, inner_sin)
    turned_re = back_re * twist_cos + back_im * twist_sin
    turned_im = back_im * twist_cos - back_re * twist_sin
    total_len = spec_re.shape[1] * spec_re.shape[2]
    return (outer_wide(outer_cos, turned_re) + outer_wide(outer_sin, turned_im)) / total_len


def correlate_plain(gathered, filters, tables):
    channel_count, seq_len = gathered.shape
    count_outer = tables[0].shape[0]
    count_inner = tables[2].shape[0]
    padding = jnp.zeros((2 * channel_count, seq_len), jnp.bfloat16)
    stacked = jnp.concatenate([gathered, filters], axis=0)
    padded = jnp.concatenate([stacked, padding], axis=1).reshape(
        2 * channel_count, count_outer, count_inner
    )
    both_re, both_im = spectral_forward(padded, tables)
    signal_re, kernel_re = (both_re[:channel_count], both_re[channel_count:])
    signal_im, kernel_im = (both_im[:channel_count], both_im[channel_count:])
    joined_re = kernel_re * signal_re + kernel_im * signal_im
    joined_im = kernel_re * signal_im - kernel_im * signal_re
    result = spectral_inverse_real(joined_re, joined_im, tables)
    return result.reshape(channel_count, -1)[:, :seq_len].astype(jnp.bfloat16)


def per_device_gathered(
    grad_out, out_weight, gate_stream, conv_output, key_stream, value_stream, long_filter
):
    seq_count = lax.axis_size("seq")
    token_count = grad_out.shape[0]
    chan_width = out_weight.shape[1]
    group_width = chan_width // seq_count
    full_grad = lax.all_gather(grad_out, "chan", axis=1, tiled=True)
    tables = dft_tables(2 * seq_count, token_count)
    grad_mix = jnp.einsum(
        "nc,tn->ct",
        lax.all_gather(out_weight, "seq", axis=0, tiled=True),
        full_grad,
        preferred_element_type=jnp.float32,
    )
    gated_grad = (grad_mix * gate_stream.astype(jnp.float32)).astype(jnp.bfloat16)
    regrouped = lax.all_to_all(
        gated_grad.reshape(seq_count, group_width, token_count),
        "seq",
        split_axis=0,
        concat_axis=2,
        tiled=True,
    )
    inner_grad = correlate_plain(regrouped[0], long_filter, tables)
    returned = lax.all_to_all(inner_grad[None], "seq", split_axis=2, concat_axis=0, tiled=True)
    grad_inner = returned.reshape(chan_width, token_count)
    grad_gate = (grad_mix * conv_output.astype(jnp.float32)).astype(jnp.bfloat16)
    inner_grad_wide = grad_inner.astype(jnp.float32)
    grad_key = (inner_grad_wide * value_stream.astype(jnp.float32)).astype(jnp.bfloat16)
    grad_value = (inner_grad_wide * key_stream.astype(jnp.float32)).astype(jnp.bfloat16)
    return (grad_gate, grad_key, grad_value)


def share_kernel(rows, flags_ref, own_ref, local_ref, first_ref, second_ref, mine_ref, mine_far_ref, theirs_ref, theirs_far_ref):
    home, core = flags_ref[0] == 1, flags_ref[1]
    tokens = own_ref.shape[0]

    def place(near, far):
        for block in range(own_ref.shape[1] // (2 * rows)):
            lanes = pl.ds(block * rows, rows)
            mine = pl.ds(pl.multiple_of((2 * block + core) * rows, rows), rows)
            theirs = pl.ds(pl.multiple_of((2 * block + 1 - core) * rows, rows), rows)
            mine_ref[:, lanes] = near[:, mine]
            mine_far_ref[:, lanes] = far[:, mine]
            theirs_ref[:tokens, lanes] = near[:, theirs]
            theirs_ref[tokens:, lanes] = far[:, theirs]
            theirs_far_ref[:, lanes] = far[:, theirs]

    pl.when(home)(lambda: place(own_ref, first_ref))
    pl.when(jnp.logical_not(home))(lambda: place(local_ref, second_ref))


def share_blocks(flags, rows, own, local, first, second):
    tokens, features = own.shape
    part = first.shape[0]
    whole = lambda a: pl.BlockSpec(a.shape, lambda: (0, 0))
    shapes = [
        jax.ShapeDtypeStruct((t, features // 2), own.dtype) for t in (tokens, part, tokens + part, part)
    ]
    return pl.pallas_call(
        functools.partial(share_kernel, rows),
        in_specs=[pl.BlockSpec(memory_space=pltpu.SMEM)] + [whole(a) for a in (own, local, first, second)],
        out_shape=shapes,
        compiler_params=pltpu.CompilerParams(vmem_limit_bytes=VMEM_BYTES),
        name="share_blocks",
    )(flags, own, local, first, second)


def mix_kernel(rows, step, flags_ref, mine_ref, mine_far_ref, beside_ref, across_ref, slant_ref, *refs):
    own_ref, near_ref, far_edge_ref, corner_edge_ref, far_ref, corner_ref, keep_ref, send_ref, grad_ref = refs
    tokens, part = mine_ref.shape[0], mine_far_ref.shape[0]

    def place(first, second):
        for distance in range(mine_ref.shape[1] // rows):
            at = pl.ds(pl.multiple_of((flags_ref[2] ^ distance) * rows, rows), rows)
            lanes = slice(distance * rows, (distance + 1) * rows)
            grad_ref[:tokens, lanes] = mine_ref[:, at]
            grad_ref[tokens + first : tokens + first + part, lanes] = mine_far_ref[:, at]
            grad_ref[tokens + second : tokens + second + part, lanes] = beside_ref[:, at]
            grad_ref[2 * tokens : 3 * tokens, lanes] = across_ref[:tokens, at]
            grad_ref[3 * tokens + first : 3 * tokens + first + part, lanes] = across_ref[tokens:, at]
            grad_ref[3 * tokens + second : 3 * tokens + second + part, lanes] = slant_ref[:, at]

    pl.when(flags_ref[0] == 1)(lambda: place(0, part))
    pl.when(flags_ref[0] != 1)(lambda: place(part, 0))

    edge = far_edge_ref.shape[1]
    for start in range(0, own_ref.shape[1], step):
        lanes = slice(start, start + step)
        if start < edge:
            others = (far_edge_ref[:, lanes], corner_edge_ref[:, lanes])
        else:
            others = (far_ref[:, start - edge : start - edge + step], corner_ref[:, start - edge : start - edge + step])
        weight = jnp.concatenate([own_ref[:, lanes], near_ref[:, lanes], *others], axis=0)
        total = jnp.dot(grad_ref[...], weight, preferred_element_type=jnp.float32)
        keep_ref[:, lanes] = total[: 2 * tokens]
        send_ref[:, lanes] = total[2 * tokens :].astype(jnp.bfloat16)


def partial_mix(flags, grads, own, near, far_parts, corner_parts, step):
    rows, channels = own.shape
    tokens, depth = grads[0].shape
    arrays = (*grads, own, near, far_parts[0], corner_parts[0], far_parts[1], corner_parts[1])
    return pl.pallas_call(
        functools.partial(mix_kernel, rows, step),
        in_specs=[pl.BlockSpec(memory_space=pltpu.SMEM)] + [pl.BlockSpec(memory_space=pltpu.VMEM) for _ in arrays],
        out_specs=(pl.BlockSpec(memory_space=pltpu.VMEM), pl.BlockSpec(memory_space=pltpu.VMEM)),
        out_shape=(
            jax.ShapeDtypeStruct((2 * tokens, channels), jnp.float32),
            jax.ShapeDtypeStruct((2 * tokens, channels), jnp.bfloat16),
        ),
        scratch_shapes=[pltpu.VMEM((4 * tokens, depth), jnp.bfloat16)],
        compiler_params=pltpu.CompilerParams(vmem_limit_bytes=VMEM_BYTES),
        cost_estimate=pl.CostEstimate(
            flops=8 * tokens * depth * channels, bytes_accessed=2 * depth * (channels + tokens), transcendentals=0
        ),
        name="partial_mix",
    )(flags, *arrays)


def gate_kernel(step, keep_ref, near_ref, far_ref, gate_ref, conv_ref, gated_ref, out_ref):
    tokens = far_ref.shape[0]
    for start in range(0, gate_ref.shape[0], step):
        at = slice(start, start + step)
        near = near_ref[:tokens, at].astype(jnp.float32)
        far = far_ref[:, at].astype(jnp.float32)
        mix = (keep_ref[:tokens, at] + near + far).T
        gated_ref[at] = (mix * gate_ref[at].astype(jnp.float32)).astype(jnp.bfloat16)
        out_ref[at] = (mix * conv_ref[at].astype(jnp.float32)).astype(jnp.bfloat16)


def gate_mix(keep, near, far, gate, conv, step):
    channels, tokens = gate.shape
    whole = pl.BlockSpec(memory_space=pltpu.VMEM)
    shape = jax.ShapeDtypeStruct((channels, tokens), jnp.bfloat16)
    return pl.pallas_call(
        functools.partial(gate_kernel, step),
        in_specs=[whole] * 5,
        out_specs=(whole, whole),
        out_shape=(shape, shape),
        compiler_params=pltpu.CompilerParams(vmem_limit_bytes=VMEM_BYTES),
        cost_estimate=pl.CostEstimate(flops=0, bytes_accessed=16 * channels * tokens, transcendentals=0),
        name="gate_mix",
    )(keep, near, far, gate, conv)


def output_kernel(inner_ref, value_ref, key_ref, grad_key_ref, grad_value_ref):
    inner = inner_ref[...].astype(jnp.float32)
    grad_key_ref[...] = (inner * value_ref[...].astype(jnp.float32)).astype(jnp.bfloat16)
    grad_value_ref[...] = (inner * key_ref[...].astype(jnp.float32)).astype(jnp.bfloat16)


def output_products(inner, value, key):
    channels, tokens = value.shape
    steps = 2
    block = pl.BlockSpec((channels // steps, tokens), lambda g: (g, 0))
    shape = jax.ShapeDtypeStruct(value.shape, jnp.bfloat16)
    return pl.pallas_call(
        output_kernel,
        grid=(steps,),
        in_specs=[block, block, block],
        out_specs=(block, block),
        out_shape=(shape, shape),
        compiler_params=pltpu.CompilerParams(vmem_limit_bytes=VMEM_BYTES),
        name="output_products",
    )(inner, value, key)


def swap(values, axis, count, mask):
    return lax.ppermute(values, axis, [(i, i ^ mask) for i in range(count)])


def per_device(
    grad_out, out_weight, gate_stream, conv_output, key_stream, value_stream, long_filter
):
    seq_count = lax.axis_size("seq")
    token_count, shard_features = grad_out.shape
    weight_rows, chan_width = out_weight.shape
    group_width = chan_width // seq_count
    group = seq_count // 2
    place = lax.axis_index("seq")
    side = place // group
    core = place % 2
    near, far = 2, 4
    hop = lambda values, mask: swap(values, "seq", seq_count, mask)

    spectrum = filter_spectrum(long_filter, seq_count, min(32, group_width))

    shard = lax.axis_index("chan")
    home = shard == side
    flags = jnp.stack([home.astype(jnp.int32), core.astype(jnp.int32), (place % group // 2).astype(jnp.int32)])
    part = token_count // 2
    both = ("seq", "chan")
    at = lambda s, y: s * 2 + y
    away = [(s, 1 - s // group) for s in range(seq_count)]
    first = lax.ppermute(grad_out[:part], both, [(at(s, y), at(s ^ group, y)) for s, y in away])
    second = lax.ppermute(grad_out[part:], both, [(at(s, y), at(s ^ group, 1 - y)) for s, y in away])
    local = lax.ppermute(grad_out, both, [(at(s, 1 - y), at(s, y)) for s, y in away])

    lead = chan_width // 8 * 3
    edge, rest = out_weight[:, :lead], out_weight[:, lead:]
    near_all, far_rest = hop(out_weight, near), hop(rest, far)
    far_edge, corner_edge, corner_rest = hop(edge, far), hop(near_all[:, :lead], far), hop(far_rest, near)

    mine, mine_far, theirs, theirs_far = share_blocks(flags, weight_rows, grad_out, local, first, second)
    beside = swap(mine_far, "chan", 2, 1)
    across = hop(theirs, 1)
    slant = lax.ppermute(
        theirs_far, both, [(at(s, y), at(s ^ 1, 1 - y)) for s in range(seq_count) for y in range(2)]
    )
    keep, send = partial_mix(
        flags, (mine, mine_far, beside, across, slant),
        out_weight, near_all, (far_edge, far_rest), (corner_edge, corner_rest), chan_width // 8,
    )
    given = hop(send, 1)
    over = hop((keep[token_count:] + given[token_count:].astype(jnp.float32)).astype(jnp.bfloat16), group)
    gated, grad_gate = gate_mix(keep, given, over, gate_stream, conv_output, chan_width // 4)
    regrouped = lax.all_to_all(
        gated.reshape(seq_count, group_width, token_count), "seq", split_axis=0, concat_axis=0, tiled=True
    )
    inner = correlate(regrouped, spectrum, min(32, group_width))
    returned = lax.all_to_all(inner, "seq", split_axis=0, concat_axis=0, tiled=True)
    grad_key, grad_value = output_products(returned.reshape(chan_width, token_count), value_stream, key_stream)
    return (grad_gate, grad_key, grad_value)


def solution(mesh):
    in_specs = (
        P("seq", "chan"),
        P("seq", "chan"),
        P("chan", "seq"),
        P("chan", "seq"),
        P("chan", "seq"),
        P("chan", "seq"),
        P(("chan", "seq"), None),
    )
    out_specs = (P("chan", "seq"), P("chan", "seq"), P("chan", "seq"))
    square = mesh.shape["chan"] == 2 and mesh.shape["seq"] == 16
    return jax.shard_map(
        per_device if square else per_device_gathered,
        mesh=mesh, in_specs=in_specs, out_specs=out_specs, check_vma=False,
    )
```

```python
import functools
import itertools
import math

import jax
import jax.numpy as jnp
import numpy as np
from jax import lax
from jax.experimental import pallas as pl
from jax.experimental.pallas import tpu as pltpu
from jax.sharding import PartitionSpec as P

VMEM_BYTES = 16 * 1024 * 1024


def dft_constants(blocks, width):
    outer = 2 * blocks
    lines = blocks + 1
    lane = np.arange(width)
    twist = 2.0 * np.pi * (np.arange(lines)[:, None] * lane[None, :] % (outer * width)) / (outer * width)
    inner = 2.0 * np.pi * (lane[:, None] * lane[None, :] % width) / width
    cos, sin = np.cos(inner), np.sin(inner)
    forward = np.block([[cos, -sin], [sin, cos]]).astype(np.float32)
    backward = np.block([[cos, sin], [-sin, cos]]).astype(np.float32)
    twist = np.stack([np.cos(twist), np.sin(twist)]).astype(np.float32)
    return twist, forward, backward


def scaled_sum(terms):
    total = None
    for scale, value in terms:
        if abs(scale) < 1e-12:
            continue
        if abs(scale - 1.0) < 1e-12:
            term = value
        elif abs(scale + 1.0) < 1e-12:
            term = -value
        else:
            term = value * np.float32(scale)
        total = term if total is None else total + term
    return total


def real_lines(parts, period):
    count = len(parts)
    half = period // 2
    if half % 2 or count < 2:
        cosines, sines = [], []
        for k in range(half + 1):
            angle = [2.0 * math.pi * (i * k % period) / period for i in range(count)]
            cosines.append(scaled_sum([(math.cos(a), p) for a, p in zip(angle, parts)]))
            sines.append(scaled_sum([(math.sin(a), p) for a, p in zip(angle, parts)]))
        return cosines, sines
    even_cos, even_sin = real_lines(parts[0::2], half)
    quarter = half // 2
    cosines, sines = [None] * (half + 1), [None] * (half + 1)
    odd = parts[1::2]
    for k in range(quarter + 1):
        angle = [2.0 * math.pi * ((2 * m + 1) * k % period) / period for m in range(len(odd))]
        odd_cos = scaled_sum([(math.cos(a), p) for a, p in zip(angle, odd)])
        odd_sin = scaled_sum([(math.sin(a), p) for a, p in zip(angle, odd)])
        cosines[k] = add(even_cos[k], odd_cos)
        sines[k] = add(even_sin[k], odd_sin)
        if k != half - k:
            cosines[half - k] = subtract(even_cos[k], odd_cos)
            sines[half - k] = subtract(odd_sin, even_sin[k])
    return cosines, sines


def add(a, b):
    if a is None or b is None:
        return b if a is None else a
    return a + b


def subtract(a, b):
    if b is None:
        return a
    return -b if a is None else a - b


def real_parts(re, im, period, count):
    half = period // 2
    if half % 2 or count < 2:
        out = []
        for i in range(count):
            angle = [2.0 * math.pi * (i * k % period) / period for k in range(half + 1)]
            terms = [(math.cos(a), r) for a, r in zip(angle, re) if r is not None]
            terms += [(-math.sin(a), m) for a, m in zip(angle, im) if m is not None]
            out.append(scaled_sum(terms))
        return out
    quarter = half // 2
    sum_re, sum_im, gap_re, gap_im = [], [], [], []
    for k in range(quarter + 1):
        if k == half - k:
            sum_re.append(re[k]); sum_im.append(None)
            gap_re.append(None); gap_im.append(im[k])
        else:
            sum_re.append(add(re[k], re[half - k])); sum_im.append(subtract(im[k], im[half - k]))
            gap_re.append(subtract(re[k], re[half - k])); gap_im.append(add(im[k], im[half - k]))
    out = [None] * count
    out[0::2] = real_parts(sum_re, sum_im, half, (count + 1) // 2)
    for i in range(1, count, 2):
        angle = [2.0 * math.pi * (i * k % period) / period for k in range(quarter + 1)]
        terms = [(math.cos(a), r) for a, r in zip(angle, gap_re) if r is not None]
        terms += [(-math.sin(a), m) for a, m in zip(angle, gap_im) if m is not None]
        out[i] = scaled_sum(terms)
    return out


def put_split(pair_ref, row, rows, re, im):
    width = re.shape[-1]
    for at, value in ((0, re), (1, im)):
        high = value.astype(jnp.bfloat16)
        low = (value - high.astype(jnp.float32)).astype(jnp.bfloat16)
        pair_ref[row : row + rows, at * width : (at + 1) * width] = high
        pair_ref[row : row + rows, (2 + at) * width : (3 + at) * width] = low


def wide_dot(pair, high, low):
    depth = high.shape[0]
    return (
        jnp.dot(pair[:, :depth], high, preferred_element_type=jnp.float32)
        + jnp.dot(pair[:, depth:], high, preferred_element_type=jnp.float32)
        + jnp.dot(pair[:, :depth], low, preferred_element_type=jnp.float32)
    )


def to_spectrum(read, twist_ref, high_ref, low_ref, pair_ref, spec_ref, blocks, channels, rows):
    for at in range(0, channels, rows):
        parts = [read(i, at).astype(jnp.float32) for i in range(blocks)]
        cosines, sines = real_lines(parts, 2 * blocks)
        for k in range(blocks + 1):
            width = cosines[k].shape[1]
            turn_cos, turn_sin = twist_ref[k : k + 1, :width], twist_ref[k : k + 1, width:]
            re, im = cosines[k], sines[k]
            if im is None:
                new_re, new_im = re * turn_cos, -(re * turn_sin)
            else:
                new_re, new_im = re * turn_cos - im * turn_sin, -(re * turn_sin + im * turn_cos)
            put_split(pair_ref, k * channels + at, rows, new_re, new_im)
    spec_ref[...] = wide_dot(pair_ref[...], high_ref[...], low_ref[...])


def each_step(channels, step, body):
    pl.loop(0, channels // step)(lambda c: body(pl.multiple_of(c * step, step)))


def table_rows(blocks, width):
    twist, forward, backward = dft_constants(blocks, width)
    lines = np.zeros((-(-(blocks + 1) // 8) * 8, 2 * width), np.float32)
    lines[: blocks + 1, :width], lines[: blocks + 1, width:] = twist
    return np.concatenate([lines, forward, backward])


def split_into(high_ref, low_ref, table):
    high = table.astype(jnp.bfloat16)
    high_ref[...] = high
    low_ref[...] = (table - high.astype(jnp.float32)).astype(jnp.bfloat16)


def filter_kernel(blocks, step, rows, taps_ref, table_ref, out_ref, pair_ref, spec_ref, high_ref, low_ref):
    channels, length = taps_ref.shape
    width = length // blocks
    total = 2 * blocks * width
    spectra = (blocks + 1) * channels
    tail = table_ref.shape[0] - 4 * width
    out_ref[spectra:] = table_ref[...]
    twist_ref = table_ref.at[:tail]
    split_into(high_ref, low_ref, table_ref[tail : tail + 2 * width])

    def body(start):
        to_spectrum(
            lambda i, at: taps_ref[pl.ds(start + at, rows), i * width : (i + 1) * width],
            twist_ref, high_ref, low_ref, pair_ref, spec_ref, blocks, step, rows,
        )
        for k in range(blocks + 1):
            scale = (1.0 if k in (0, blocks) else 2.0) / total
            out_ref[pl.ds(k * channels + start, step)] = spec_ref[k * step : (k + 1) * step, :] * np.float32(scale)

    each_step(channels, step, body)


def transform_scratch(blocks, width, step, tables):
    lines = blocks + 1
    return [
        pltpu.VMEM((lines * step, 4 * width), jnp.bfloat16),
        pltpu.VMEM((lines * step, 2 * width), jnp.float32),
    ] + [pltpu.VMEM((2 * width, 2 * width), jnp.bfloat16) for _ in range(2 * tables)]


def filter_spectrum(taps, blocks, step):
    channels, length = taps.shape
    width = length // blocks
    table = table_rows(blocks, width)
    in_vmem = pl.BlockSpec(memory_space=pltpu.VMEM)
    return pl.pallas_call(
        functools.partial(filter_kernel, blocks, step, min(16, step)),
        in_specs=[in_vmem, in_vmem],
        out_specs=in_vmem,
        out_shape=jax.ShapeDtypeStruct(((blocks + 1) * channels + table.shape[0], 2 * width), jnp.float32),
        scratch_shapes=transform_scratch(blocks, width, step, 1),
        compiler_params=pltpu.CompilerParams(vmem_limit_bytes=VMEM_BYTES),
        name="filter_spectrum",
    )(taps, table)


def correlate_kernel(
    blocks, step, rows, sig_ref, filt_ref, out_ref, pair_ref, spec_ref, fh_ref, fl_ref, bh_ref, bl_ref
):
    channels, width = sig_ref.shape[1:]
    spectra = (blocks + 1) * channels
    tail = filt_ref.shape[0] - 4 * width
    twist_ref = filt_ref.at[spectra:tail]
    split_into(fh_ref, fl_ref, filt_ref[tail : tail + 2 * width])
    split_into(bh_ref, bl_ref, filt_ref[tail + 2 * width :])

    def body(start):
        to_spectrum(
            lambda i, at: sig_ref[i, pl.ds(start + at, rows), :],
            twist_ref, fh_ref, fl_ref, pair_ref, spec_ref, blocks, step, rows,
        )
        for k in range(blocks + 1):
            for at in range(0, step, rows):
                row = k * step + at
                sig_re = spec_ref[row : row + rows, :width]
                sig_im = spec_ref[row : row + rows, width:]
                filt_re = filt_ref[pl.ds(k * channels + start + at, rows), :width]
                filt_im = filt_ref[pl.ds(k * channels + start + at, rows), width:]
                put_split(
                    pair_ref, row, rows,
                    filt_re * sig_re + filt_im * sig_im, filt_re * sig_im - filt_im * sig_re,
                )
        spec_ref[...] = wide_dot(pair_ref[...], bh_ref[...], bl_ref[...])
        for at in range(0, step, rows):
            re_lines, im_lines = [], []
            for k in range(blocks + 1):
                turn_cos, turn_sin = twist_ref[k : k + 1, :width], twist_ref[k : k + 1, width:]
                row = k * step + at
                re, im = spec_ref[row : row + rows, :width], spec_ref[row : row + rows, width:]
                re_lines.append(re * turn_cos - im * turn_sin)
                im_lines.append(re * turn_sin + im * turn_cos)
            for i, value in enumerate(real_parts(re_lines, im_lines, 2 * blocks, blocks)):
                out_ref[i, pl.ds(start + at, rows), :] = value.astype(jnp.bfloat16)

    each_step(channels, step, body)


def correlate(signal, spectrum, step):
    blocks, channels, width = signal.shape
    in_vmem = pl.BlockSpec(memory_space=pltpu.VMEM)
    return pl.pallas_call(
        functools.partial(correlate_kernel, blocks, step, min(16, step)),
        in_specs=[in_vmem, in_vmem],
        out_specs=in_vmem,
        out_shape=jax.ShapeDtypeStruct((blocks, channels, width), jnp.bfloat16),
        scratch_shapes=transform_scratch(blocks, width, step, 2),
        compiler_params=pltpu.CompilerParams(vmem_limit_bytes=VMEM_BYTES),
        name="correlate",
    )(signal, spectrum)


def dft_tables(count_outer, count_inner):
    total_len = count_outer * count_inner
    index_outer = jnp.arange(count_outer, dtype=jnp.int32)
    index_inner = jnp.arange(count_inner, dtype=jnp.int32)
    angle_outer = (index_outer[:, None] * index_outer[None, :] % count_outer).astype(
        jnp.float32
    ) * (2.0 * math.pi / count_outer)
    angle_inner = (index_inner[:, None] * index_inner[None, :] % count_inner).astype(
        jnp.float32
    ) * (2.0 * math.pi / count_inner)
    angle_twist = (index_outer[:, None] * index_inner[None, :] % total_len).astype(jnp.float32) * (
        2.0 * math.pi / total_len
    )
    return (
        jnp.cos(angle_outer),
        -jnp.sin(angle_outer),
        jnp.cos(angle_inner),
        -jnp.sin(angle_inner),
        jnp.cos(angle_twist),
        -jnp.sin(angle_twist),
    )


def outer_exact(table, signal):
    table_high = table.astype(jnp.bfloat16)
    table_low = (table - table_high.astype(jnp.float32)).astype(jnp.bfloat16)
    first = jnp.einsum("ab,cbk->cak", table_high, signal, preferred_element_type=jnp.float32)
    return first + jnp.einsum("ab,cbk->cak", table_low, signal, preferred_element_type=jnp.float32)


def outer_wide(table, values):
    return jnp.einsum(
        "ab,cbk->cak",
        table,
        values,
        precision=lax.Precision.HIGH,
        preferred_element_type=jnp.float32,
    )


def inner_wide(values, table):
    return jnp.einsum(
        "cak,kl->cal",
        values,
        table,
        precision=lax.Precision.HIGH,
        preferred_element_type=jnp.float32,
    )


def spectral_forward(signal, tables):
    outer_cos, outer_sin, inner_cos, inner_sin, twist_cos, twist_sin = tables
    part_re = outer_exact(outer_cos, signal)
    part_im = outer_exact(outer_sin, signal)
    turned_re = part_re * twist_cos - part_im * twist_sin
    turned_im = part_re * twist_sin + part_im * twist_cos
    spec_re = inner_wide(turned_re, inner_cos) - inner_wide(turned_im, inner_sin)
    spec_im = inner_wide(turned_re, inner_sin) + inner_wide(turned_im, inner_cos)
    return (spec_re, spec_im)


def spectral_inverse_real(spec_re, spec_im, tables):
    outer_cos, outer_sin, inner_cos, inner_sin, twist_cos, twist_sin = tables
    back_re = inner_wide(spec_re, inner_cos) + inner_wide(spec_im, inner_sin)
    back_im = inner_wide(spec_im, inner_cos) - inner_wide(spec_re, inner_sin)
    turned_re = back_re * twist_cos + back_im * twist_sin
    turned_im = back_im * twist_cos - back_re * twist_sin
    total_len = spec_re.shape[1] * spec_re.shape[2]
    return (outer_wide(outer_cos, turned_re) + outer_wide(outer_sin, turned_im)) / total_len


def correlate_plain(gathered, filters, tables):
    channel_count, seq_len = gathered.shape
    count_outer = tables[0].shape[0]
    count_inner = tables[2].shape[0]
    padding = jnp.zeros((2 * channel_count, seq_len), jnp.bfloat16)
    stacked = jnp.concatenate([gathered, filters], axis=0)
    padded = jnp.concatenate([stacked, padding], axis=1).reshape(
        2 * channel_count, count_outer, count_inner
    )
    both_re, both_im = spectral_forward(padded, tables)
    signal_re, kernel_re = (both_re[:channel_count], both_re[channel_count:])
    signal_im, kernel_im = (both_im[:channel_count], both_im[channel_count:])
    joined_re = kernel_re * signal_re + kernel_im * signal_im
    joined_im = kernel_re * signal_im - kernel_im * signal_re
    result = spectral_inverse_real(joined_re, joined_im, tables)
    return result.reshape(channel_count, -1)[:, :seq_len].astype(jnp.bfloat16)


def per_device_gathered(
    grad_out, out_weight, gate_stream, conv_output, key_stream, value_stream, long_filter
):
    seq_count = lax.axis_size("seq")
    token_count = grad_out.shape[0]
    chan_width = out_weight.shape[1]
    group_width = chan_width // seq_count
    full_grad = lax.all_gather(grad_out, "chan", axis=1, tiled=True)
    tables = dft_tables(2 * seq_count, token_count)
    grad_mix = jnp.einsum(
        "nc,tn->ct",
        lax.all_gather(out_weight, "seq", axis=0, tiled=True),
        full_grad,
        preferred_element_type=jnp.float32,
    )
    gated_grad = (grad_mix * gate_stream.astype(jnp.float32)).astype(jnp.bfloat16)
    regrouped = lax.all_to_all(
        gated_grad.reshape(seq_count, group_width, token_count),
        "seq",
        split_axis=0,
        concat_axis=2,
        tiled=True,
    )
    inner_grad = correlate_plain(regrouped[0], long_filter, tables)
    returned = lax.all_to_all(inner_grad[None], "seq", split_axis=2, concat_axis=0, tiled=True)
    grad_inner = returned.reshape(chan_width, token_count)
    grad_gate = (grad_mix * conv_output.astype(jnp.float32)).astype(jnp.bfloat16)
    inner_grad_wide = grad_inner.astype(jnp.float32)
    grad_key = (inner_grad_wide * value_stream.astype(jnp.float32)).astype(jnp.bfloat16)
    grad_value = (inner_grad_wide * key_stream.astype(jnp.float32)).astype(jnp.bfloat16)
    return (grad_gate, grad_key, grad_value)


def share_kernel(rows, flags_ref, own_ref, local_ref, first_ref, second_ref, mine_ref, mine_far_ref, theirs_ref, theirs_far_ref):
    home, core = flags_ref[0] == 1, flags_ref[1]
    tokens = own_ref.shape[0]

    def place(near, far):
        for block in range(own_ref.shape[1] // (2 * rows)):
            lanes = pl.ds(block * rows, rows)
            mine = pl.ds(pl.multiple_of((2 * block + core) * rows, rows), rows)
            theirs = pl.ds(pl.multiple_of((2 * block + 1 - core) * rows, rows), rows)
            mine_ref[:, lanes] = near[:, mine]
            mine_far_ref[:, lanes] = far[:, mine]
            theirs_ref[:tokens, lanes] = near[:, theirs]
            theirs_ref[tokens:, lanes] = far[:, theirs]
            theirs_far_ref[:, lanes] = far[:, theirs]

    pl.when(home)(lambda: place(own_ref, first_ref))
    pl.when(jnp.logical_not(home))(lambda: place(local_ref, second_ref))


def share_blocks(flags, rows, own, local, first, second):
    tokens, features = own.shape
    part = first.shape[0]
    whole = lambda a: pl.BlockSpec(a.shape, lambda: (0, 0))
    shapes = [
        jax.ShapeDtypeStruct((t, features // 2), own.dtype) for t in (tokens, part, tokens + part, part)
    ]
    return pl.pallas_call(
        functools.partial(share_kernel, rows),
        in_specs=[pl.BlockSpec(memory_space=pltpu.SMEM)] + [whole(a) for a in (own, local, first, second)],
        out_shape=shapes,
        compiler_params=pltpu.CompilerParams(vmem_limit_bytes=VMEM_BYTES),
        name="share_blocks",
    )(flags, own, local, first, second)


def mix_kernel(rows, step, flags_ref, mine_ref, mine_far_ref, beside_ref, across_ref, slant_ref, *refs):
    own_ref, near_ref, far_edge_ref, corner_edge_ref, far_ref, corner_ref, keep_ref, send_ref, grad_ref = refs
    tokens, part = mine_ref.shape[0], mine_far_ref.shape[0]

    def place(first, second):
        for distance in range(mine_ref.shape[1] // rows):
            at = pl.ds(pl.multiple_of((flags_ref[2] ^ distance) * rows, rows), rows)
            lanes = slice(distance * rows, (distance + 1) * rows)
            grad_ref[:tokens, lanes] = mine_ref[:, at]
            grad_ref[tokens + first : tokens + first + part, lanes] = mine_far_ref[:, at]
            grad_ref[tokens + second : tokens + second + part, lanes] = beside_ref[:, at]
            grad_ref[2 * tokens : 3 * tokens, lanes] = across_ref[:tokens, at]
            grad_ref[3 * tokens + first : 3 * tokens + first + part, lanes] = across_ref[tokens:, at]
            grad_ref[3 * tokens + second : 3 * tokens + second + part, lanes] = slant_ref[:, at]

    pl.when(flags_ref[0] == 1)(lambda: place(0, part))
    pl.when(flags_ref[0] != 1)(lambda: place(part, 0))

    edge = far_edge_ref.shape[1]
    for start in range(0, own_ref.shape[1], step):
        lanes = slice(start, start + step)
        if start < edge:
            others = (far_edge_ref[:, lanes], corner_edge_ref[:, lanes])
        else:
            others = (far_ref[:, start - edge : start - edge + step], corner_ref[:, start - edge : start - edge + step])
        weight = jnp.concatenate([own_ref[:, lanes], near_ref[:, lanes], *others], axis=0)
        total = jnp.dot(grad_ref[...], weight, preferred_element_type=jnp.float32)
        keep_ref[:, lanes] = total[: 2 * tokens]
        send_ref[:, lanes] = total[2 * tokens :].astype(jnp.bfloat16)


def partial_mix(flags, grads, own, near, far_parts, corner_parts, step):
    rows, channels = own.shape
    tokens, depth = grads[0].shape
    arrays = (*grads, own, near, far_parts[0], corner_parts[0], far_parts[1], corner_parts[1])
    return pl.pallas_call(
        functools.partial(mix_kernel, rows, step),
        in_specs=[pl.BlockSpec(memory_space=pltpu.SMEM)] + [pl.BlockSpec(memory_space=pltpu.VMEM) for _ in arrays],
        out_specs=(pl.BlockSpec(memory_space=pltpu.VMEM), pl.BlockSpec(memory_space=pltpu.VMEM)),
        out_shape=(
            jax.ShapeDtypeStruct((2 * tokens, channels), jnp.float32),
            jax.ShapeDtypeStruct((2 * tokens, channels), jnp.bfloat16),
        ),
        scratch_shapes=[pltpu.VMEM((4 * tokens, depth), jnp.bfloat16)],
        compiler_params=pltpu.CompilerParams(vmem_limit_bytes=VMEM_BYTES),
        cost_estimate=pl.CostEstimate(
            flops=8 * tokens * depth * channels, bytes_accessed=2 * depth * (channels + tokens), transcendentals=0
        ),
        name="partial_mix",
    )(flags, *arrays)


def gate_kernel(step, keep_ref, near_ref, far_ref, gate_ref, conv_ref, gated_ref, out_ref):
    tokens = far_ref.shape[0]
    for start in range(0, gate_ref.shape[0], step):
        at = slice(start, start + step)
        near = near_ref[:tokens, at].astype(jnp.float32)
        far = far_ref[:, at].astype(jnp.float32)
        mix = (keep_ref[:tokens, at] + near + far).T
        gated_ref[at] = (mix * gate_ref[at].astype(jnp.float32)).astype(jnp.bfloat16)
        out_ref[at] = (mix * conv_ref[at].astype(jnp.float32)).astype(jnp.bfloat16)


def gate_mix(keep, near, far, gate, conv, step):
    channels, tokens = gate.shape
    whole = pl.BlockSpec(memory_space=pltpu.VMEM)
    shape = jax.ShapeDtypeStruct((channels, tokens), jnp.bfloat16)
    return pl.pallas_call(
        functools.partial(gate_kernel, step),
        in_specs=[whole] * 5,
        out_specs=(whole, whole),
        out_shape=(shape, shape),
        compiler_params=pltpu.CompilerParams(vmem_limit_bytes=VMEM_BYTES),
        cost_estimate=pl.CostEstimate(flops=0, bytes_accessed=16 * channels * tokens, transcendentals=0),
        name="gate_mix",
    )(keep, near, far, gate, conv)


def output_kernel(inner_ref, value_ref, key_ref, grad_key_ref, grad_value_ref):
    inner = inner_ref[...].astype(jnp.float32)
    grad_key_ref[...] = (inner * value_ref[...].astype(jnp.float32)).astype(jnp.bfloat16)
    grad_value_ref[...] = (inner * key_ref[...].astype(jnp.float32)).astype(jnp.bfloat16)


def output_products(inner, value, key):
    channels, tokens = value.shape
    steps = 2
    block = pl.BlockSpec((channels // steps, tokens), lambda g: (g, 0))
    shape = jax.ShapeDtypeStruct(value.shape, jnp.bfloat16)
    return pl.pallas_call(
        output_kernel,
        grid=(steps,),
        in_specs=[block, block, block],
        out_specs=(block, block),
        out_shape=(shape, shape),
        compiler_params=pltpu.CompilerParams(vmem_limit_bytes=VMEM_BYTES),
        name="output_products",
    )(inner, value, key)


def swap(values, axis, count, mask):
    return lax.ppermute(values, axis, [(i, i ^ mask) for i in range(count)])


def per_device(
    grad_out, out_weight, gate_stream, conv_output, key_stream, value_stream, long_filter
):
    seq_count = lax.axis_size("seq")
    token_count, shard_features = grad_out.shape
    weight_rows, chan_width = out_weight.shape
    group_width = chan_width // seq_count
    group = seq_count // 2
    place = lax.axis_index("seq")
    side = place // group
    core = place % 2
    near, far = 2, 4
    hop = lambda values, mask: swap(values, "seq", seq_count, mask)

    spectrum = filter_spectrum(long_filter, seq_count, min(128, group_width))

    shard = lax.axis_index("chan")
    home = shard == side
    flags = jnp.stack([home.astype(jnp.int32), core.astype(jnp.int32), (place % group // 2).astype(jnp.int32)])
    part = token_count // 2
    both = ("seq", "chan")
    at = lambda s, y: s * 2 + y
    away = [(s, 1 - s // group) for s in range(seq_count)]
    first = lax.ppermute(grad_out[:part], both, [(at(s, y), at(s ^ group, y)) for s, y in away])
    second = lax.ppermute(grad_out[part:], both, [(at(s, y), at(s ^ group, 1 - y)) for s, y in away])
    local = lax.ppermute(grad_out, both, [(at(s, 1 - y), at(s, y)) for s, y in away])

    lead = chan_width // 8 * 3
    edge, rest = out_weight[:, :lead], out_weight[:, lead:]
    near_all, far_rest = hop(out_weight, near), hop(rest, far)
    far_edge, corner_edge, corner_rest = hop(edge, far), hop(near_all[:, :lead], far), hop(far_rest, near)

    mine, mine_far, theirs, theirs_far = share_blocks(flags, weight_rows, grad_out, local, first, second)
    beside = swap(mine_far, "chan", 2, 1)
    across = hop(theirs, 1)
    slant = lax.ppermute(
        theirs_far, both, [(at(s, y), at(s ^ 1, 1 - y)) for s in range(seq_count) for y in range(2)]
    )
    keep, send = partial_mix(
        flags, (mine, mine_far, beside, across, slant),
        out_weight, near_all, (far_edge, far_rest), (corner_edge, corner_rest), chan_width // 8,
    )
    given = hop(send, 1)
    over = hop((keep[token_count:] + given[token_count:].astype(jnp.float32)).astype(jnp.bfloat16), group)
    gated, grad_gate = gate_mix(keep, given, over, gate_stream, conv_output, chan_width // 4)
    regrouped = lax.all_to_all(
        gated.reshape(seq_count, group_width, token_count), "seq", split_axis=0, concat_axis=0, tiled=True
    )
    inner = correlate(regrouped, spectrum, min(128, group_width))
    returned = lax.all_to_all(inner, "seq", split_axis=0, concat_axis=0, tiled=True)
    grad_key, grad_value = output_products(returned.reshape(chan_width, token_count), value_stream, key_stream)
    return (grad_gate, grad_key, grad_value)


def solution(mesh):
    in_specs = (
        P("seq", "chan"),
        P("seq", "chan"),
        P("chan", "seq"),
        P("chan", "seq"),
        P("chan", "seq"),
        P("chan", "seq"),
        P(("chan", "seq"), None),
    )
    out_specs = (P("chan", "seq"), P("chan", "seq"), P("chan", "seq"))
    square = mesh.shape["chan"] == 2 and mesh.shape["seq"] == 16
    return jax.shard_map(
        per_device if square else per_device_gathered,
        mesh=mesh, in_specs=in_specs, out_specs=out_specs, check_vma=False,
    )
```

```python
import functools
import itertools
import math

import jax
import jax.numpy as jnp
import numpy as np
from jax import lax
from jax.experimental import pallas as pl
from jax.experimental.pallas import tpu as pltpu
from jax.sharding import PartitionSpec as P

VMEM_BYTES = 16 * 1024 * 1024


def dft_constants(blocks, width):
    outer = 2 * blocks
    lines = blocks + 1
    lane = np.arange(width)
    twist = 2.0 * np.pi * (np.arange(lines)[:, None] * lane[None, :] % (outer * width)) / (outer * width)
    inner = 2.0 * np.pi * (lane[:, None] * lane[None, :] % width) / width
    cos, sin = np.cos(inner), np.sin(inner)
    forward = np.block([[cos, -sin], [sin, cos]]).astype(np.float32)
    backward = np.block([[cos, sin], [-sin, cos]]).astype(np.float32)
    twist = np.stack([np.cos(twist), np.sin(twist)]).astype(np.float32)
    return twist, forward, backward


def scaled_sum(terms):
    total = None
    for scale, value in terms:
        if abs(scale) < 1e-12:
            continue
        if abs(scale - 1.0) < 1e-12:
            term = value
        elif abs(scale + 1.0) < 1e-12:
            term = -value
        else:
            term = value * np.float32(scale)
        total = term if total is None else total + term
    return total


def real_lines(parts, period):
    count = len(parts)
    half = period // 2
    if half % 2 or count < 2:
        cosines, sines = [], []
        for k in range(half + 1):
            angle = [2.0 * math.pi * (i * k % period) / period for i in range(count)]
            cosines.append(scaled_sum([(math.cos(a), p) for a, p in zip(angle, parts)]))
            sines.append(scaled_sum([(math.sin(a), p) for a, p in zip(angle, parts)]))
        return cosines, sines
    even_cos, even_sin = real_lines(parts[0::2], half)
    quarter = half // 2
    cosines, sines = [None] * (half + 1), [None] * (half + 1)
    odd = parts[1::2]
    for k in range(quarter + 1):
        angle = [2.0 * math.pi * ((2 * m + 1) * k % period) / period for m in range(len(odd))]
        odd_cos = scaled_sum([(math.cos(a), p) for a, p in zip(angle, odd)])
        odd_sin = scaled_sum([(math.sin(a), p) for a, p in zip(angle, odd)])
        cosines[k] = add(even_cos[k], odd_cos)
        sines[k] = add(even_sin[k], odd_sin)
        if k != half - k:
            cosines[half - k] = subtract(even_cos[k], odd_cos)
            sines[half - k] = subtract(odd_sin, even_sin[k])
    return cosines, sines


def add(a, b):
    if a is None or b is None:
        return b if a is None else a
    return a + b


def subtract(a, b):
    if b is None:
        return a
    return -b if a is None else a - b


def real_parts(re, im, period, count):
    half = period // 2
    if half % 2 or count < 2:
        out = []
        for i in range(count):
            angle = [2.0 * math.pi * (i * k % period) / period for k in range(half + 1)]
            terms = [(math.cos(a), r) for a, r in zip(angle, re) if r is not None]
            terms += [(-math.sin(a), m) for a, m in zip(angle, im) if m is not None]
            out.append(scaled_sum(terms))
        return out
    quarter = half // 2
    sum_re, sum_im, gap_re, gap_im = [], [], [], []
    for k in range(quarter + 1):
        if k == half - k:
            sum_re.append(re[k]); sum_im.append(None)
            gap_re.append(None); gap_im.append(im[k])
        else:
            sum_re.append(add(re[k], re[half - k])); sum_im.append(subtract(im[k], im[half - k]))
            gap_re.append(subtract(re[k], re[half - k])); gap_im.append(add(im[k], im[half - k]))
    out = [None] * count
    out[0::2] = real_parts(sum_re, sum_im, half, (count + 1) // 2)
    for i in range(1, count, 2):
        angle = [2.0 * math.pi * (i * k % period) / period for k in range(quarter + 1)]
        terms = [(math.cos(a), r) for a, r in zip(angle, gap_re) if r is not None]
        terms += [(-math.sin(a), m) for a, m in zip(angle, gap_im) if m is not None]
        out[i] = scaled_sum(terms)
    return out


def put_split(pair_ref, row, rows, re, im):
    width = re.shape[-1]
    for at, value in ((0, re), (1, im)):
        high = value.astype(jnp.bfloat16)
        low = (value - high.astype(jnp.float32)).astype(jnp.bfloat16)
        pair_ref[row : row + rows, at * width : (at + 1) * width] = high
        pair_ref[row : row + rows, (2 + at) * width : (3 + at) * width] = low


def wide_dot(pair, high, low):
    depth = high.shape[0]
    return (
        jnp.dot(pair[:, :depth], high, preferred_element_type=jnp.float32)
        + jnp.dot(pair[:, depth:], high, preferred_element_type=jnp.float32)
        + jnp.dot(pair[:, :depth], low, preferred_element_type=jnp.float32)
    )


def to_spectrum(read, twist_ref, high_ref, low_ref, pair_ref, spec_ref, blocks, channels, rows):
    for at in range(0, channels, rows):
        parts = [read(i, at).astype(jnp.float32) for i in range(blocks)]
        cosines, sines = real_lines(parts, 2 * blocks)
        for k in range(blocks + 1):
            width = cosines[k].shape[1]
            turn_cos, turn_sin = twist_ref[k : k + 1, :width], twist_ref[k : k + 1, width:]
            re, im = cosines[k], sines[k]
            if im is None:
                new_re, new_im = re * turn_cos, -(re * turn_sin)
            else:
                new_re, new_im = re * turn_cos - im * turn_sin, -(re * turn_sin + im * turn_cos)
            put_split(pair_ref, k * channels + at, rows, new_re, new_im)
    spec_ref[...] = wide_dot(pair_ref[...], high_ref[...], low_ref[...])


def each_step(channels, step, body):
    pl.loop(0, channels // step)(lambda c: body(pl.multiple_of(c * step, step)))


def table_rows(blocks, width):
    twist, forward, backward = dft_constants(blocks, width)
    lines = np.zeros((-(-(blocks + 1) // 8) * 8, 2 * width), np.float32)
    lines[: blocks + 1, :width], lines[: blocks + 1, width:] = twist
    return np.concatenate([lines, forward, backward])


def split_into(high_ref, low_ref, table):
    high = table.astype(jnp.bfloat16)
    high_ref[...] = high
    low_ref[...] = (table - high.astype(jnp.float32)).astype(jnp.bfloat16)


def filter_kernel(blocks, step, rows, taps_ref, table_ref, out_ref, pair_ref, spec_ref, high_ref, low_ref):
    channels, length = taps_ref.shape
    width = length // blocks
    total = 2 * blocks * width
    spectra = (blocks + 1) * channels
    tail = table_ref.shape[0] - 4 * width
    out_ref[spectra:] = table_ref[...]
    twist_ref = table_ref.at[:tail]
    split_into(high_ref, low_ref, table_ref[tail : tail + 2 * width])

    def body(start):
        to_spectrum(
            lambda i, at: taps_ref[pl.ds(start + at, rows), i * width : (i + 1) * width],
            twist_ref, high_ref, low_ref, pair_ref, spec_ref, blocks, step, rows,
        )
        for k in range(blocks + 1):
            scale = (1.0 if k in (0, blocks) else 2.0) / total
            out_ref[pl.ds(k * channels + start, step)] = spec_ref[k * step : (k + 1) * step, :] * np.float32(scale)

    each_step(channels, step, body)


def transform_scratch(blocks, width, step, tables):
    lines = blocks + 1
    return [
        pltpu.VMEM((lines * step, 4 * width), jnp.bfloat16),
        pltpu.VMEM((lines * step, 2 * width), jnp.float32),
    ] + [pltpu.VMEM((2 * width, 2 * width), jnp.bfloat16) for _ in range(2 * tables)]


def filter_spectrum(taps, blocks, step):
    channels, length = taps.shape
    width = length // blocks
    table = table_rows(blocks, width)
    in_vmem = pl.BlockSpec(memory_space=pltpu.VMEM)
    return pl.pallas_call(
        functools.partial(filter_kernel, blocks, step, min(16, step)),
        in_specs=[in_vmem, in_vmem],
        out_specs=in_vmem,
        out_shape=jax.ShapeDtypeStruct(((blocks + 1) * channels + table.shape[0], 2 * width), jnp.float32),
        scratch_shapes=transform_scratch(blocks, width, step, 1),
        compiler_params=pltpu.CompilerParams(vmem_limit_bytes=VMEM_BYTES),
        name="filter_spectrum",
    )(taps, table)


def correlate_kernel(
    blocks, step, rows, sig_ref, filt_ref, out_ref, pair_ref, spec_ref, fh_ref, fl_ref, bh_ref, bl_ref
):
    channels, width = sig_ref.shape[1:]
    spectra = (blocks + 1) * channels
    tail = filt_ref.shape[0] - 4 * width
    twist_ref = filt_ref.at[spectra:tail]
    split_into(fh_ref, fl_ref, filt_ref[tail : tail + 2 * width])
    split_into(bh_ref, bl_ref, filt_ref[tail + 2 * width :])

    def body(start):
        to_spectrum(
            lambda i, at: sig_ref[i, pl.ds(start + at, rows), :],
            twist_ref, fh_ref, fl_ref, pair_ref, spec_ref, blocks, step, rows,
        )
        for k in range(blocks + 1):
            for at in range(0, step, rows):
                row = k * step + at
                sig_re = spec_ref[row : row + rows, :width]
                sig_im = spec_ref[row : row + rows, width:]
                filt_re = filt_ref[pl.ds(k * channels + start + at, rows), :width]
                filt_im = filt_ref[pl.ds(k * channels + start + at, rows), width:]
                put_split(
                    pair_ref, row, rows,
                    filt_re * sig_re + filt_im * sig_im, filt_re * sig_im - filt_im * sig_re,
                )
        spec_ref[...] = wide_dot(pair_ref[...], bh_ref[...], bl_ref[...])
        for at in range(0, step, rows):
            re_lines, im_lines = [], []
            for k in range(blocks + 1):
                turn_cos, turn_sin = twist_ref[k : k + 1, :width], twist_ref[k : k + 1, width:]
                row = k * step + at
                re, im = spec_ref[row : row + rows, :width], spec_ref[row : row + rows, width:]
                re_lines.append(re * turn_cos - im * turn_sin)
                im_lines.append(re * turn_sin + im * turn_cos)
            for i, value in enumerate(real_parts(re_lines, im_lines, 2 * blocks, blocks)):
                out_ref[i, pl.ds(start + at, rows), :] = value.astype(jnp.bfloat16)

    each_step(channels, step, body)


def correlate(signal, spectrum, step):
    blocks, channels, width = signal.shape
    in_vmem = pl.BlockSpec(memory_space=pltpu.VMEM)
    return pl.pallas_call(
        functools.partial(correlate_kernel, blocks, step, min(16, step)),
        in_specs=[in_vmem, in_vmem],
        out_specs=in_vmem,
        out_shape=jax.ShapeDtypeStruct((blocks, channels, width), jnp.bfloat16),
        scratch_shapes=transform_scratch(blocks, width, step, 2),
        compiler_params=pltpu.CompilerParams(vmem_limit_bytes=VMEM_BYTES),
        name="correlate",
    )(signal, spectrum)


def dft_tables(count_outer, count_inner):
    total_len = count_outer * count_inner
    index_outer = jnp.arange(count_outer, dtype=jnp.int32)
    index_inner = jnp.arange(count_inner, dtype=jnp.int32)
    angle_outer = (index_outer[:, None] * index_outer[None, :] % count_outer).astype(
        jnp.float32
    ) * (2.0 * math.pi / count_outer)
    angle_inner = (index_inner[:, None] * index_inner[None, :] % count_inner).astype(
        jnp.float32
    ) * (2.0 * math.pi / count_inner)
    angle_twist = (index_outer[:, None] * index_inner[None, :] % total_len).astype(jnp.float32) * (
        2.0 * math.pi / total_len
    )
    return (
        jnp.cos(angle_outer),
        -jnp.sin(angle_outer),
        jnp.cos(angle_inner),
        -jnp.sin(angle_inner),
        jnp.cos(angle_twist),
        -jnp.sin(angle_twist),
    )


def outer_exact(table, signal):
    table_high = table.astype(jnp.bfloat16)
    table_low = (table - table_high.astype(jnp.float32)).astype(jnp.bfloat16)
    first = jnp.einsum("ab,cbk->cak", table_high, signal, preferred_element_type=jnp.float32)
    return first + jnp.einsum("ab,cbk->cak", table_low, signal, preferred_element_type=jnp.float32)


def outer_wide(table, values):
    return jnp.einsum(
        "ab,cbk->cak",
        table,
        values,
        precision=lax.Precision.HIGH,
        preferred_element_type=jnp.float32,
    )


def inner_wide(values, table):
    return jnp.einsum(
        "cak,kl->cal",
        values,
        table,
        precision=lax.Precision.HIGH,
        preferred_element_type=jnp.float32,
    )


def spectral_forward(signal, tables):
    outer_cos, outer_sin, inner_cos, inner_sin, twist_cos, twist_sin = tables
    part_re = outer_exact(outer_cos, signal)
    part_im = outer_exact(outer_sin, signal)
    turned_re = part_re * twist_cos - part_im * twist_sin
    turned_im = part_re * twist_sin + part_im * twist_cos
    spec_re = inner_wide(turned_re, inner_cos) - inner_wide(turned_im, inner_sin)
    spec_im = inner_wide(turned_re, inner_sin) + inner_wide(turned_im, inner_cos)
    return (spec_re, spec_im)


def spectral_inverse_real(spec_re, spec_im, tables):
    outer_cos, outer_sin, inner_cos, inner_sin, twist_cos, twist_sin = tables
    back_re = inner_wide(spec_re, inner_cos) + inner_wide(spec_im, inner_sin)
    back_im = inner_wide(spec_im, inner_cos) - inner_wide(spec_re, inner_sin)
    turned_re = back_re * twist_cos + back_im * twist_sin
    turned_im = back_im * twist_cos - back_re * twist_sin
    total_len = spec_re.shape[1] * spec_re.shape[2]
    return (outer_wide(outer_cos, turned_re) + outer_wide(outer_sin, turned_im)) / total_len


def correlate_plain(gathered, filters, tables):
    channel_count, seq_len = gathered.shape
    count_outer = tables[0].shape[0]
    count_inner = tables[2].shape[0]
    padding = jnp.zeros((2 * channel_count, seq_len), jnp.bfloat16)
    stacked = jnp.concatenate([gathered, filters], axis=0)
    padded = jnp.concatenate([stacked, padding], axis=1).reshape(
        2 * channel_count, count_outer, count_inner
    )
    both_re, both_im = spectral_forward(padded, tables)
    signal_re, kernel_re = (both_re[:channel_count], both_re[channel_count:])
    signal_im, kernel_im = (both_im[:channel_count], both_im[channel_count:])
    joined_re = kernel_re * signal_re + kernel_im * signal_im
    joined_im = kernel_re * signal_im - kernel_im * signal_re
    result = spectral_inverse_real(joined_re, joined_im, tables)
    return result.reshape(channel_count, -1)[:, :seq_len].astype(jnp.bfloat16)


def per_device_gathered(
    grad_out, out_weight, gate_stream, conv_output, key_stream, value_stream, long_filter
):
    seq_count = lax.axis_size("seq")
    token_count = grad_out.shape[0]
    chan_width = out_weight.shape[1]
    group_width = chan_width // seq_count
    full_grad = lax.all_gather(grad_out, "chan", axis=1, tiled=True)
    tables = dft_tables(2 * seq_count, token_count)
    grad_mix = jnp.einsum(
        "nc,tn->ct",
        lax.all_gather(out_weight, "seq", axis=0, tiled=True),
        full_grad,
        preferred_element_type=jnp.float32,
    )
    gated_grad = (grad_mix * gate_stream.astype(jnp.float32)).astype(jnp.bfloat16)
    regrouped = lax.all_to_all(
        gated_grad.reshape(seq_count, group_width, token_count),
        "seq",
        split_axis=0,
        concat_axis=2,
        tiled=True,
    )
    inner_grad = correlate_plain(regrouped[0], long_filter, tables)
    returned = lax.all_to_all(inner_grad[None], "seq", split_axis=2, concat_axis=0, tiled=True)
    grad_inner = returned.reshape(chan_width, token_count)
    grad_gate = (grad_mix * conv_output.astype(jnp.float32)).astype(jnp.bfloat16)
    inner_grad_wide = grad_inner.astype(jnp.float32)
    grad_key = (inner_grad_wide * value_stream.astype(jnp.float32)).astype(jnp.bfloat16)
    grad_value = (inner_grad_wide * key_stream.astype(jnp.float32)).astype(jnp.bfloat16)
    return (grad_gate, grad_key, grad_value)


def share_kernel(rows, flags_ref, own_ref, local_ref, first_ref, second_ref, mine_ref, mine_far_ref, theirs_ref, theirs_far_ref):
    home, core = flags_ref[0] == 1, flags_ref[1]
    tokens = own_ref.shape[0]

    def place(near, far):
        for block in range(own_ref.shape[1] // (2 * rows)):
            lanes = pl.ds(block * rows, rows)
            mine = pl.ds(pl.multiple_of((2 * block + core) * rows, rows), rows)
            theirs = pl.ds(pl.multiple_of((2 * block + 1 - core) * rows, rows), rows)
            mine_ref[:, lanes] = near[:, mine]
            mine_far_ref[:, lanes] = far[:, mine]
            theirs_ref[:tokens, lanes] = near[:, theirs]
            theirs_ref[tokens:, lanes] = far[:, theirs]
            theirs_far_ref[:, lanes] = far[:, theirs]

    pl.when(home)(lambda: place(own_ref, first_ref))
    pl.when(jnp.logical_not(home))(lambda: place(local_ref, second_ref))


def share_blocks(flags, rows, own, local, first, second):
    tokens, features = own.shape
    part = first.shape[0]
    whole = lambda a: pl.BlockSpec(a.shape, lambda: (0, 0))
    shapes = [
        jax.ShapeDtypeStruct((t, features // 2), own.dtype) for t in (tokens, part, tokens + part, part)
    ]
    return pl.pallas_call(
        functools.partial(share_kernel, rows),
        in_specs=[pl.BlockSpec(memory_space=pltpu.SMEM)] + [whole(a) for a in (own, local, first, second)],
        out_shape=shapes,
        compiler_params=pltpu.CompilerParams(vmem_limit_bytes=VMEM_BYTES),
        name="share_blocks",
    )(flags, own, local, first, second)


def mix_kernel(rows, step, flags_ref, mine_ref, mine_far_ref, beside_ref, across_ref, slant_ref, *refs):
    own_ref, near_ref, far_edge_ref, corner_edge_ref, far_ref, corner_ref, keep_ref, send_ref, grad_ref = refs
    tokens, part = mine_ref.shape[0], mine_far_ref.shape[0]

    def place(first, second):
        for distance in range(mine_ref.shape[1] // rows):
            at = pl.ds(pl.multiple_of((flags_ref[2] ^ distance) * rows, rows), rows)
            lanes = slice(distance * rows, (distance + 1) * rows)
            grad_ref[:tokens, lanes] = mine_ref[:, at]
            grad_ref[tokens + first : tokens + first + part, lanes] = mine_far_ref[:, at]
            grad_ref[tokens + second : tokens + second + part, lanes] = beside_ref[:, at]
            grad_ref[2 * tokens : 3 * tokens, lanes] = across_ref[:tokens, at]
            grad_ref[3 * tokens + first : 3 * tokens + first + part, lanes] = across_ref[tokens:, at]
            grad_ref[3 * tokens + second : 3 * tokens + second + part, lanes] = slant_ref[:, at]

    pl.when(flags_ref[0] == 1)(lambda: place(0, part))
    pl.when(flags_ref[0] != 1)(lambda: place(part, 0))

    edge = far_edge_ref.shape[1]
    for start in range(0, own_ref.shape[1], step):
        lanes = slice(start, start + step)
        if start < edge:
            others = (far_edge_ref[:, lanes], corner_edge_ref[:, lanes])
        else:
            others = (far_ref[:, start - edge : start - edge + step], corner_ref[:, start - edge : start - edge + step])
        weight = jnp.concatenate([own_ref[:, lanes], near_ref[:, lanes], *others], axis=0)
        total = jnp.dot(grad_ref[...], weight, preferred_element_type=jnp.float32)
        keep_ref[:, lanes] = total[: 2 * tokens]
        send_ref[:, lanes] = total[2 * tokens :].astype(jnp.bfloat16)


def partial_mix(flags, grads, own, near, far_parts, corner_parts, step):
    rows, channels = own.shape
    tokens, depth = grads[0].shape
    arrays = (*grads, own, near, far_parts[0], corner_parts[0], far_parts[1], corner_parts[1])
    return pl.pallas_call(
        functools.partial(mix_kernel, rows, step),
        in_specs=[pl.BlockSpec(memory_space=pltpu.SMEM)] + [pl.BlockSpec(memory_space=pltpu.VMEM) for _ in arrays],
        out_specs=(pl.BlockSpec(memory_space=pltpu.VMEM), pl.BlockSpec(memory_space=pltpu.VMEM)),
        out_shape=(
            jax.ShapeDtypeStruct((2 * tokens, channels), jnp.float32),
            jax.ShapeDtypeStruct((2 * tokens, channels), jnp.bfloat16),
        ),
        scratch_shapes=[pltpu.VMEM((4 * tokens, depth), jnp.bfloat16)],
        compiler_params=pltpu.CompilerParams(vmem_limit_bytes=VMEM_BYTES),
        cost_estimate=pl.CostEstimate(
            flops=8 * tokens * depth * channels, bytes_accessed=2 * depth * (channels + tokens), transcendentals=0
        ),
        name="partial_mix",
    )(flags, *arrays)


def gate_kernel(step, keep_ref, near_ref, far_ref, gate_ref, conv_ref, gated_ref, out_ref):
    tokens = far_ref.shape[0]
    for start in range(0, gate_ref.shape[0], step):
        at = slice(start, start + step)
        near = near_ref[:tokens, at].astype(jnp.float32)
        far = far_ref[:, at].astype(jnp.float32)
        mix = (keep_ref[:tokens, at] + near + far).T
        gated_ref[at] = (mix * gate_ref[at].astype(jnp.float32)).astype(jnp.bfloat16)
        out_ref[at] = (mix * conv_ref[at].astype(jnp.float32)).astype(jnp.bfloat16)


def gate_mix(keep, near, far, gate, conv, step):
    channels, tokens = gate.shape
    whole = pl.BlockSpec(memory_space=pltpu.VMEM)
    shape = jax.ShapeDtypeStruct((channels, tokens), jnp.bfloat16)
    return pl.pallas_call(
        functools.partial(gate_kernel, step),
        in_specs=[whole] * 5,
        out_specs=(whole, whole),
        out_shape=(shape, shape),
        compiler_params=pltpu.CompilerParams(vmem_limit_bytes=VMEM_BYTES),
        cost_estimate=pl.CostEstimate(flops=0, bytes_accessed=16 * channels * tokens, transcendentals=0),
        name="gate_mix",
    )(keep, near, far, gate, conv)


def output_kernel(inner_ref, value_ref, key_ref, grad_key_ref, grad_value_ref):
    inner = inner_ref[...].astype(jnp.float32)
    grad_key_ref[...] = (inner * value_ref[...].astype(jnp.float32)).astype(jnp.bfloat16)
    grad_value_ref[...] = (inner * key_ref[...].astype(jnp.float32)).astype(jnp.bfloat16)


def output_products(inner, value, key):
    channels, tokens = value.shape
    steps = 2
    block = pl.BlockSpec((channels // steps, tokens), lambda g: (g, 0))
    shape = jax.ShapeDtypeStruct(value.shape, jnp.bfloat16)
    return pl.pallas_call(
        output_kernel,
        grid=(steps,),
        in_specs=[block, block, block],
        out_specs=(block, block),
        out_shape=(shape, shape),
        compiler_params=pltpu.CompilerParams(vmem_limit_bytes=VMEM_BYTES),
        name="output_products",
    )(inner, value, key)


def swap(values, axis, count, mask):
    return lax.ppermute(values, axis, [(i, i ^ mask) for i in range(count)])


def per_device(
    grad_out, out_weight, gate_stream, conv_output, key_stream, value_stream, long_filter
):
    seq_count = lax.axis_size("seq")
    token_count, shard_features = grad_out.shape
    weight_rows, chan_width = out_weight.shape
    group_width = chan_width // seq_count
    group = seq_count // 2
    place = lax.axis_index("seq")
    side = place // group
    core = place % 2
    near, far = 2, 4
    hop = lambda values, mask: swap(values, "seq", seq_count, mask)

    spectrum = filter_spectrum(long_filter, seq_count, min(128, group_width))

    shard = lax.axis_index("chan")
    home = shard == side
    flags = jnp.stack([home.astype(jnp.int32), core.astype(jnp.int32), (place % group // 2).astype(jnp.int32)])
    part = token_count // 2
    both = ("seq", "chan")
    at = lambda s, y: s * 2 + y
    away = [(s, 1 - s // group) for s in range(seq_count)]
    first = lax.ppermute(grad_out[:part], both, [(at(s, y), at(s ^ group, y)) for s, y in away])
    local = swap(grad_out, "chan", 2, 1)
    second = lax.ppermute(local[part:], both, [(at(s, 1 - y), at(s ^ group, 1 - y)) for s, y in away])

    lead = chan_width // 8 * 3
    edge, rest = out_weight[:, :lead], out_weight[:, lead:]
    near_all, far_rest = hop(out_weight, near), hop(rest, far)
    far_edge, corner_edge, corner_rest = hop(edge, far), hop(near_all[:, :lead], far), hop(far_rest, near)

    mine, mine_far, theirs, theirs_far = share_blocks(flags, weight_rows, grad_out, local, first, second)
    beside = swap(mine_far, "chan", 2, 1)
    across = hop(theirs, 1)
    slant = lax.ppermute(
        theirs_far, both, [(at(s, y), at(s ^ 1, 1 - y)) for s in range(seq_count) for y in range(2)]
    )
    keep, send = partial_mix(
        flags, (mine, mine_far, beside, across, slant),
        out_weight, near_all, (far_edge, far_rest), (corner_edge, corner_rest), chan_width // 8,
    )
    given = hop(send, 1)
    over = hop((keep[token_count:] + given[token_count:].astype(jnp.float32)).astype(jnp.bfloat16), group)
    gated, grad_gate = gate_mix(keep, given, over, gate_stream, conv_output, chan_width // 4)
    regrouped = lax.all_to_all(
        gated.reshape(seq_count, group_width, token_count), "seq", split_axis=0, concat_axis=0, tiled=True
    )
    inner = correlate(regrouped, spectrum, min(128, group_width))
    returned = lax.all_to_all(inner, "seq", split_axis=0, concat_axis=0, tiled=True)
    grad_key, grad_value = output_products(returned.reshape(chan_width, token_count), value_stream, key_stream)
    return (grad_gate, grad_key, grad_value)


def solution(mesh):
    in_specs = (
        P("seq", "chan"),
        P("seq", "chan"),
        P("chan", "seq"),
        P("chan", "seq"),
        P("chan", "seq"),
        P("chan", "seq"),
        P(("chan", "seq"), None),
    )
    out_specs = (P("chan", "seq"), P("chan", "seq"), P("chan", "seq"))
    square = mesh.shape["chan"] == 2 and mesh.shape["seq"] == 16
    return jax.shard_map(
        per_device if square else per_device_gathered,
        mesh=mesh, in_specs=in_specs, out_specs=out_specs, check_vma=False,
    )
```

```python
import functools
import itertools
import math

import jax
import jax.numpy as jnp
import numpy as np
from jax import lax
from jax.experimental import pallas as pl
from jax.experimental.pallas import tpu as pltpu
from jax.sharding import PartitionSpec as P

VMEM_BYTES = 16 * 1024 * 1024


def dft_constants(blocks, width):
    outer = 2 * blocks
    lines = blocks + 1
    lane = np.arange(width)
    twist = 2.0 * np.pi * (np.arange(lines)[:, None] * lane[None, :] % (outer * width)) / (outer * width)
    inner = 2.0 * np.pi * (lane[:, None] * lane[None, :] % width) / width
    cos, sin = np.cos(inner), np.sin(inner)
    forward = np.block([[cos, -sin], [sin, cos]]).astype(np.float32)
    backward = np.block([[cos, sin], [-sin, cos]]).astype(np.float32)
    twist = np.stack([np.cos(twist), np.sin(twist)]).astype(np.float32)
    return twist, forward, backward


def scaled_sum(terms):
    total = None
    for scale, value in terms:
        if abs(scale) < 1e-12:
            continue
        if abs(scale - 1.0) < 1e-12:
            term = value
        elif abs(scale + 1.0) < 1e-12:
            term = -value
        else:
            term = value * np.float32(scale)
        total = term if total is None else total + term
    return total


def real_lines(parts, period):
    count = len(parts)
    half = period // 2
    if half % 2 or count < 2:
        cosines, sines = [], []
        for k in range(half + 1):
            angle = [2.0 * math.pi * (i * k % period) / period for i in range(count)]
            cosines.append(scaled_sum([(math.cos(a), p) for a, p in zip(angle, parts)]))
            sines.append(scaled_sum([(math.sin(a), p) for a, p in zip(angle, parts)]))
        return cosines, sines
    even_cos, even_sin = real_lines(parts[0::2], half)
    quarter = half // 2
    cosines, sines = [None] * (half + 1), [None] * (half + 1)
    odd = parts[1::2]
    for k in range(quarter + 1):
        angle = [2.0 * math.pi * ((2 * m + 1) * k % period) / period for m in range(len(odd))]
        odd_cos = scaled_sum([(math.cos(a), p) for a, p in zip(angle, odd)])
        odd_sin = scaled_sum([(math.sin(a), p) for a, p in zip(angle, odd)])
        cosines[k] = add(even_cos[k], odd_cos)
        sines[k] = add(even_sin[k], odd_sin)
        if k != half - k:
            cosines[half - k] = subtract(even_cos[k], odd_cos)
            sines[half - k] = subtract(odd_sin, even_sin[k])
    return cosines, sines


def add(a, b):
    if a is None or b is None:
        return b if a is None else a
    return a + b


def subtract(a, b):
    if b is None:
        return a
    return -b if a is None else a - b


def real_parts(re, im, period, count):
    half = period // 2
    if half % 2 or count < 2:
        out = []
        for i in range(count):
            angle = [2.0 * math.pi * (i * k % period) / period for k in range(half + 1)]
            terms = [(math.cos(a), r) for a, r in zip(angle, re) if r is not None]
            terms += [(-math.sin(a), m) for a, m in zip(angle, im) if m is not None]
            out.append(scaled_sum(terms))
        return out
    quarter = half // 2
    sum_re, sum_im, gap_re, gap_im = [], [], [], []
    for k in range(quarter + 1):
        if k == half - k:
            sum_re.append(re[k]); sum_im.append(None)
            gap_re.append(None); gap_im.append(im[k])
        else:
            sum_re.append(add(re[k], re[half - k])); sum_im.append(subtract(im[k], im[half - k]))
            gap_re.append(subtract(re[k], re[half - k])); gap_im.append(add(im[k], im[half - k]))
    out = [None] * count
    out[0::2] = real_parts(sum_re, sum_im, half, (count + 1) // 2)
    for i in range(1, count, 2):
        angle = [2.0 * math.pi * (i * k % period) / period for k in range(quarter + 1)]
        terms = [(math.cos(a), r) for a, r in zip(angle, gap_re) if r is not None]
        terms += [(-math.sin(a), m) for a, m in zip(angle, gap_im) if m is not None]
        out[i] = scaled_sum(terms)
    return out


def put_split(pair_ref, row, rows, re, im):
    width = re.shape[-1]
    for at, value in ((0, re), (1, im)):
        high = value.astype(jnp.bfloat16)
        low = (value - high.astype(jnp.float32)).astype(jnp.bfloat16)
        pair_ref[row : row + rows, at * width : (at + 1) * width] = high
        pair_ref[row : row + rows, (2 + at) * width : (3 + at) * width] = low


def wide_dot(pair, high, low):
    depth = high.shape[0]
    return (
        jnp.dot(pair[:, :depth], high, preferred_element_type=jnp.float32)
        + jnp.dot(pair[:, depth:], high, preferred_element_type=jnp.float32)
        + jnp.dot(pair[:, :depth], low, preferred_element_type=jnp.float32)
    )


def to_spectrum(read, twist_ref, high_ref, low_ref, pair_ref, spec_ref, blocks, channels, rows):
    for at in range(0, channels, rows):
        parts = [read(i, at).astype(jnp.float32) for i in range(blocks)]
        cosines, sines = real_lines(parts, 2 * blocks)
        for k in range(blocks + 1):
            width = cosines[k].shape[1]
            turn_cos, turn_sin = twist_ref[k : k + 1, :width], twist_ref[k : k + 1, width:]
            re, im = cosines[k], sines[k]
            if im is None:
                new_re, new_im = re * turn_cos, -(re * turn_sin)
            else:
                new_re, new_im = re * turn_cos - im * turn_sin, -(re * turn_sin + im * turn_cos)
            put_split(pair_ref, k * channels + at, rows, new_re, new_im)
    spec_ref[...] = wide_dot(pair_ref[...], high_ref[...], low_ref[...])


def each_step(channels, step, body):
    pl.loop(0, channels // step)(lambda c: body(pl.multiple_of(c * step, step)))


def table_rows(blocks, width):
    twist, forward, backward = dft_constants(blocks, width)
    lines = np.zeros((-(-(blocks + 1) // 8) * 8, 2 * width), np.float32)
    lines[: blocks + 1, :width], lines[: blocks + 1, width:] = twist
    return np.concatenate([lines, forward, backward])


def split_into(high_ref, low_ref, table):
    high = table.astype(jnp.bfloat16)
    high_ref[...] = high
    low_ref[...] = (table - high.astype(jnp.float32)).astype(jnp.bfloat16)


def filter_kernel(blocks, step, rows, taps_ref, table_ref, out_ref, pair_ref, spec_ref, high_ref, low_ref):
    channels, length = taps_ref.shape
    width = length // blocks
    total = 2 * blocks * width
    spectra = (blocks + 1) * channels
    tail = table_ref.shape[0] - 4 * width
    out_ref[spectra:] = table_ref[...]
    twist_ref = table_ref.at[:tail]
    split_into(high_ref, low_ref, table_ref[tail : tail + 2 * width])

    def body(start):
        to_spectrum(
            lambda i, at: taps_ref[pl.ds(start + at, rows), i * width : (i + 1) * width],
            twist_ref, high_ref, low_ref, pair_ref, spec_ref, blocks, step, rows,
        )
        for k in range(blocks + 1):
            scale = (1.0 if k in (0, blocks) else 2.0) / total
            out_ref[pl.ds(k * channels + start, step)] = spec_ref[k * step : (k + 1) * step, :] * np.float32(scale)

    each_step(channels, step, body)


def transform_scratch(blocks, width, step, tables):
    lines = blocks + 1
    return [
        pltpu.VMEM((lines * step, 4 * width), jnp.bfloat16),
        pltpu.VMEM((lines * step, 2 * width), jnp.float32),
    ] + [pltpu.VMEM((2 * width, 2 * width), jnp.bfloat16) for _ in range(2 * tables)]


def filter_spectrum(taps, blocks, step):
    channels, length = taps.shape
    width = length // blocks
    table = table_rows(blocks, width)
    in_vmem = pl.BlockSpec(memory_space=pltpu.VMEM)
    return pl.pallas_call(
        functools.partial(filter_kernel, blocks, step, min(16, step)),
        in_specs=[in_vmem, in_vmem],
        out_specs=in_vmem,
        out_shape=jax.ShapeDtypeStruct(((blocks + 1) * channels + table.shape[0], 2 * width), jnp.float32),
        scratch_shapes=transform_scratch(blocks, width, step, 1),
        compiler_params=pltpu.CompilerParams(vmem_limit_bytes=VMEM_BYTES),
        name="filter_spectrum",
    )(taps, table)


def correlate_kernel(
    blocks, step, rows, sig_ref, filt_ref, out_ref, pair_ref, spec_ref, fh_ref, fl_ref, bh_ref, bl_ref
):
    channels, width = sig_ref.shape[1:]
    spectra = (blocks + 1) * channels
    tail = filt_ref.shape[0] - 4 * width
    twist_ref = filt_ref.at[spectra:tail]
    split_into(fh_ref, fl_ref, filt_ref[tail : tail + 2 * width])
    split_into(bh_ref, bl_ref, filt_ref[tail + 2 * width :])

    def body(start):
        to_spectrum(
            lambda i, at: sig_ref[i, pl.ds(start + at, rows), :],
            twist_ref, fh_ref, fl_ref, pair_ref, spec_ref, blocks, step, rows,
        )
        for k in range(blocks + 1):
            for at in range(0, step, rows):
                row = k * step + at
                sig_re = spec_ref[row : row + rows, :width]
                sig_im = spec_ref[row : row + rows, width:]
                filt_re = filt_ref[pl.ds(k * channels + start + at, rows), :width]
                filt_im = filt_ref[pl.ds(k * channels + start + at, rows), width:]
                put_split(
                    pair_ref, row, rows,
                    filt_re * sig_re + filt_im * sig_im, filt_re * sig_im - filt_im * sig_re,
                )
        spec_ref[...] = wide_dot(pair_ref[...], bh_ref[...], bl_ref[...])
        for at in range(0, step, rows):
            re_lines, im_lines = [], []
            for k in range(blocks + 1):
                turn_cos, turn_sin = twist_ref[k : k + 1, :width], twist_ref[k : k + 1, width:]
                row = k * step + at
                re, im = spec_ref[row : row + rows, :width], spec_ref[row : row + rows, width:]
                re_lines.append(re * turn_cos - im * turn_sin)
                im_lines.append(re * turn_sin + im * turn_cos)
            for i, value in enumerate(real_parts(re_lines, im_lines, 2 * blocks, blocks)):
                out_ref[i, pl.ds(start + at, rows), :] = value.astype(jnp.bfloat16)

    each_step(channels, step, body)


def correlate(signal, spectrum, step):
    blocks, channels, width = signal.shape
    in_vmem = pl.BlockSpec(memory_space=pltpu.VMEM)
    return pl.pallas_call(
        functools.partial(correlate_kernel, blocks, step, min(16, step)),
        in_specs=[in_vmem, in_vmem],
        out_specs=in_vmem,
        out_shape=jax.ShapeDtypeStruct((blocks, channels, width), jnp.bfloat16),
        scratch_shapes=transform_scratch(blocks, width, step, 2),
        compiler_params=pltpu.CompilerParams(vmem_limit_bytes=VMEM_BYTES),
        name="correlate",
    )(signal, spectrum)


def dft_tables(count_outer, count_inner):
    total_len = count_outer * count_inner
    index_outer = jnp.arange(count_outer, dtype=jnp.int32)
    index_inner = jnp.arange(count_inner, dtype=jnp.int32)
    angle_outer = (index_outer[:, None] * index_outer[None, :] % count_outer).astype(
        jnp.float32
    ) * (2.0 * math.pi / count_outer)
    angle_inner = (index_inner[:, None] * index_inner[None, :] % count_inner).astype(
        jnp.float32
    ) * (2.0 * math.pi / count_inner)
    angle_twist = (index_outer[:, None] * index_inner[None, :] % total_len).astype(jnp.float32) * (
        2.0 * math.pi / total_len
    )
    return (
        jnp.cos(angle_outer),
        -jnp.sin(angle_outer),
        jnp.cos(angle_inner),
        -jnp.sin(angle_inner),
        jnp.cos(angle_twist),
        -jnp.sin(angle_twist),
    )


def outer_exact(table, signal):
    table_high = table.astype(jnp.bfloat16)
    table_low = (table - table_high.astype(jnp.float32)).astype(jnp.bfloat16)
    first = jnp.einsum("ab,cbk->cak", table_high, signal, preferred_element_type=jnp.float32)
    return first + jnp.einsum("ab,cbk->cak", table_low, signal, preferred_element_type=jnp.float32)


def outer_wide(table, values):
    return jnp.einsum(
        "ab,cbk->cak",
        table,
        values,
        precision=lax.Precision.HIGH,
        preferred_element_type=jnp.float32,
    )


def inner_wide(values, table):
    return jnp.einsum(
        "cak,kl->cal",
        values,
        table,
        precision=lax.Precision.HIGH,
        preferred_element_type=jnp.float32,
    )


def spectral_forward(signal, tables):
    outer_cos, outer_sin, inner_cos, inner_sin, twist_cos, twist_sin = tables
    part_re = outer_exact(outer_cos, signal)
    part_im = outer_exact(outer_sin, signal)
    turned_re = part_re * twist_cos - part_im * twist_sin
    turned_im = part_re * twist_sin + part_im * twist_cos
    spec_re = inner_wide(turned_re, inner_cos) - inner_wide(turned_im, inner_sin)
    spec_im = inner_wide(turned_re, inner_sin) + inner_wide(turned_im, inner_cos)
    return (spec_re, spec_im)


def spectral_inverse_real(spec_re, spec_im, tables):
    outer_cos, outer_sin, inner_cos, inner_sin, twist_cos, twist_sin = tables
    back_re = inner_wide(spec_re, inner_cos) + inner_wide(spec_im, inner_sin)
    back_im = inner_wide(spec_im, inner_cos) - inner_wide(spec_re, inner_sin)
    turned_re = back_re * twist_cos + back_im * twist_sin
    turned_im = back_im * twist_cos - back_re * twist_sin
    total_len = spec_re.shape[1] * spec_re.shape[2]
    return (outer_wide(outer_cos, turned_re) + outer_wide(outer_sin, turned_im)) / total_len


def correlate_plain(gathered, filters, tables):
    channel_count, seq_len = gathered.shape
    count_outer = tables[0].shape[0]
    count_inner = tables[2].shape[0]
    padding = jnp.zeros((2 * channel_count, seq_len), jnp.bfloat16)
    stacked = jnp.concatenate([gathered, filters], axis=0)
    padded = jnp.concatenate([stacked, padding], axis=1).reshape(
        2 * channel_count, count_outer, count_inner
    )
    both_re, both_im = spectral_forward(padded, tables)
    signal_re, kernel_re = (both_re[:channel_count], both_re[channel_count:])
    signal_im, kernel_im = (both_im[:channel_count], both_im[channel_count:])
    joined_re = kernel_re * signal_re + kernel_im * signal_im
    joined_im = kernel_re * signal_im - kernel_im * signal_re
    result = spectral_inverse_real(joined_re, joined_im, tables)
    return result.reshape(channel_count, -1)[:, :seq_len].astype(jnp.bfloat16)


def per_device_gathered(
    grad_out, out_weight, gate_stream, conv_output, key_stream, value_stream, long_filter
):
    seq_count = lax.axis_size("seq")
    token_count = grad_out.shape[0]
    chan_width = out_weight.shape[1]
    group_width = chan_width // seq_count
    full_grad = lax.all_gather(grad_out, "chan", axis=1, tiled=True)
    tables = dft_tables(2 * seq_count, token_count)
    grad_mix = jnp.einsum(
        "nc,tn->ct",
        lax.all_gather(out_weight, "seq", axis=0, tiled=True),
        full_grad,
        preferred_element_type=jnp.float32,
    )
    gated_grad = (grad_mix * gate_stream.astype(jnp.float32)).astype(jnp.bfloat16)
    regrouped = lax.all_to_all(
        gated_grad.reshape(seq_count, group_width, token_count),
        "seq",
        split_axis=0,
        concat_axis=2,
        tiled=True,
    )
    inner_grad = correlate_plain(regrouped[0], long_filter, tables)
    returned = lax.all_to_all(inner_grad[None], "seq", split_axis=2, concat_axis=0, tiled=True)
    grad_inner = returned.reshape(chan_width, token_count)
    grad_gate = (grad_mix * conv_output.astype(jnp.float32)).astype(jnp.bfloat16)
    inner_grad_wide = grad_inner.astype(jnp.float32)
    grad_key = (inner_grad_wide * value_stream.astype(jnp.float32)).astype(jnp.bfloat16)
    grad_value = (inner_grad_wide * key_stream.astype(jnp.float32)).astype(jnp.bfloat16)
    return (grad_gate, grad_key, grad_value)


def share_kernel(rows, flags_ref, own_ref, local_ref, first_ref, second_ref, mine_ref, mine_far_ref, theirs_ref, theirs_far_ref):
    home, core = flags_ref[0] == 1, flags_ref[1]
    tokens = own_ref.shape[0]

    def place(near, far):
        for block in range(own_ref.shape[1] // (2 * rows)):
            lanes = pl.ds(block * rows, rows)
            mine = pl.ds(pl.multiple_of((2 * block + core) * rows, rows), rows)
            theirs = pl.ds(pl.multiple_of((2 * block + 1 - core) * rows, rows), rows)
            mine_ref[:, lanes] = near[:, mine]
            mine_far_ref[:, lanes] = far[:, mine]
            theirs_ref[:tokens, lanes] = near[:, theirs]
            theirs_ref[tokens:, lanes] = far[:, theirs]
            theirs_far_ref[:, lanes] = far[:, theirs]

    pl.when(home)(lambda: place(own_ref, first_ref))
    pl.when(jnp.logical_not(home))(lambda: place(local_ref, second_ref))


def share_blocks(flags, rows, own, local, first, second):
    tokens, features = own.shape
    part = first.shape[0]
    whole = lambda a: pl.BlockSpec(a.shape, lambda: (0, 0))
    shapes = [
        jax.ShapeDtypeStruct((t, features // 2), own.dtype) for t in (tokens, part, tokens + part, part)
    ]
    return pl.pallas_call(
        functools.partial(share_kernel, rows),
        in_specs=[pl.BlockSpec(memory_space=pltpu.SMEM)] + [whole(a) for a in (own, local, first, second)],
        out_shape=shapes,
        compiler_params=pltpu.CompilerParams(vmem_limit_bytes=VMEM_BYTES),
        name="share_blocks",
    )(flags, own, local, first, second)


def mix_kernel(rows, step, flags_ref, mine_ref, mine_far_ref, beside_ref, across_ref, slant_ref, *refs):
    own_ref, near_ref, far_edge_ref, corner_edge_ref, far_ref, corner_ref, keep_ref, send_ref, grad_ref = refs
    tokens, part = mine_ref.shape[0], mine_far_ref.shape[0]

    def place(first, second):
        for distance in range(mine_ref.shape[1] // rows):
            at = pl.ds(pl.multiple_of((flags_ref[2] ^ distance) * rows, rows), rows)
            lanes = slice(distance * rows, (distance + 1) * rows)
            grad_ref[:tokens, lanes] = mine_ref[:, at]
            grad_ref[tokens + first : tokens + first + part, lanes] = mine_far_ref[:, at]
            grad_ref[tokens + second : tokens + second + part, lanes] = beside_ref[:, at]
            grad_ref[2 * tokens : 3 * tokens, lanes] = across_ref[:tokens, at]
            grad_ref[3 * tokens + first : 3 * tokens + first + part, lanes] = across_ref[tokens:, at]
            grad_ref[3 * tokens + second : 3 * tokens + second + part, lanes] = slant_ref[:, at]

    pl.when(flags_ref[0] == 1)(lambda: place(0, part))
    pl.when(flags_ref[0] != 1)(lambda: place(part, 0))

    edge = far_edge_ref.shape[1]
    for start in range(0, own_ref.shape[1], step):
        lanes = slice(start, start + step)
        if start < edge:
            others = (far_edge_ref[:, lanes], corner_edge_ref[:, lanes])
        else:
            others = (far_ref[:, start - edge : start - edge + step], corner_ref[:, start - edge : start - edge + step])
        weight = jnp.concatenate([own_ref[:, lanes], near_ref[:, lanes], *others], axis=0)
        total = jnp.dot(grad_ref[...], weight, preferred_element_type=jnp.float32)
        keep_ref[:, lanes] = total[: 2 * tokens]
        send_ref[:, lanes] = total[2 * tokens :].astype(jnp.bfloat16)


def partial_mix(flags, grads, own, near, far_parts, corner_parts, step):
    rows, channels = own.shape
    tokens, depth = grads[0].shape
    arrays = (*grads, own, near, far_parts[0], corner_parts[0], far_parts[1], corner_parts[1])
    return pl.pallas_call(
        functools.partial(mix_kernel, rows, step),
        in_specs=[pl.BlockSpec(memory_space=pltpu.SMEM)] + [pl.BlockSpec(memory_space=pltpu.VMEM) for _ in arrays],
        out_specs=(pl.BlockSpec(memory_space=pltpu.VMEM), pl.BlockSpec(memory_space=pltpu.VMEM)),
        out_shape=(
            jax.ShapeDtypeStruct((2 * tokens, channels), jnp.float32),
            jax.ShapeDtypeStruct((2 * tokens, channels), jnp.bfloat16),
        ),
        scratch_shapes=[pltpu.VMEM((4 * tokens, depth), jnp.bfloat16)],
        compiler_params=pltpu.CompilerParams(vmem_limit_bytes=VMEM_BYTES),
        cost_estimate=pl.CostEstimate(
            flops=8 * tokens * depth * channels, bytes_accessed=2 * depth * (channels + tokens), transcendentals=0
        ),
        name="partial_mix",
    )(flags, *arrays)


def gate_kernel(step, keep_ref, near_ref, far_ref, gate_ref, conv_ref, gated_ref, out_ref):
    tokens = far_ref.shape[0]
    for start in range(0, gate_ref.shape[0], step):
        at = slice(start, start + step)
        near = near_ref[:tokens, at].astype(jnp.float32)
        far = far_ref[:, at].astype(jnp.float32)
        mix = (keep_ref[:tokens, at] + near + far).T
        gated_ref[at] = (mix * gate_ref[at].astype(jnp.float32)).astype(jnp.bfloat16)
        out_ref[at] = (mix * conv_ref[at].astype(jnp.float32)).astype(jnp.bfloat16)


def gate_mix(keep, near, far, gate, conv, step):
    channels, tokens = gate.shape
    whole = pl.BlockSpec(memory_space=pltpu.VMEM)
    shape = jax.ShapeDtypeStruct((channels, tokens), jnp.bfloat16)
    return pl.pallas_call(
        functools.partial(gate_kernel, step),
        in_specs=[whole] * 5,
        out_specs=(whole, whole),
        out_shape=(shape, shape),
        compiler_params=pltpu.CompilerParams(vmem_limit_bytes=VMEM_BYTES),
        cost_estimate=pl.CostEstimate(flops=0, bytes_accessed=16 * channels * tokens, transcendentals=0),
        name="gate_mix",
    )(keep, near, far, gate, conv)


def output_kernel(inner_ref, value_ref, key_ref, grad_key_ref, grad_value_ref):
    inner = inner_ref[...].astype(jnp.float32)
    grad_key_ref[...] = (inner * value_ref[...].astype(jnp.float32)).astype(jnp.bfloat16)
    grad_value_ref[...] = (inner * key_ref[...].astype(jnp.float32)).astype(jnp.bfloat16)


def output_products(inner, value, key):
    channels, tokens = value.shape
    steps = 2
    block = pl.BlockSpec((channels // steps, tokens), lambda g: (g, 0))
    shape = jax.ShapeDtypeStruct(value.shape, jnp.bfloat16)
    return pl.pallas_call(
        output_kernel,
        grid=(steps,),
        in_specs=[block, block, block],
        out_specs=(block, block),
        out_shape=(shape, shape),
        compiler_params=pltpu.CompilerParams(vmem_limit_bytes=VMEM_BYTES),
        name="output_products",
    )(inner, value, key)


def swap(values, axis, count, mask):
    return lax.ppermute(values, axis, [(i, i ^ mask) for i in range(count)])


def per_device(
    grad_out, out_weight, gate_stream, conv_output, key_stream, value_stream, long_filter
):
    seq_count = lax.axis_size("seq")
    token_count, shard_features = grad_out.shape
    weight_rows, chan_width = out_weight.shape
    group_width = chan_width // seq_count
    group = seq_count // 2
    place = lax.axis_index("seq")
    side = place // group
    core = place % 2
    near, far = 2, 4
    hop = lambda values, mask: swap(values, "seq", seq_count, mask)

    spectrum = filter_spectrum(long_filter, seq_count, min(128, group_width))

    shard = lax.axis_index("chan")
    home = shard == side
    flags = jnp.stack([home.astype(jnp.int32), core.astype(jnp.int32), (place % group // 2).astype(jnp.int32)])
    part = token_count // 2
    both = ("seq", "chan")
    at = lambda s, y: s * 2 + y
    away = [(s, 1 - s // group) for s in range(seq_count)]
    first = lax.ppermute(grad_out[:part], both, [(at(s, y), at(s ^ group, y)) for s, y in away])
    local = swap(grad_out, "chan", 2, 1)
    second = lax.ppermute(local[part:], both, [(at(s, 1 - y), at(s ^ group, 1 - y)) for s, y in away])

    lead = chan_width // 8 * 3
    edge, rest = out_weight[:, :lead], out_weight[:, lead:]
    near_all, far_rest = hop(out_weight, near), hop(rest, far)
    near_edge = near_all[:, :lead]
    first, second, local, near_edge = lax.optimization_barrier((first, second, local, near_edge))
    far_edge, corner_edge, corner_rest = hop(edge, far), hop(near_edge, far), hop(far_rest, near)

    mine, mine_far, theirs, theirs_far = share_blocks(flags, weight_rows, grad_out, local, first, second)
    beside = swap(mine_far, "chan", 2, 1)
    across = hop(theirs, 1)
    slant = lax.ppermute(
        theirs_far, both, [(at(s, y), at(s ^ 1, 1 - y)) for s in range(seq_count) for y in range(2)]
    )
    keep, send = partial_mix(
        flags, (mine, mine_far, beside, across, slant),
        out_weight, near_all, (far_edge, far_rest), (corner_edge, corner_rest), chan_width // 8,
    )
    given = hop(send, 1)
    over = hop((keep[token_count:] + given[token_count:].astype(jnp.float32)).astype(jnp.bfloat16), group)
    gated, grad_gate = gate_mix(keep, given, over, gate_stream, conv_output, chan_width // 4)
    regrouped = lax.all_to_all(
        gated.reshape(seq_count, group_width, token_count), "seq", split_axis=0, concat_axis=0, tiled=True
    )
    inner = correlate(regrouped, spectrum, min(128, group_width))
    returned = lax.all_to_all(inner, "seq", split_axis=0, concat_axis=0, tiled=True)
    grad_key, grad_value = output_products(returned.reshape(chan_width, token_count), value_stream, key_stream)
    return (grad_gate, grad_key, grad_value)


def solution(mesh):
    in_specs = (
        P("seq", "chan"),
        P("seq", "chan"),
        P("chan", "seq"),
        P("chan", "seq"),
        P("chan", "seq"),
        P("chan", "seq"),
        P(("chan", "seq"), None),
    )
    out_specs = (P("chan", "seq"), P("chan", "seq"), P("chan", "seq"))
    square = mesh.shape["chan"] == 2 and mesh.shape["seq"] == 16
    return jax.shard_map(
        per_device if square else per_device_gathered,
        mesh=mesh, in_specs=in_specs, out_specs=out_specs, check_vma=False,
    )
```

```python
import functools
import itertools
import math

import jax
import jax.numpy as jnp
import numpy as np
from jax import lax
from jax.experimental import pallas as pl
from jax.experimental.pallas import tpu as pltpu
from jax.sharding import PartitionSpec as P

VMEM_BYTES = 16 * 1024 * 1024


def dft_constants(blocks, width):
    outer = 2 * blocks
    lines = blocks + 1
    lane = np.arange(width)
    twist = 2.0 * np.pi * (np.arange(lines)[:, None] * lane[None, :] % (outer * width)) / (outer * width)
    inner = 2.0 * np.pi * (lane[:, None] * lane[None, :] % width) / width
    cos, sin = np.cos(inner), np.sin(inner)
    forward = np.block([[cos, -sin], [sin, cos]]).astype(np.float32)
    backward = np.block([[cos, sin], [-sin, cos]]).astype(np.float32)
    twist = np.stack([np.cos(twist), np.sin(twist)]).astype(np.float32)
    return twist, forward, backward


def scaled_sum(terms):
    total = None
    for scale, value in terms:
        if abs(scale) < 1e-12:
            continue
        if abs(scale - 1.0) < 1e-12:
            term = value
        elif abs(scale + 1.0) < 1e-12:
            term = -value
        else:
            term = value * np.float32(scale)
        total = term if total is None else total + term
    return total


def real_lines(parts, period):
    count = len(parts)
    half = period // 2
    if half % 2 or count < 2:
        cosines, sines = [], []
        for k in range(half + 1):
            angle = [2.0 * math.pi * (i * k % period) / period for i in range(count)]
            cosines.append(scaled_sum([(math.cos(a), p) for a, p in zip(angle, parts)]))
            sines.append(scaled_sum([(math.sin(a), p) for a, p in zip(angle, parts)]))
        return cosines, sines
    even_cos, even_sin = real_lines(parts[0::2], half)
    quarter = half // 2
    cosines, sines = [None] * (half + 1), [None] * (half + 1)
    odd = parts[1::2]
    for k in range(quarter + 1):
        angle = [2.0 * math.pi * ((2 * m + 1) * k % period) / period for m in range(len(odd))]
        odd_cos = scaled_sum([(math.cos(a), p) for a, p in zip(angle, odd)])
        odd_sin = scaled_sum([(math.sin(a), p) for a, p in zip(angle, odd)])
        cosines[k] = add(even_cos[k], odd_cos)
        sines[k] = add(even_sin[k], odd_sin)
        if k != half - k:
            cosines[half - k] = subtract(even_cos[k], odd_cos)
            sines[half - k] = subtract(odd_sin, even_sin[k])
    return cosines, sines


def add(a, b):
    if a is None or b is None:
        return b if a is None else a
    return a + b


def subtract(a, b):
    if b is None:
        return a
    return -b if a is None else a - b


def real_parts(re, im, period, count):
    half = period // 2
    if half % 2 or count < 2:
        out = []
        for i in range(count):
            angle = [2.0 * math.pi * (i * k % period) / period for k in range(half + 1)]
            terms = [(math.cos(a), r) for a, r in zip(angle, re) if r is not None]
            terms += [(-math.sin(a), m) for a, m in zip(angle, im) if m is not None]
            out.append(scaled_sum(terms))
        return out
    quarter = half // 2
    sum_re, sum_im, gap_re, gap_im = [], [], [], []
    for k in range(quarter + 1):
        if k == half - k:
            sum_re.append(re[k]); sum_im.append(None)
            gap_re.append(None); gap_im.append(im[k])
        else:
            sum_re.append(add(re[k], re[half - k])); sum_im.append(subtract(im[k], im[half - k]))
            gap_re.append(subtract(re[k], re[half - k])); gap_im.append(add(im[k], im[half - k]))
    out = [None] * count
    out[0::2] = real_parts(sum_re, sum_im, half, (count + 1) // 2)
    for i in range(1, count, 2):
        angle = [2.0 * math.pi * (i * k % period) / period for k in range(quarter + 1)]
        terms = [(math.cos(a), r) for a, r in zip(angle, gap_re) if r is not None]
        terms += [(-math.sin(a), m) for a, m in zip(angle, gap_im) if m is not None]
        out[i] = scaled_sum(terms)
    return out


def put_split(pair_ref, row, rows, re, im):
    width = re.shape[-1]
    for at, value in ((0, re), (1, im)):
        high = value.astype(jnp.bfloat16)
        low = (value - high.astype(jnp.float32)).astype(jnp.bfloat16)
        pair_ref[row : row + rows, at * width : (at + 1) * width] = high
        pair_ref[row : row + rows, (2 + at) * width : (3 + at) * width] = low


def wide_dot(pair, high, low):
    depth = high.shape[0]
    return jnp.dot(
        jnp.concatenate([pair, pair[:, :depth]], axis=1),
        jnp.concatenate([high, high, low], axis=0),
        preferred_element_type=jnp.float32,
    )


def to_spectrum(read, twist_ref, high_ref, low_ref, pair_ref, spec_ref, blocks, channels, rows):
    for at in range(0, channels, rows):
        parts = [read(i, at).astype(jnp.float32) for i in range(blocks)]
        cosines, sines = real_lines(parts, 2 * blocks)
        for k in range(blocks + 1):
            width = cosines[k].shape[1]
            turn_cos, turn_sin = twist_ref[k : k + 1, :width], twist_ref[k : k + 1, width:]
            re, im = cosines[k], sines[k]
            if im is None:
                new_re, new_im = re * turn_cos, -(re * turn_sin)
            else:
                new_re, new_im = re * turn_cos - im * turn_sin, -(re * turn_sin + im * turn_cos)
            put_split(pair_ref, k * channels + at, rows, new_re, new_im)
    spec_ref[...] = wide_dot(pair_ref[...], high_ref[...], low_ref[...])


def each_step(channels, step, body):
    pl.loop(0, channels // step)(lambda c: body(pl.multiple_of(c * step, step)))


def table_rows(blocks, width):
    twist, forward, backward = dft_constants(blocks, width)
    lines = np.zeros((-(-(blocks + 1) // 8) * 8, 2 * width), np.float32)
    lines[: blocks + 1, :width], lines[: blocks + 1, width:] = twist
    return np.concatenate([lines, forward, backward])


def split_into(high_ref, low_ref, table):
    high = table.astype(jnp.bfloat16)
    high_ref[...] = high
    low_ref[...] = (table - high.astype(jnp.float32)).astype(jnp.bfloat16)


def filter_kernel(blocks, step, rows, taps_ref, table_ref, out_ref, pair_ref, spec_ref, high_ref, low_ref):
    channels, length = taps_ref.shape
    width = length // blocks
    total = 2 * blocks * width
    spectra = (blocks + 1) * channels
    tail = table_ref.shape[0] - 4 * width
    out_ref[spectra:] = table_ref[...]
    twist_ref = table_ref.at[:tail]
    split_into(high_ref, low_ref, table_ref[tail : tail + 2 * width])

    def body(start):
        to_spectrum(
            lambda i, at: taps_ref[pl.ds(start + at, rows), i * width : (i + 1) * width],
            twist_ref, high_ref, low_ref, pair_ref, spec_ref, blocks, step, rows,
        )
        for k in range(blocks + 1):
            scale = (1.0 if k in (0, blocks) else 2.0) / total
            out_ref[pl.ds(k * channels + start, step)] = spec_ref[k * step : (k + 1) * step, :] * np.float32(scale)

    each_step(channels, step, body)


def transform_scratch(blocks, width, step, tables):
    lines = blocks + 1
    return [
        pltpu.VMEM((lines * step, 4 * width), jnp.bfloat16),
        pltpu.VMEM((lines * step, 2 * width), jnp.float32),
    ] + [pltpu.VMEM((2 * width, 2 * width), jnp.bfloat16) for _ in range(2 * tables)]


def filter_spectrum(taps, blocks, step):
    channels, length = taps.shape
    width = length // blocks
    table = table_rows(blocks, width)
    in_vmem = pl.BlockSpec(memory_space=pltpu.VMEM)
    return pl.pallas_call(
        functools.partial(filter_kernel, blocks, step, min(16, step)),
        in_specs=[in_vmem, in_vmem],
        out_specs=in_vmem,
        out_shape=jax.ShapeDtypeStruct(((blocks + 1) * channels + table.shape[0], 2 * width), jnp.float32),
        scratch_shapes=transform_scratch(blocks, width, step, 1),
        compiler_params=pltpu.CompilerParams(vmem_limit_bytes=VMEM_BYTES),
        name="filter_spectrum",
    )(taps, table)


def correlate_kernel(
    blocks, step, rows, sig_ref, filt_ref, out_ref, pair_ref, spec_ref, fh_ref, fl_ref, bh_ref, bl_ref
):
    channels, width = sig_ref.shape[1:]
    spectra = (blocks + 1) * channels
    tail = filt_ref.shape[0] - 4 * width
    twist_ref = filt_ref.at[spectra:tail]
    split_into(fh_ref, fl_ref, filt_ref[tail : tail + 2 * width])
    split_into(bh_ref, bl_ref, filt_ref[tail + 2 * width :])

    def body(start):
        to_spectrum(
            lambda i, at: sig_ref[i, pl.ds(start + at, rows), :],
            twist_ref, fh_ref, fl_ref, pair_ref, spec_ref, blocks, step, rows,
        )
        for k in range(blocks + 1):
            for at in range(0, step, rows):
                row = k * step + at
                sig_re = spec_ref[row : row + rows, :width]
                sig_im = spec_ref[row : row + rows, width:]
                filt_re = filt_ref[pl.ds(k * channels + start + at, rows), :width]
                filt_im = filt_ref[pl.ds(k * channels + start + at, rows), width:]
                put_split(
                    pair_ref, row, rows,
                    filt_re * sig_re + filt_im * sig_im, filt_re * sig_im - filt_im * sig_re,
                )
        spec_ref[...] = wide_dot(pair_ref[...], bh_ref[...], bl_ref[...])
        for at in range(0, step, rows):
            re_lines, im_lines = [], []
            for k in range(blocks + 1):
                turn_cos, turn_sin = twist_ref[k : k + 1, :width], twist_ref[k : k + 1, width:]
                row = k * step + at
                re, im = spec_ref[row : row + rows, :width], spec_ref[row : row + rows, width:]
                re_lines.append(re * turn_cos - im * turn_sin)
                im_lines.append(re * turn_sin + im * turn_cos)
            for i, value in enumerate(real_parts(re_lines, im_lines, 2 * blocks, blocks)):
                out_ref[i, pl.ds(start + at, rows), :] = value.astype(jnp.bfloat16)

    each_step(channels, step, body)


def correlate(signal, spectrum, step):
    blocks, channels, width = signal.shape
    in_vmem = pl.BlockSpec(memory_space=pltpu.VMEM)
    return pl.pallas_call(
        functools.partial(correlate_kernel, blocks, step, min(16, step)),
        in_specs=[in_vmem, in_vmem],
        out_specs=in_vmem,
        out_shape=jax.ShapeDtypeStruct((blocks, channels, width), jnp.bfloat16),
        scratch_shapes=transform_scratch(blocks, width, step, 2),
        compiler_params=pltpu.CompilerParams(vmem_limit_bytes=VMEM_BYTES),
        name="correlate",
    )(signal, spectrum)


def dft_tables(count_outer, count_inner):
    total_len = count_outer * count_inner
    index_outer = jnp.arange(count_outer, dtype=jnp.int32)
    index_inner = jnp.arange(count_inner, dtype=jnp.int32)
    angle_outer = (index_outer[:, None] * index_outer[None, :] % count_outer).astype(
        jnp.float32
    ) * (2.0 * math.pi / count_outer)
    angle_inner = (index_inner[:, None] * index_inner[None, :] % count_inner).astype(
        jnp.float32
    ) * (2.0 * math.pi / count_inner)
    angle_twist = (index_outer[:, None] * index_inner[None, :] % total_len).astype(jnp.float32) * (
        2.0 * math.pi / total_len
    )
    return (
        jnp.cos(angle_outer),
        -jnp.sin(angle_outer),
        jnp.cos(angle_inner),
        -jnp.sin(angle_inner),
        jnp.cos(angle_twist),
        -jnp.sin(angle_twist),
    )


def outer_exact(table, signal):
    table_high = table.astype(jnp.bfloat16)
    table_low = (table - table_high.astype(jnp.float32)).astype(jnp.bfloat16)
    first = jnp.einsum("ab,cbk->cak", table_high, signal, preferred_element_type=jnp.float32)
    return first + jnp.einsum("ab,cbk->cak", table_low, signal, preferred_element_type=jnp.float32)


def outer_wide(table, values):
    return jnp.einsum(
        "ab,cbk->cak",
        table,
        values,
        precision=lax.Precision.HIGH,
        preferred_element_type=jnp.float32,
    )


def inner_wide(values, table):
    return jnp.einsum(
        "cak,kl->cal",
        values,
        table,
        precision=lax.Precision.HIGH,
        preferred_element_type=jnp.float32,
    )


def spectral_forward(signal, tables):
    outer_cos, outer_sin, inner_cos, inner_sin, twist_cos, twist_sin = tables
    part_re = outer_exact(outer_cos, signal)
    part_im = outer_exact(outer_sin, signal)
    turned_re = part_re * twist_cos - part_im * twist_sin
    turned_im = part_re * twist_sin + part_im * twist_cos
    spec_re = inner_wide(turned_re, inner_cos) - inner_wide(turned_im, inner_sin)
    spec_im = inner_wide(turned_re, inner_sin) + inner_wide(turned_im, inner_cos)
    return (spec_re, spec_im)


def spectral_inverse_real(spec_re, spec_im, tables):
    outer_cos, outer_sin, inner_cos, inner_sin, twist_cos, twist_sin = tables
    back_re = inner_wide(spec_re, inner_cos) + inner_wide(spec_im, inner_sin)
    back_im = inner_wide(spec_im, inner_cos) - inner_wide(spec_re, inner_sin)
    turned_re = back_re * twist_cos + back_im * twist_sin
    turned_im = back_im * twist_cos - back_re * twist_sin
    total_len = spec_re.shape[1] * spec_re.shape[2]
    return (outer_wide(outer_cos, turned_re) + outer_wide(outer_sin, turned_im)) / total_len


def correlate_plain(gathered, filters, tables):
    channel_count, seq_len = gathered.shape
    count_outer = tables[0].shape[0]
    count_inner = tables[2].shape[0]
    padding = jnp.zeros((2 * channel_count, seq_len), jnp.bfloat16)
    stacked = jnp.concatenate([gathered, filters], axis=0)
    padded = jnp.concatenate([stacked, padding], axis=1).reshape(
        2 * channel_count, count_outer, count_inner
    )
    both_re, both_im = spectral_forward(padded, tables)
    signal_re, kernel_re = (both_re[:channel_count], both_re[channel_count:])
    signal_im, kernel_im = (both_im[:channel_count], both_im[channel_count:])
    joined_re = kernel_re * signal_re + kernel_im * signal_im
    joined_im = kernel_re * signal_im - kernel_im * signal_re
    result = spectral_inverse_real(joined_re, joined_im, tables)
    return result.reshape(channel_count, -1)[:, :seq_len].astype(jnp.bfloat16)


def per_device_gathered(
    grad_out, out_weight, gate_stream, conv_output, key_stream, value_stream, long_filter
):
    seq_count = lax.axis_size("seq")
    token_count = grad_out.shape[0]
    chan_width = out_weight.shape[1]
    group_width = chan_width // seq_count
    full_grad = lax.all_gather(grad_out, "chan", axis=1, tiled=True)
    tables = dft_tables(2 * seq_count, token_count)
    grad_mix = jnp.einsum(
        "nc,tn->ct",
        lax.all_gather(out_weight, "seq", axis=0, tiled=True),
        full_grad,
        preferred_element_type=jnp.float32,
    )
    gated_grad = (grad_mix * gate_stream.astype(jnp.float32)).astype(jnp.bfloat16)
    regrouped = lax.all_to_all(
        gated_grad.reshape(seq_count, group_width, token_count),
        "seq",
        split_axis=0,
        concat_axis=2,
        tiled=True,
    )
    inner_grad = correlate_plain(regrouped[0], long_filter, tables)
    returned = lax.all_to_all(inner_grad[None], "seq", split_axis=2, concat_axis=0, tiled=True)
    grad_inner = returned.reshape(chan_width, token_count)
    grad_gate = (grad_mix * conv_output.astype(jnp.float32)).astype(jnp.bfloat16)
    inner_grad_wide = grad_inner.astype(jnp.float32)
    grad_key = (inner_grad_wide * value_stream.astype(jnp.float32)).astype(jnp.bfloat16)
    grad_value = (inner_grad_wide * key_stream.astype(jnp.float32)).astype(jnp.bfloat16)
    return (grad_gate, grad_key, grad_value)


def share_kernel(rows, flags_ref, own_ref, low_ref, high_ref, first_ref, second_ref, mine_ref, mine_far_ref, theirs_ref, theirs_far_ref):
    home, core = flags_ref[0] == 1, flags_ref[1]
    tokens, part = own_ref.shape[0], low_ref.shape[0]

    def place(nears, far):
        for block in range(own_ref.shape[1] // (2 * rows)):
            lanes = pl.ds(block * rows, rows)
            mine = pl.ds(pl.multiple_of((2 * block + core) * rows, rows), rows)
            theirs = pl.ds(pl.multiple_of((2 * block + 1 - core) * rows, rows), rows)
            for start, near in nears:
                mine_ref[start : start + near.shape[0], lanes] = near[:, mine]
                theirs_ref[start : start + near.shape[0], lanes] = near[:, theirs]
            mine_far_ref[:, lanes] = far[:, mine]
            theirs_ref[tokens:, lanes] = far[:, theirs]
            theirs_far_ref[:, lanes] = far[:, theirs]

    pl.when(home)(lambda: place([(0, own_ref)], first_ref))
    pl.when(jnp.logical_not(home))(lambda: place([(0, low_ref), (part, high_ref)], second_ref))


def share_blocks(flags, rows, own, low, high, first, second):
    tokens, features = own.shape
    part = first.shape[0]
    whole = lambda a: pl.BlockSpec(a.shape, lambda: (0, 0))
    shapes = [
        jax.ShapeDtypeStruct((t, features // 2), own.dtype) for t in (tokens, part, tokens + part, part)
    ]
    return pl.pallas_call(
        functools.partial(share_kernel, rows),
        in_specs=[pl.BlockSpec(memory_space=pltpu.SMEM)] + [whole(a) for a in (own, low, high, first, second)],
        out_shape=shapes,
        compiler_params=pltpu.CompilerParams(vmem_limit_bytes=VMEM_BYTES),
        name="share_blocks",
    )(flags, own, low, high, first, second)


def mix_kernel(rows, step, flags_ref, mine_ref, mine_far_ref, beside_ref, across_ref, slant_ref, *refs):
    own_ref, near_ref, far_edge_ref, corner_edge_ref, far_ref, corner_ref, keep_ref, send_ref, grad_ref = refs
    tokens, part = mine_ref.shape[0], mine_far_ref.shape[0]

    def place(first, second):
        for distance in range(mine_ref.shape[1] // rows):
            at = pl.ds(pl.multiple_of((flags_ref[2] ^ distance) * rows, rows), rows)
            lanes = slice(distance * rows, (distance + 1) * rows)
            grad_ref[:tokens, lanes] = mine_ref[:, at]
            grad_ref[tokens + first : tokens + first + part, lanes] = mine_far_ref[:, at]
            grad_ref[tokens + second : tokens + second + part, lanes] = beside_ref[:, at]
            grad_ref[2 * tokens : 3 * tokens, lanes] = across_ref[:tokens, at]
            grad_ref[3 * tokens + first : 3 * tokens + first + part, lanes] = across_ref[tokens:, at]
            grad_ref[3 * tokens + second : 3 * tokens + second + part, lanes] = slant_ref[:, at]

    pl.when(flags_ref[0] == 1)(lambda: place(0, part))
    pl.when(flags_ref[0] != 1)(lambda: place(part, 0))

    edge, channels = far_edge_ref.shape[1], own_ref.shape[1]
    for start in [*range(0, edge, step), *range(edge, channels, step)]:
        stop = min(start + step, edge if start < edge else channels)
        lanes = slice(start, stop)
        if start < edge:
            others = (far_edge_ref[:, lanes], corner_edge_ref[:, lanes])
        else:
            others = (far_ref[:, start - edge : stop - edge], corner_ref[:, start - edge : stop - edge])
        weight = jnp.concatenate([own_ref[:, lanes], near_ref[:, lanes], *others], axis=0)
        total = jnp.dot(grad_ref[...], weight, preferred_element_type=jnp.float32)
        keep_ref[:, lanes] = total[: 2 * tokens]
        send_ref[:, lanes] = total[2 * tokens :].astype(jnp.bfloat16)


def partial_mix(flags, grads, own, near, far_parts, corner_parts, step):
    rows, channels = own.shape
    tokens, depth = grads[0].shape
    arrays = (*grads, own, near, far_parts[0], corner_parts[0], far_parts[1], corner_parts[1])
    return pl.pallas_call(
        functools.partial(mix_kernel, rows, step),
        in_specs=[pl.BlockSpec(memory_space=pltpu.SMEM)] + [pl.BlockSpec(memory_space=pltpu.VMEM) for _ in arrays],
        out_specs=(pl.BlockSpec(memory_space=pltpu.VMEM), pl.BlockSpec(memory_space=pltpu.VMEM)),
        out_shape=(
            jax.ShapeDtypeStruct((2 * tokens, channels), jnp.float32),
            jax.ShapeDtypeStruct((2 * tokens, channels), jnp.bfloat16),
        ),
        scratch_shapes=[pltpu.VMEM((4 * tokens, depth), jnp.bfloat16)],
        compiler_params=pltpu.CompilerParams(vmem_limit_bytes=VMEM_BYTES),
        cost_estimate=pl.CostEstimate(
            flops=8 * tokens * depth * channels, bytes_accessed=2 * depth * (channels + tokens), transcendentals=0
        ),
        name="partial_mix",
    )(flags, *arrays)


def gate_kernel(step, keep_ref, near_ref, far_ref, gate_ref, conv_ref, gated_ref, out_ref):
    tokens = far_ref.shape[0]
    for start in range(0, gate_ref.shape[0], step):
        at = slice(start, start + step)
        near = near_ref[:tokens, at].astype(jnp.float32)
        far = far_ref[:, at].astype(jnp.float32)
        mix = (keep_ref[:tokens, at] + near + far).T
        gated_ref[at] = (mix * gate_ref[at].astype(jnp.float32)).astype(jnp.bfloat16)
        out_ref[at] = (mix * conv_ref[at].astype(jnp.float32)).astype(jnp.bfloat16)


def gate_mix(keep, near, far, gate, conv, step):
    channels, tokens = gate.shape
    whole = pl.BlockSpec(memory_space=pltpu.VMEM)
    shape = jax.ShapeDtypeStruct((channels, tokens), jnp.bfloat16)
    return pl.pallas_call(
        functools.partial(gate_kernel, step),
        in_specs=[whole] * 5,
        out_specs=(whole, whole),
        out_shape=(shape, shape),
        compiler_params=pltpu.CompilerParams(vmem_limit_bytes=VMEM_BYTES),
        cost_estimate=pl.CostEstimate(flops=0, bytes_accessed=16 * channels * tokens, transcendentals=0),
        name="gate_mix",
    )(keep, near, far, gate, conv)


def output_kernel(inner_ref, value_ref, key_ref, grad_key_ref, grad_value_ref):
    inner = inner_ref[...].astype(jnp.float32)
    grad_key_ref[...] = (inner * value_ref[...].astype(jnp.float32)).astype(jnp.bfloat16)
    grad_value_ref[...] = (inner * key_ref[...].astype(jnp.float32)).astype(jnp.bfloat16)


def output_products(inner, value, key):
    channels, tokens = value.shape
    steps = 2
    block = pl.BlockSpec((channels // steps, tokens), lambda g: (g, 0))
    shape = jax.ShapeDtypeStruct(value.shape, jnp.bfloat16)
    return pl.pallas_call(
        output_kernel,
        grid=(steps,),
        in_specs=[block, block, block],
        out_specs=(block, block),
        out_shape=(shape, shape),
        compiler_params=pltpu.CompilerParams(vmem_limit_bytes=VMEM_BYTES),
        name="output_products",
    )(inner, value, key)


def swap(values, axis, count, mask):
    return lax.ppermute(values, axis, [(i, i ^ mask) for i in range(count)])


def per_device(
    grad_out, out_weight, gate_stream, conv_output, key_stream, value_stream, long_filter
):
    seq_count = lax.axis_size("seq")
    token_count, shard_features = grad_out.shape
    weight_rows, chan_width = out_weight.shape
    group_width = chan_width // seq_count
    group = seq_count // 2
    place = lax.axis_index("seq")
    side = place // group
    core = place % 2
    near, far = 2, 4
    hop = lambda values, mask: swap(values, "seq", seq_count, mask)

    spectrum = filter_spectrum(long_filter, seq_count, min(128, group_width))

    shard = lax.axis_index("chan")
    home = shard == side
    flags = jnp.stack([home.astype(jnp.int32), core.astype(jnp.int32), (place % group // 2).astype(jnp.int32)])
    part = token_count // 2
    both = ("seq", "chan")
    at = lambda s, y: s * 2 + y
    away = [(s, 1 - s // group) for s in range(seq_count)]
    first = lax.ppermute(grad_out[:part], both, [(at(s, y), at(s ^ group, y)) for s, y in away])
    high = swap(grad_out[part:], "chan", 2, 1)
    low = swap(grad_out[:part], "chan", 2, 1)
    second = lax.ppermute(high, both, [(at(s, 1 - y), at(s ^ group, 1 - y)) for s, y in away])

    lead = chan_width // 16 * 7
    edge, rest = out_weight[:, :lead], out_weight[:, lead:]
    near_all, far_rest = hop(out_weight, near), hop(rest, far)
    near_edge = near_all[:, :lead]
    first, second, low, near_edge = lax.optimization_barrier((first, second, low, near_edge))
    far_edge, corner_edge, corner_rest = hop(edge, far), hop(near_edge, far), hop(far_rest, near)

    mine, mine_far, theirs, theirs_far = share_blocks(flags, weight_rows, grad_out, low, high, first, second)
    beside = swap(mine_far, "chan", 2, 1)
    across = hop(theirs, 1)
    slant = lax.ppermute(
        theirs_far, both, [(at(s, y), at(s ^ 1, 1 - y)) for s in range(seq_count) for y in range(2)]
    )
    keep, send = partial_mix(
        flags, (mine, mine_far, beside, across, slant),
        out_weight, near_all, (far_edge, far_rest), (corner_edge, corner_rest), chan_width // 8,
    )
    given = hop(send, 1)
    over = hop((keep[token_count:] + given[token_count:].astype(jnp.float32)).astype(jnp.bfloat16), group)
    gated, grad_gate = gate_mix(keep, given, over, gate_stream, conv_output, chan_width // 4)
    regrouped = lax.all_to_all(
        gated.reshape(seq_count, group_width, token_count), "seq", split_axis=0, concat_axis=0, tiled=True
    )
    inner = correlate(regrouped, spectrum, min(128, group_width))
    returned = lax.all_to_all(inner, "seq", split_axis=0, concat_axis=0, tiled=True)
    grad_key, grad_value = output_products(returned.reshape(chan_width, token_count), value_stream, key_stream)
    return (grad_gate, grad_key, grad_value)


def solution(mesh):
    in_specs = (
        P("seq", "chan"),
        P("seq", "chan"),
        P("chan", "seq"),
        P("chan", "seq"),
        P("chan", "seq"),
        P("chan", "seq"),
        P(("chan", "seq"), None),
    )
    out_specs = (P("chan", "seq"), P("chan", "seq"), P("chan", "seq"))
    square = mesh.shape["chan"] == 2 and mesh.shape["seq"] == 16
    return jax.shard_map(
        per_device if square else per_device_gathered,
        mesh=mesh, in_specs=in_specs, out_specs=out_specs, check_vma=False,
    )
```

```python
import functools
import itertools
import math

import jax
import jax.numpy as jnp
import numpy as np
from jax import lax
from jax.experimental import pallas as pl
from jax.experimental.pallas import tpu as pltpu
from jax.sharding import PartitionSpec as P

VMEM_BYTES = 16 * 1024 * 1024


def dft_constants(blocks, width):
    outer = 2 * blocks
    lines = blocks + 1
    lane = np.arange(width)
    twist = 2.0 * np.pi * (np.arange(lines)[:, None] * lane[None, :] % (outer * width)) / (outer * width)
    inner = 2.0 * np.pi * (lane[:, None] * lane[None, :] % width) / width
    cos, sin = np.cos(inner), np.sin(inner)
    forward = np.block([[cos, -sin], [sin, cos]]).astype(np.float32)
    backward = np.block([[cos, sin], [-sin, cos]]).astype(np.float32)
    twist = np.stack([np.cos(twist), np.sin(twist)]).astype(np.float32)
    return twist, forward, backward


def scaled_sum(terms):
    total = None
    for scale, value in terms:
        if abs(scale) < 1e-12:
            continue
        if abs(scale - 1.0) < 1e-12:
            term = value
        elif abs(scale + 1.0) < 1e-12:
            term = -value
        else:
            term = value * np.float32(scale)
        total = term if total is None else total + term
    return total


def real_lines(parts, period):
    count = len(parts)
    half = period // 2
    if half % 2 or count < 2:
        cosines, sines = [], []
        for k in range(half + 1):
            angle = [2.0 * math.pi * (i * k % period) / period for i in range(count)]
            cosines.append(scaled_sum([(math.cos(a), p) for a, p in zip(angle, parts)]))
            sines.append(scaled_sum([(math.sin(a), p) for a, p in zip(angle, parts)]))
        return cosines, sines
    even_cos, even_sin = real_lines(parts[0::2], half)
    quarter = half // 2
    cosines, sines = [None] * (half + 1), [None] * (half + 1)
    odd = parts[1::2]
    for k in range(quarter + 1):
        angle = [2.0 * math.pi * ((2 * m + 1) * k % period) / period for m in range(len(odd))]
        odd_cos = scaled_sum([(math.cos(a), p) for a, p in zip(angle, odd)])
        odd_sin = scaled_sum([(math.sin(a), p) for a, p in zip(angle, odd)])
        cosines[k] = add(even_cos[k], odd_cos)
        sines[k] = add(even_sin[k], odd_sin)
        if k != half - k:
            cosines[half - k] = subtract(even_cos[k], odd_cos)
            sines[half - k] = subtract(odd_sin, even_sin[k])
    return cosines, sines


def add(a, b):
    if a is None or b is None:
        return b if a is None else a
    return a + b


def subtract(a, b):
    if b is None:
        return a
    return -b if a is None else a - b


def real_parts(re, im, period, count):
    half = period // 2
    if half % 2 or count < 2:
        out = []
        for i in range(count):
            angle = [2.0 * math.pi * (i * k % period) / period for k in range(half + 1)]
            terms = [(math.cos(a), r) for a, r in zip(angle, re) if r is not None]
            terms += [(-math.sin(a), m) for a, m in zip(angle, im) if m is not None]
            out.append(scaled_sum(terms))
        return out
    quarter = half // 2
    sum_re, sum_im, gap_re, gap_im = [], [], [], []
    for k in range(quarter + 1):
        if k == half - k:
            sum_re.append(re[k]); sum_im.append(None)
            gap_re.append(None); gap_im.append(im[k])
        else:
            sum_re.append(add(re[k], re[half - k])); sum_im.append(subtract(im[k], im[half - k]))
            gap_re.append(subtract(re[k], re[half - k])); gap_im.append(add(im[k], im[half - k]))
    out = [None] * count
    out[0::2] = real_parts(sum_re, sum_im, half, (count + 1) // 2)
    for i in range(1, count, 2):
        angle = [2.0 * math.pi * (i * k % period) / period for k in range(quarter + 1)]
        terms = [(math.cos(a), r) for a, r in zip(angle, gap_re) if r is not None]
        terms += [(-math.sin(a), m) for a, m in zip(angle, gap_im) if m is not None]
        out[i] = scaled_sum(terms)
    return out


def put_split(pair_ref, row, rows, re, im):
    width = re.shape[-1]
    for at, value in ((0, re), (1, im)):
        high = value.astype(jnp.bfloat16)
        low = (value - high.astype(jnp.float32)).astype(jnp.bfloat16)
        pair_ref[row : row + rows, at * width : (at + 1) * width] = high
        pair_ref[row : row + rows, (2 + at) * width : (3 + at) * width] = low


def wide_dot(pair, high, low):
    depth = high.shape[0]
    return jnp.dot(
        jnp.concatenate([pair, pair[:, :depth]], axis=1),
        jnp.concatenate([high, high, low], axis=0),
        preferred_element_type=jnp.float32,
    )


def to_spectrum(read, twist_ref, high_ref, low_ref, pair_ref, spec_ref, blocks, channels, rows):
    for at in range(0, channels, rows):
        parts = [read(i, at).astype(jnp.float32) for i in range(blocks)]
        cosines, sines = real_lines(parts, 2 * blocks)
        for k in range(blocks + 1):
            width = cosines[k].shape[1]
            turn_cos, turn_sin = twist_ref[k : k + 1, :width], twist_ref[k : k + 1, width:]
            re, im = cosines[k], sines[k]
            if im is None:
                new_re, new_im = re * turn_cos, -(re * turn_sin)
            else:
                new_re, new_im = re * turn_cos - im * turn_sin, -(re * turn_sin + im * turn_cos)
            put_split(pair_ref, k * channels + at, rows, new_re, new_im)
    spec_ref[...] = wide_dot(pair_ref[...], high_ref[...], low_ref[...])


def each_step(channels, step, body):
    pl.loop(0, channels // step)(lambda c: body(pl.multiple_of(c * step, step)))


def table_rows(blocks, width):
    twist, forward, backward = dft_constants(blocks, width)
    lines = np.zeros((-(-(blocks + 1) // 8) * 8, 2 * width), np.float32)
    lines[: blocks + 1, :width], lines[: blocks + 1, width:] = twist
    return np.concatenate([lines, forward, backward])


def split_into(high_ref, low_ref, table):
    high = table.astype(jnp.bfloat16)
    high_ref[...] = high
    low_ref[...] = (table - high.astype(jnp.float32)).astype(jnp.bfloat16)


def filter_kernel(blocks, step, rows, taps_ref, table_ref, out_ref, pair_ref, spec_ref, high_ref, low_ref):
    channels, length = taps_ref.shape
    width = length // blocks
    total = 2 * blocks * width
    spectra = (blocks + 1) * channels
    tail = table_ref.shape[0] - 4 * width
    out_ref[spectra:] = table_ref[...]
    twist_ref = table_ref.at[:tail]
    split_into(high_ref, low_ref, table_ref[tail : tail + 2 * width])

    def body(start):
        to_spectrum(
            lambda i, at: taps_ref[pl.ds(start + at, rows), i * width : (i + 1) * width],
            twist_ref, high_ref, low_ref, pair_ref, spec_ref, blocks, step, rows,
        )
        for k in range(blocks + 1):
            scale = (1.0 if k in (0, blocks) else 2.0) / total
            out_ref[pl.ds(k * channels + start, step)] = spec_ref[k * step : (k + 1) * step, :] * np.float32(scale)

    each_step(channels, step, body)


def transform_scratch(blocks, width, step, tables):
    lines = blocks + 1
    return [
        pltpu.VMEM((lines * step, 4 * width), jnp.bfloat16),
        pltpu.VMEM((lines * step, 2 * width), jnp.float32),
    ] + [pltpu.VMEM((2 * width, 2 * width), jnp.bfloat16) for _ in range(2 * tables)]


def filter_spectrum(taps, blocks, step):
    channels, length = taps.shape
    width = length // blocks
    table = table_rows(blocks, width)
    in_vmem = pl.BlockSpec(memory_space=pltpu.VMEM)
    return pl.pallas_call(
        functools.partial(filter_kernel, blocks, step, min(16, step)),
        in_specs=[in_vmem, in_vmem],
        out_specs=in_vmem,
        out_shape=jax.ShapeDtypeStruct(((blocks + 1) * channels + table.shape[0], 2 * width), jnp.float32),
        scratch_shapes=transform_scratch(blocks, width, step, 1),
        compiler_params=pltpu.CompilerParams(vmem_limit_bytes=VMEM_BYTES),
        name="filter_spectrum",
    )(taps, table)


def correlate_kernel(
    blocks, step, rows, sig_ref, filt_ref, out_ref, pair_ref, spec_ref, fh_ref, fl_ref, bh_ref, bl_ref
):
    channels, width = sig_ref.shape[1:]
    spectra = (blocks + 1) * channels
    tail = filt_ref.shape[0] - 4 * width
    twist_ref = filt_ref.at[spectra:tail]
    split_into(fh_ref, fl_ref, filt_ref[tail : tail + 2 * width])
    split_into(bh_ref, bl_ref, filt_ref[tail + 2 * width :])

    def body(start):
        to_spectrum(
            lambda i, at: sig_ref[i, pl.ds(start + at, rows), :],
            twist_ref, fh_ref, fl_ref, pair_ref, spec_ref, blocks, step, rows,
        )
        for k in range(blocks + 1):
            for at in range(0, step, rows):
                row = k * step + at
                sig_re = spec_ref[row : row + rows, :width]
                sig_im = spec_ref[row : row + rows, width:]
                filt_re = filt_ref[pl.ds(k * channels + start + at, rows), :width]
                filt_im = filt_ref[pl.ds(k * channels + start + at, rows), width:]
                put_split(
                    pair_ref, row, rows,
                    filt_re * sig_re + filt_im * sig_im, filt_re * sig_im - filt_im * sig_re,
                )
        spec_ref[...] = wide_dot(pair_ref[...], bh_ref[...], bl_ref[...])
        for at in range(0, step, rows):
            re_lines, im_lines = [], []
            for k in range(blocks + 1):
                turn_cos, turn_sin = twist_ref[k : k + 1, :width], twist_ref[k : k + 1, width:]
                row = k * step + at
                re, im = spec_ref[row : row + rows, :width], spec_ref[row : row + rows, width:]
                re_lines.append(re * turn_cos - im * turn_sin)
                im_lines.append(re * turn_sin + im * turn_cos)
            for i, value in enumerate(real_parts(re_lines, im_lines, 2 * blocks, blocks)):
                out_ref[i, pl.ds(start + at, rows), :] = value.astype(jnp.bfloat16)

    each_step(channels, step, body)


def correlate(signal, spectrum, step):
    blocks, channels, width = signal.shape
    in_vmem = pl.BlockSpec(memory_space=pltpu.VMEM)
    return pl.pallas_call(
        functools.partial(correlate_kernel, blocks, step, min(16, step)),
        in_specs=[in_vmem, in_vmem],
        out_specs=in_vmem,
        out_shape=jax.ShapeDtypeStruct((blocks, channels, width), jnp.bfloat16),
        scratch_shapes=transform_scratch(blocks, width, step, 2),
        compiler_params=pltpu.CompilerParams(vmem_limit_bytes=VMEM_BYTES),
        name="correlate",
    )(signal, spectrum)


def dft_tables(count_outer, count_inner):
    total_len = count_outer * count_inner
    index_outer = jnp.arange(count_outer, dtype=jnp.int32)
    index_inner = jnp.arange(count_inner, dtype=jnp.int32)
    angle_outer = (index_outer[:, None] * index_outer[None, :] % count_outer).astype(
        jnp.float32
    ) * (2.0 * math.pi / count_outer)
    angle_inner = (index_inner[:, None] * index_inner[None, :] % count_inner).astype(
        jnp.float32
    ) * (2.0 * math.pi / count_inner)
    angle_twist = (index_outer[:, None] * index_inner[None, :] % total_len).astype(jnp.float32) * (
        2.0 * math.pi / total_len
    )
    return (
        jnp.cos(angle_outer),
        -jnp.sin(angle_outer),
        jnp.cos(angle_inner),
        -jnp.sin(angle_inner),
        jnp.cos(angle_twist),
        -jnp.sin(angle_twist),
    )


def outer_exact(table, signal):
    table_high = table.astype(jnp.bfloat16)
    table_low = (table - table_high.astype(jnp.float32)).astype(jnp.bfloat16)
    first = jnp.einsum("ab,cbk->cak", table_high, signal, preferred_element_type=jnp.float32)
    return first + jnp.einsum("ab,cbk->cak", table_low, signal, preferred_element_type=jnp.float32)


def outer_wide(table, values):
    return jnp.einsum(
        "ab,cbk->cak",
        table,
        values,
        precision=lax.Precision.HIGH,
        preferred_element_type=jnp.float32,
    )


def inner_wide(values, table):
    return jnp.einsum(
        "cak,kl->cal",
        values,
        table,
        precision=lax.Precision.HIGH,
        preferred_element_type=jnp.float32,
    )


def spectral_forward(signal, tables):
    outer_cos, outer_sin, inner_cos, inner_sin, twist_cos, twist_sin = tables
    part_re = outer_exact(outer_cos, signal)
    part_im = outer_exact(outer_sin, signal)
    turned_re = part_re * twist_cos - part_im * twist_sin
    turned_im = part_re * twist_sin + part_im * twist_cos
    spec_re = inner_wide(turned_re, inner_cos) - inner_wide(turned_im, inner_sin)
    spec_im = inner_wide(turned_re, inner_sin) + inner_wide(turned_im, inner_cos)
    return (spec_re, spec_im)


def spectral_inverse_real(spec_re, spec_im, tables):
    outer_cos, outer_sin, inner_cos, inner_sin, twist_cos, twist_sin = tables
    back_re = inner_wide(spec_re, inner_cos) + inner_wide(spec_im, inner_sin)
    back_im = inner_wide(spec_im, inner_cos) - inner_wide(spec_re, inner_sin)
    turned_re = back_re * twist_cos + back_im * twist_sin
    turned_im = back_im * twist_cos - back_re * twist_sin
    total_len = spec_re.shape[1] * spec_re.shape[2]
    return (outer_wide(outer_cos, turned_re) + outer_wide(outer_sin, turned_im)) / total_len


def correlate_plain(gathered, filters, tables):
    channel_count, seq_len = gathered.shape
    count_outer = tables[0].shape[0]
    count_inner = tables[2].shape[0]
    padding = jnp.zeros((2 * channel_count, seq_len), jnp.bfloat16)
    stacked = jnp.concatenate([gathered, filters], axis=0)
    padded = jnp.concatenate([stacked, padding], axis=1).reshape(
        2 * channel_count, count_outer, count_inner
    )
    both_re, both_im = spectral_forward(padded, tables)
    signal_re, kernel_re = (both_re[:channel_count], both_re[channel_count:])
    signal_im, kernel_im = (both_im[:channel_count], both_im[channel_count:])
    joined_re = kernel_re * signal_re + kernel_im * signal_im
    joined_im = kernel_re * signal_im - kernel_im * signal_re
    result = spectral_inverse_real(joined_re, joined_im, tables)
    return result.reshape(channel_count, -1)[:, :seq_len].astype(jnp.bfloat16)


def per_device_gathered(
    grad_out, out_weight, gate_stream, conv_output, key_stream, value_stream, long_filter
):
    seq_count = lax.axis_size("seq")
    token_count = grad_out.shape[0]
    chan_width = out_weight.shape[1]
    group_width = chan_width // seq_count
    full_grad = lax.all_gather(grad_out, "chan", axis=1, tiled=True)
    tables = dft_tables(2 * seq_count, token_count)
    grad_mix = jnp.einsum(
        "nc,tn->ct",
        lax.all_gather(out_weight, "seq", axis=0, tiled=True),
        full_grad,
        preferred_element_type=jnp.float32,
    )
    gated_grad = (grad_mix * gate_stream.astype(jnp.float32)).astype(jnp.bfloat16)
    regrouped = lax.all_to_all(
        gated_grad.reshape(seq_count, group_width, token_count),
        "seq",
        split_axis=0,
        concat_axis=2,
        tiled=True,
    )
    inner_grad = correlate_plain(regrouped[0], long_filter, tables)
    returned = lax.all_to_all(inner_grad[None], "seq", split_axis=2, concat_axis=0, tiled=True)
    grad_inner = returned.reshape(chan_width, token_count)
    grad_gate = (grad_mix * conv_output.astype(jnp.float32)).astype(jnp.bfloat16)
    inner_grad_wide = grad_inner.astype(jnp.float32)
    grad_key = (inner_grad_wide * value_stream.astype(jnp.float32)).astype(jnp.bfloat16)
    grad_value = (inner_grad_wide * key_stream.astype(jnp.float32)).astype(jnp.bfloat16)
    return (grad_gate, grad_key, grad_value)


def share_kernel(rows, flags_ref, own_ref, low_ref, high_ref, first_ref, second_ref, mine_ref, mine_far_ref, theirs_ref, theirs_far_ref):
    home, core = flags_ref[0] == 1, flags_ref[1]
    tokens, part = own_ref.shape[0], low_ref.shape[0]

    def place(nears, far):
        for block in range(own_ref.shape[1] // (2 * rows)):
            lanes = pl.ds(block * rows, rows)
            mine = pl.ds(pl.multiple_of((2 * block + core) * rows, rows), rows)
            theirs = pl.ds(pl.multiple_of((2 * block + 1 - core) * rows, rows), rows)
            for start, near in nears:
                mine_ref[start : start + near.shape[0], lanes] = near[:, mine]
                theirs_ref[start : start + near.shape[0], lanes] = near[:, theirs]
            mine_far_ref[:, lanes] = far[:, mine]
            theirs_ref[tokens:, lanes] = far[:, theirs]
            theirs_far_ref[:, lanes] = far[:, theirs]

    pl.when(home)(lambda: place([(0, own_ref)], first_ref))
    pl.when(jnp.logical_not(home))(lambda: place([(0, low_ref), (part, high_ref)], second_ref))


def share_blocks(flags, rows, own, low, high, first, second):
    tokens, features = own.shape
    part = first.shape[0]
    whole = lambda a: pl.BlockSpec(a.shape, lambda: (0, 0))
    shapes = [
        jax.ShapeDtypeStruct((t, features // 2), own.dtype) for t in (tokens, part, tokens + part, part)
    ]
    return pl.pallas_call(
        functools.partial(share_kernel, rows),
        in_specs=[pl.BlockSpec(memory_space=pltpu.SMEM)] + [whole(a) for a in (own, low, high, first, second)],
        out_shape=shapes,
        compiler_params=pltpu.CompilerParams(vmem_limit_bytes=VMEM_BYTES),
        name="share_blocks",
    )(flags, own, low, high, first, second)


def mix_kernel(rows, step, flags_ref, mine_ref, mine_far_ref, beside_ref, across_ref, slant_ref, *refs):
    own_ref, near_ref, far_edge_ref, corner_edge_ref, far_ref, corner_ref, keep_ref, send_ref, grad_ref = refs
    tokens, part = mine_ref.shape[0], mine_far_ref.shape[0]

    def place(first, second):
        for distance in range(mine_ref.shape[1] // rows):
            at = pl.ds(pl.multiple_of((flags_ref[2] ^ distance) * rows, rows), rows)
            lanes = slice(distance * rows, (distance + 1) * rows)
            grad_ref[:tokens, lanes] = mine_ref[:, at]
            grad_ref[tokens + first : tokens + first + part, lanes] = mine_far_ref[:, at]
            grad_ref[tokens + second : tokens + second + part, lanes] = beside_ref[:, at]
            grad_ref[2 * tokens : 3 * tokens, lanes] = across_ref[:tokens, at]
            grad_ref[3 * tokens + first : 3 * tokens + first + part, lanes] = across_ref[tokens:, at]
            grad_ref[3 * tokens + second : 3 * tokens + second + part, lanes] = slant_ref[:, at]

    pl.when(flags_ref[0] == 1)(lambda: place(0, part))
    pl.when(flags_ref[0] != 1)(lambda: place(part, 0))

    edge, channels = far_edge_ref.shape[1], own_ref.shape[1]
    for start in [*range(0, edge, step), *range(edge, channels, step)]:
        stop = min(start + step, edge if start < edge else channels)
        lanes = slice(start, stop)
        if start < edge:
            others = (far_edge_ref[:, lanes], corner_edge_ref[:, lanes])
        else:
            others = (far_ref[:, start - edge : stop - edge], corner_ref[:, start - edge : stop - edge])
        weight = jnp.concatenate([own_ref[:, lanes], near_ref[:, lanes], *others], axis=0)
        total = jnp.dot(grad_ref[...], weight, preferred_element_type=jnp.float32)
        keep_ref[:, lanes] = total[: 2 * tokens]
        send_ref[:, lanes] = total[2 * tokens :].astype(jnp.bfloat16)


def partial_mix(flags, grads, own, near, far_parts, corner_parts, step):
    rows, channels = own.shape
    tokens, depth = grads[0].shape
    arrays = (*grads, own, near, far_parts[0], corner_parts[0], far_parts[1], corner_parts[1])
    return pl.pallas_call(
        functools.partial(mix_kernel, rows, step),
        in_specs=[pl.BlockSpec(memory_space=pltpu.SMEM)] + [pl.BlockSpec(memory_space=pltpu.VMEM) for _ in arrays],
        out_specs=(pl.BlockSpec(memory_space=pltpu.VMEM), pl.BlockSpec(memory_space=pltpu.VMEM)),
        out_shape=(
            jax.ShapeDtypeStruct((2 * tokens, channels), jnp.float32),
            jax.ShapeDtypeStruct((2 * tokens, channels), jnp.bfloat16),
        ),
        scratch_shapes=[pltpu.VMEM((4 * tokens, depth), jnp.bfloat16)],
        compiler_params=pltpu.CompilerParams(vmem_limit_bytes=VMEM_BYTES),
        cost_estimate=pl.CostEstimate(
            flops=8 * tokens * depth * channels, bytes_accessed=2 * depth * (channels + tokens), transcendentals=0
        ),
        name="partial_mix",
    )(flags, *arrays)


def gate_kernel(step, keep_ref, near_ref, far_ref, gate_ref, conv_ref, gated_ref, out_ref):
    tokens = far_ref.shape[0]
    for start in range(0, gate_ref.shape[0], step):
        at = slice(start, start + step)
        near = near_ref[:tokens, at].astype(jnp.float32)
        far = far_ref[:, at].astype(jnp.float32)
        mix = (keep_ref[:tokens, at] + near + far).T
        gated_ref[at] = (mix * gate_ref[at].astype(jnp.float32)).astype(jnp.bfloat16)
        out_ref[at] = (mix * conv_ref[at].astype(jnp.float32)).astype(jnp.bfloat16)


def gate_mix(keep, near, far, gate, conv, step):
    channels, tokens = gate.shape
    whole = pl.BlockSpec(memory_space=pltpu.VMEM)
    shape = jax.ShapeDtypeStruct((channels, tokens), jnp.bfloat16)
    return pl.pallas_call(
        functools.partial(gate_kernel, step),
        in_specs=[whole] * 5,
        out_specs=(whole, whole),
        out_shape=(shape, shape),
        compiler_params=pltpu.CompilerParams(vmem_limit_bytes=VMEM_BYTES),
        cost_estimate=pl.CostEstimate(flops=0, bytes_accessed=16 * channels * tokens, transcendentals=0),
        name="gate_mix",
    )(keep, near, far, gate, conv)


def output_kernel(inner_ref, value_ref, key_ref, grad_key_ref, grad_value_ref):
    inner = inner_ref[...].astype(jnp.float32)
    grad_key_ref[...] = (inner * value_ref[...].astype(jnp.float32)).astype(jnp.bfloat16)
    grad_value_ref[...] = (inner * key_ref[...].astype(jnp.float32)).astype(jnp.bfloat16)


def output_products(inner, value, key):
    channels, tokens = value.shape
    steps = 2
    block = pl.BlockSpec((channels // steps, tokens), lambda g: (g, 0))
    shape = jax.ShapeDtypeStruct(value.shape, jnp.bfloat16)
    return pl.pallas_call(
        output_kernel,
        grid=(steps,),
        in_specs=[block, block, block],
        out_specs=(block, block),
        out_shape=(shape, shape),
        compiler_params=pltpu.CompilerParams(vmem_limit_bytes=VMEM_BYTES),
        name="output_products",
    )(inner, value, key)


def swap(values, axis, count, mask):
    return lax.ppermute(values, axis, [(i, i ^ mask) for i in range(count)])


def per_device(
    grad_out, out_weight, gate_stream, conv_output, key_stream, value_stream, long_filter
):
    seq_count = lax.axis_size("seq")
    token_count, shard_features = grad_out.shape
    weight_rows, chan_width = out_weight.shape
    group_width = chan_width // seq_count
    group = seq_count // 2
    place = lax.axis_index("seq")
    side = place // group
    core = place % 2
    near, far = 2, 4
    hop = lambda values, mask: swap(values, "seq", seq_count, mask)

    spectrum = filter_spectrum(long_filter, seq_count, min(128, group_width))

    shard = lax.axis_index("chan")
    home = shard == side
    flags = jnp.stack([home.astype(jnp.int32), core.astype(jnp.int32), (place % group // 2).astype(jnp.int32)])
    part = token_count // 2
    both = ("seq", "chan")
    at = lambda s, y: s * 2 + y
    away = [(s, 1 - s // group) for s in range(seq_count)]
    first = lax.ppermute(grad_out[:part], both, [(at(s, y), at(s ^ group, y)) for s, y in away])
    high = swap(grad_out[part:], "chan", 2, 1)
    low = swap(grad_out[:part], "chan", 2, 1)
    second = lax.ppermute(high, both, [(at(s, 1 - y), at(s ^ group, 1 - y)) for s, y in away])

    lead = chan_width // 16 * 7
    edge, rest = out_weight[:, :lead], out_weight[:, lead:]
    near_all, far_rest = hop(out_weight, near), hop(rest, far)
    near_edge = near_all[:, :lead]
    first, second, low, near_edge = lax.optimization_barrier((first, second, low, near_edge))
    far_edge, corner_edge, corner_rest = hop(edge, far), hop(near_edge, far), hop(far_rest, near)

    mine, mine_far, theirs, theirs_far = share_blocks(flags, weight_rows, grad_out, low, high, first, second)
    beside = swap(mine_far, "chan", 2, 1)
    across = hop(theirs, 1)
    slant = lax.ppermute(
        theirs_far, both, [(at(s, y), at(s ^ 1, 1 - y)) for s in range(seq_count) for y in range(2)]
    )
    keep, send = partial_mix(
        flags, (mine, mine_far, beside, across, slant),
        out_weight, near_all, (far_edge, far_rest), (corner_edge, corner_rest), chan_width // 4,
    )
    given = hop(send, 1)
    over = hop((keep[token_count:] + given[token_count:].astype(jnp.float32)).astype(jnp.bfloat16), group)
    gated, grad_gate = gate_mix(keep, given, over, gate_stream, conv_output, chan_width // 4)
    regrouped = lax.all_to_all(
        gated.reshape(seq_count, group_width, token_count), "seq", split_axis=0, concat_axis=0, tiled=True
    )
    inner = correlate(regrouped, spectrum, min(128, group_width))
    returned = lax.all_to_all(inner, "seq", split_axis=0, concat_axis=0, tiled=True)
    grad_key, grad_value = output_products(returned.reshape(chan_width, token_count), value_stream, key_stream)
    return (grad_gate, grad_key, grad_value)


def solution(mesh):
    in_specs = (
        P("seq", "chan"),
        P("seq", "chan"),
        P("chan", "seq"),
        P("chan", "seq"),
        P("chan", "seq"),
        P("chan", "seq"),
        P(("chan", "seq"), None),
    )
    out_specs = (P("chan", "seq"), P("chan", "seq"), P("chan", "seq"))
    square = mesh.shape["chan"] == 2 and mesh.shape["seq"] == 16
    return jax.shard_map(
        per_device if square else per_device_gathered,
        mesh=mesh, in_specs=in_specs, out_specs=out_specs, check_vma=False,
    )
```
